128 devices in a mesh: fsdp: 16 (over x_hi, z, core), tp: 8 (over x_lo, y).
Axes of the slice: x: 4 (x_hi: 2, x_lo: 2; x = x_hi * 2 + x_lo), y: 4, z: 4, core: 2. Of those that a mesh axis runs over, the one named last changes fastest.
Arguments:
- tokens: bfloat16 [16384, 1024], P(('fsdp', 'tp')), may hold values from -6 to 6
- gain_attention: float32 [1024], replicated, may hold values from 0.5 to 1.5
- w_query: bfloat16 [1024, 1024], P('fsdp', 'tp'), may hold values from -0.1875 to 0.1875
- key_value_weight: bfloat16 [1024, 1024], P('fsdp', 'tp'), may hold values from -0.1875 to 0.1875
- w_output: bfloat16 [1024, 1024], P('tp', 'fsdp'), may hold values from -1 to 1
- sinks: float32 [16], replicated, may hold values from 2 to 5.5
- gain_expert: float32 [1024], replicated, may hold values from 0.5 to 1.5
- w_gate: bfloat16 [1024, 16384], P('fsdp', 'tp'), may hold values from -0.1875 to 0.1875
- w_up: bfloat16 [1024, 16384], P('fsdp', 'tp'), may hold values from -0.1875 to 0.1875
- w_down: bfloat16 [1024, 16384], P('fsdp', 'tp'), may hold values from -0.25 to 0.25
- bias_gate: float32 [32, 512], replicated, may hold values from -3 to 3
- bias_up: float32 [32, 512], replicated, may hold values from -3 to 3
- bias_down: float32 [32, 1024], replicated, may hold values from -2 to 2
- gates: float32 [16384, 8], P('fsdp'), as said below
- routes: int32 [16384, 8], P('fsdp'), may hold values from 0 to 31, all different within a row; in each aligned block of 1024 rows (0 to 1023, 1024 to 2047, ...) at most 272 rows name the same one
- segments: int32 [16384], P('fsdp'), may hold values from 0 to 47, as said below
- cotangent: bfloat16 [16384, 1024], P(('fsdp', 'tp')), may hold values from -6 to 6
Outputs:
- layer_out: float32 [16384, 1024], P(('fsdp', 'tp'))
- grad_tokens: float32 [16384, 1024], P(('fsdp', 'tp'))
- grad_gain_attention: float32 [1024], replicated
- grad_w_query: float32 [1024, 1024], P('fsdp', 'tp')
- grad_w_keyval: float32 [1024, 1024], P('fsdp', 'tp')
- grad_w_output: float32 [1024, 1024], P('tp', 'fsdp')
- grad_sinks: float32 [16], replicated
- grad_gain_expert: float32 [1024], replicated
- grad_w_gate: float32 [1024, 16384], P('fsdp', 'tp')
- grad_w_up: float32 [1024, 16384], P('fsdp', 'tp')
- grad_w_down: float32 [1024, 16384], P('fsdp', 'tp')
- grad_bias_gate: float32 [32, 512], replicated
- grad_bias_up: float32 [32, 512], replicated
- grad_bias_down: float32 [32, 1024], replicated
- grad_gates: float32 [16384, 8], P(('fsdp', 'tp'))
The draws below stay inside these ranges and needn't reach their ends.
Inputs may be any that keep to these rules, and one draw needn't show every extreme that they name: `routes`: in the 1024 tokens of one sequence no expert is named by more than 272 tokens, a bound that some block reaches; a token names 8 different experts. `segments`: never falling; sequence s holds the numbers 3 s, 3 s + 1 and 3 s + 2, each on at least one token. A token's 8 gates are positive and sum to one.
All inputs are finite; a program needn't handle non-finite values.
Results may differ from the reference program's by a relative error of at most 0.019.
Values may be sent and summed in bfloat16 or wider, within the bound.
A program may use at most 320 MiB of HBM per device.

```python
import math
import jax
import jax.numpy as jnp
import numpy as np
from jax import lax

MODEL_DIM = 1024
HQ = 16
KEY_VALUE_HEADS = 8
HEAD_DIM = 64
FF = 512
EXPERTS = 32
TOP = 8
WINDOW = 128
SEQUENCE_TOKENS = 1024
SEQUENCE_COUNT = 16
TOKENS = 16384
DEV_ROWS = 128
CAP = 272


def draw_segments(key, part):
    key = jax.random.fold_in(key, 11)
    first_key, second_key = jax.random.split(key)
    starts = jax.random.randint(first_key, (SEQUENCE_COUNT, 1), 1, DEV_ROWS)
    finish = jax.random.randint(second_key, (SEQUENCE_COUNT, 1), SEQUENCE_TOKENS - DEV_ROWS + 1, SEQUENCE_TOKENS)
    place = jnp.arange(SEQUENCE_TOKENS, dtype=jnp.int32)[None, :]
    numbers = 3 * jnp.arange(SEQUENCE_COUNT, dtype=jnp.int32)[:, None] + (place >= starts).astype(jnp.int32) + (place >= finish).astype(jnp.int32)
    return numbers.reshape(-1).astype(jnp.int32)


def draw_gates(key, part):
    key = jax.random.fold_in(key, 23)
    logits = 0.5 * jax.random.normal(key, (TOKENS, TOP), jnp.float32)
    return jax.nn.softmax(logits, -1).astype(jnp.float32)


def block_scale(rng, shape, pieces, low, largest):
    def one(position, parts):
        draws = jax.random.uniform(jax.random.fold_in(jax.random.fold_in(rng, 6), position), (parts,), jnp.float32, low / len(pieces), largest / len(pieces))
        return jnp.repeat(jnp.exp(draws), shape[position] // parts).reshape((-1,) + (1,) * (len(shape) - position - 1))

    factor_of = one(*pieces[0])
    for cut in pieces[1:]:
        factor_of = factor_of * one(*cut)
    return factor_of


def assign_block(own_key, own, number, rows, count, top, bound, skew):
    sequence = jax.random.permutation(own_key, count)
    heavy_load, usual = load_shares(count, rows * top, bound, skew, True), load_shares(count, rows * top, bound, skew, False)
    places = jnp.arange(count)

    def named(lengths, turn):
        used = int((lengths > 0).sum())
        fixed = max(1, used // 4)
        shifted = fixed + (places - fixed + turn * (used - fixed)) % max(1, count - fixed)
        return jnp.zeros((count,), jnp.int32).at[sequence[jnp.where(places < fixed, places, shifted)]].set(jnp.asarray(lengths, jnp.int32))

    lengths = jnp.where(number % 4 == 0, named(heavy_load, number // 4), named(usual, number - number // 4 - 1))
    mixed = jax.random.permutation(jax.random.fold_in(own, 3), count)
    source_of, sink = mixed[0:count // 2 * 2:2], mixed[1:count // 2 * 2:2]
    margin = jnp.minimum(lengths[source_of] - 1, bound - lengths[sink]) // 2
    margin = jnp.where((source_of == sequence[0]) | (sink == sequence[0]) | (lengths[sink] == 0), 0, jnp.maximum(margin, 0))
    shifted = jax.random.randint(jax.random.fold_in(own, 4), (count // 2,), 0, 1 << 20) % (margin + 1)
    lengths = lengths.at[source_of].add(-shifted).at[sink].add(shifted)
    members = jnp.searchsorted(jnp.cumsum(lengths), jnp.arange(rows * top), side="right").astype(jnp.int32)
    table = members.reshape(top, rows).T
    table = table[jax.random.permutation(jax.random.fold_in(own, 1), rows)]
    turn = jax.random.randint(jax.random.fold_in(own, 2), (rows, 1), 0, top)
    return jnp.take_along_axis(table, (jnp.arange(top)[None, :] + turn) % top, axis=1)


def load_shares(amount, total, limit, slope, full):
    portions = [(1 << 20) // math.isqrt(grade ** slope) + 1 for grade in range(1, amount + 1)]
    largest = limit if full else min(limit, max(-(-total // amount), total * portions[0] // sum(portions)))
    least = 1 if total - largest >= amount - 1 else 0
    counts, surplus = [largest] + [least] * (amount - 1), total - largest - least * (amount - 1)
    while surplus > 0:
        movable = [i for i in range(1, amount) if counts[i] < largest] or [i for i in range(1, amount) if counts[i] < limit]
        mass, remaining = sum([portions[i] for i in movable]), surplus
        for i in movable:
            addition = min(limit - counts[i], max(1, remaining * portions[i] // mass), surplus)
            counts[i] = counts[i] + addition
            surplus = surplus - addition
    return np.array(counts)


def normal_values(own_key, shape, spread, bound, shards=(), held_as=jnp.bfloat16):
    level = block_scale(own_key, shape, shards, -0.22, 0.18) if shards else 1.0
    result = jax.random.normal(own_key, shape, jnp.float32) * spread * level
    return jnp.minimum(jnp.maximum(result, -bound), bound).astype(held_as)


def setup_inputs(seed: int = 0) -> dict:
    seeds = jax.random.split(jax.random.key(seed), 18)
    tokens = normal_values(seeds[0], (TOKENS, MODEL_DIM), 1.0, 6.0, ((0, 128),))
    gain_attention = jnp.clip(1.0 + 0.1 * jax.random.normal(seeds[1], (MODEL_DIM,), jnp.float32), 0.5, 1.5)
    w_query = normal_values(seeds[2], (MODEL_DIM, HQ * HEAD_DIM), MODEL_DIM ** -0.5, 0.1875, ((0, 16), (1, 8)))
    key_value_weight = normal_values(seeds[3], (MODEL_DIM, KEY_VALUE_HEADS * 2 * HEAD_DIM), MODEL_DIM ** -0.5, 0.1875, ((0, 16), (1, 8)))
    w_output = normal_values(seeds[4], (HQ * HEAD_DIM, MODEL_DIM), (HQ * HEAD_DIM * 4 // WINDOW) ** -0.5, 1.0, ((0, 8), (1, 16)))
    sinks = jnp.clip(jax.random.uniform(seeds[5], (HQ,), jnp.float32, 2.0, 5.5), 2.0, 5.5)
    gain_expert = jnp.clip(1.0 + 0.1 * jax.random.normal(seeds[6], (MODEL_DIM,), jnp.float32), 0.5, 1.5)
    w_gate = normal_values(seeds[7], (MODEL_DIM, FF * EXPERTS), MODEL_DIM ** -0.5, 0.1875, ((0, 16), (1, 8)))
    w_up = normal_values(seeds[8], (MODEL_DIM, FF * EXPERTS), MODEL_DIM ** -0.5, 0.1875, ((0, 16), (1, 8)))
    w_down = normal_values(seeds[9], (MODEL_DIM, FF * EXPERTS), FF ** -0.5, 0.25, ((0, 16), (1, 8)))
    bias_gate = normal_values(seeds[10], (EXPERTS, FF), 0.5, 3.0, (), jnp.float32)
    bias_up = normal_values(seeds[11], (EXPERTS, FF), 0.5, 3.0, (), jnp.float32)
    bias_down = normal_values(seeds[12], (EXPERTS, MODEL_DIM), 0.3, 2.0, (), jnp.float32)
    gates = draw_gates(jax.random.fold_in(seeds[17], 71), 0)
    routes_keys = jax.random.split(jax.random.fold_in(seeds[14], 1), TOKENS // SEQUENCE_TOKENS)
    routes_turns = jax.random.permutation(jax.random.fold_in(seeds[14], 3), TOKENS // SEQUENCE_TOKENS)
    routes = jax.vmap(lambda own, number: assign_block(jax.random.fold_in(seeds[14], 2), own, number, SEQUENCE_TOKENS, EXPERTS, TOP, CAP, 0))(routes_keys, routes_turns).reshape((TOKENS, TOP))
    segments = draw_segments(jax.random.fold_in(seeds[17], 71), 0)
    cotangent = normal_values(seeds[16], (TOKENS, MODEL_DIM), 1.0, 6.0, ((0, 128),))
    return {"tokens": tokens, "gain_attention": gain_attention, "w_query": w_query, "key_value_weight": key_value_weight, "w_output": w_output, "sinks": sinks, "gain_expert": gain_expert, "w_gate": w_gate, "w_up": w_up, "w_down": w_down, "bias_gate": bias_gate, "bias_up": bias_up, "bias_down": bias_down, "gates": gates, "routes": routes, "segments": segments, "cotangent": cotangent}


epsilon = 1e-05
ROPE_BASE = 10000.0
CLAMP = 7.0
sigmoid_slope = 1.702
HIGHEST = lax.Precision.HIGHEST

@jax.custom_vjp
def low(v):
    return lax.optimization_barrier(v.astype(jnp.bfloat16)).astype(jnp.float32)

@jax.custom_vjp
def low_back(v):
    return v

def low_keep(v):
    return (low(v), None)

def low_pass(kept, grad):
    return (grad,)

def back_keep(v):
    return (v, None)

def back_low(kept, grad):
    return (low(grad),)
low.defvjp(low_keep, low_pass)
low_back.defvjp(back_keep, back_low)

def normalize(values, gain):
    return values * lax.rsqrt(lax.optimization_barrier(jnp.mean(values * values, -1, keepdims=True)) + epsilon) * gain

def rope_tables(length, head_size):
    half = head_size // 2
    frequency = ROPE_BASE ** (-2.0 * jnp.arange(half, dtype=jnp.float32) / head_size)
    angles = jnp.arange(length, dtype=jnp.float32)[:, None] * frequency[None, :]
    return (jnp.cos(angles), jnp.sin(angles))

def rotate(values, cosine, sine_table):
    half = values.shape[-1] // 2
    lower = values[..., :half]
    upper = values[..., half:]
    cosine = cosine[:, None, :]
    sine_table = sine_table[:, None, :]
    return jnp.concatenate([lower * cosine - upper * sine_table, upper * cosine + lower * sine_table], -1)

def activate(gate_pre, up_pre):
    gate_soft = CLAMP * jnp.tanh(gate_pre / CLAMP)
    up_soft = CLAMP * jnp.tanh(up_pre / CLAMP)
    return gate_soft * jax.nn.sigmoid(sigmoid_slope * gate_soft) * (up_soft + 1.0)

def slot_table(routes, experts, capacity):
    length = routes.shape[0]
    labels = jnp.arange(experts, dtype=jnp.int32)
    hits = lax.optimization_barrier(jnp.sum((routes[:, :, None] == labels).astype(jnp.int32), 1)).astype(jnp.int32)
    earlier = (jnp.cumsum(hits, 0) - hits).astype(jnp.int32)
    slots = jnp.take_along_axis(earlier, routes, 1).astype(jnp.int32)
    token_ids = jnp.broadcast_to(jnp.arange(length, dtype=jnp.int32)[:, None], routes.shape)
    table = jnp.zeros((experts, capacity), jnp.int32).at[routes, slots].set(token_ids)
    flat = (routes * capacity + slots).astype(jnp.int32)
    return (table, flat, slots)

def attend(queries, keys, values, segments, sinks):
    length, heads, head_size = queries.shape
    pair_heads = keys.shape[1]
    group = heads // pair_heads
    block = min(512, length)
    count = length // block
    keys_padded = jnp.concatenate([jnp.zeros((WINDOW, pair_heads, head_size), jnp.float32), keys], 0)
    values_padded = jnp.concatenate([jnp.zeros((WINDOW, pair_heads, head_size), jnp.float32), values], 0)
    segments_padded = jnp.concatenate([jnp.full((WINDOW,), -1, jnp.int32), segments], 0)
    sink_columns = sinks.reshape(pair_heads, group)[:, :, None, None]

    def one_block(start):
        query_block = lax.dynamic_slice_in_dim(queries, start, block, 0).reshape(block, pair_heads, group, head_size)
        key_block = lax.dynamic_slice_in_dim(keys_padded, start, block + WINDOW, 0)
        value_block = lax.dynamic_slice_in_dim(values_padded, start, block + WINDOW, 0)
        query_place = start + jnp.arange(block, dtype=jnp.int32)
        key_place = start - WINDOW + jnp.arange(block + WINDOW, dtype=jnp.int32)
        distance = query_place[:, None] - key_place[None, :]
        same = lax.dynamic_slice_in_dim(segments, start, block, 0)[:, None] == lax.dynamic_slice_in_dim(segments_padded, start, block + WINDOW, 0)[None, :]
        allowed = same & (distance >= 0) & (distance < WINDOW)
        scores = low_back(jnp.einsum('qkgd,skd->kgqs', query_block, key_block, precision=HIGHEST) * head_size ** (-0.5))
        masked = jnp.where(allowed, scores, -jnp.inf)
        extended = jnp.concatenate([jnp.broadcast_to(sink_columns, (pair_heads, group, block, 1)), masked], -1)
        shares = low(jax.nn.softmax(extended, -1)[..., 1:])
        mixed = jnp.einsum('kgqs,skd->qkgd', shares, value_block, precision=HIGHEST)
        return mixed.reshape(block, heads * head_size)
    starts = jnp.arange(count, dtype=jnp.int32) * block
    return lax.map(jax.checkpoint(one_block), starts).reshape(length, heads * head_size)

def forward(inputs, gain_attention, w_query, key_value_weight, w_output, sinks, gain_expert, w_gate, w_up, w_down, bias_gate, bias_up, bias_down, gates, segments, tables, flats):
    gate_mats = w_gate.reshape(MODEL_DIM, FF, EXPERTS).transpose(2, 0, 1)
    up_mats = w_up.reshape(MODEL_DIM, FF, EXPERTS).transpose(2, 0, 1)
    down_mats = w_down.reshape(MODEL_DIM, FF, EXPERTS).transpose(2, 1, 0)
    normed_first = low(normalize(inputs, gain_attention))
    query_pre = low_back(jnp.dot(normed_first, w_query, precision=HIGHEST))
    key_value_unrotated = low_back(jnp.dot(normed_first, key_value_weight, precision=HIGHEST))
    cosine, sine_table = rope_tables(SEQUENCE_TOKENS, HEAD_DIM)
    queries = low(rotate(query_pre.reshape(SEQUENCE_COUNT, SEQUENCE_TOKENS, HQ, HEAD_DIM), cosine, sine_table))
    key_value_rows = key_value_unrotated.reshape(SEQUENCE_COUNT, SEQUENCE_TOKENS, KEY_VALUE_HEADS, 2, HEAD_DIM)
    keys = low(rotate(key_value_rows[:, :, :, 0], cosine, sine_table))
    values = low(key_value_rows[:, :, :, 1])

    def sequence_attention(items):
        return attend(items[0], items[1], items[2], items[3], sinks)
    attended = lax.map(sequence_attention, (queries, keys, values, segments))
    attended = low(low_back(attended.reshape(TOKENS, HQ * HEAD_DIM)))
    branch = low_back(jnp.dot(attended, w_output, precision=HIGHEST))
    mid = inputs + branch
    normed_second = low(normalize(mid, gain_expert)).reshape(SEQUENCE_COUNT, SEQUENCE_TOKENS, MODEL_DIM)

    def sequence_experts(items):
        rows_sequence, gates_sequence, table, flat = items
        rows_in = jnp.take(rows_sequence, table.reshape(-1), 0).reshape(EXPERTS, CAP, MODEL_DIM)
        gate_pre = low_back(jnp.einsum('ecd,edf->ecf', rows_in, gate_mats, precision=HIGHEST)) + bias_gate[:, None, :]
        up_pre = low_back(jnp.einsum('ecd,edf->ecf', rows_in, up_mats, precision=HIGHEST)) + bias_up[:, None, :]
        hidden = low(activate(gate_pre, up_pre))
        expert_rows = low_back(jnp.einsum('ecf,efd->ecd', hidden, down_mats, precision=HIGHEST)) + bias_down[:, None, :]
        picked = jnp.take(expert_rows.reshape(EXPERTS * CAP, MODEL_DIM), flat.reshape(-1), 0).reshape(SEQUENCE_TOKENS, TOP, MODEL_DIM)
        return lax.optimization_barrier(jnp.sum(gates_sequence[:, :, None] * picked, 1))
    mixed = lax.map(jax.checkpoint(sequence_experts), (normed_second, gates.reshape(SEQUENCE_COUNT, SEQUENCE_TOKENS, TOP), tables, flats))
    return mid + mixed.reshape(TOKENS, MODEL_DIM)

def reference(tokens, gain_attention, w_query, key_value_weight, w_output, sinks, gain_expert, w_gate, w_up, w_down, bias_gate, bias_up, bias_down, gates, routes, segments, cotangent):
    tables, flats, unused = jax.vmap(lambda routed: slot_table(routed, EXPERTS, CAP))(routes.reshape(SEQUENCE_COUNT, SEQUENCE_TOKENS, TOP))
    segment_rows = segments.reshape(SEQUENCE_COUNT, SEQUENCE_TOKENS)
    floats = (tokens.astype(jnp.float32), gain_attention.astype(jnp.float32), w_query.astype(jnp.float32), key_value_weight.astype(jnp.float32), w_output.astype(jnp.float32), sinks.astype(jnp.float32), gain_expert.astype(jnp.float32), w_gate.astype(jnp.float32), w_up.astype(jnp.float32), w_down.astype(jnp.float32), bias_gate.astype(jnp.float32), bias_up.astype(jnp.float32), bias_down.astype(jnp.float32), gates.astype(jnp.float32))

    def closed(*arrays):
        return forward(*arrays, segment_rows, tables, flats)
    output, backward = jax.vjp(closed, *floats)
    grads = backward(cotangent.astype(jnp.float32))
    return (output, grads[0], grads[1], grads[2], grads[3], grads[4], grads[5], grads[6], grads[7], grads[8], grads[9], grads[10], grads[11], grads[12], grads[13])
```

```python
import functools
import itertools

import jax
import jax.numpy as jnp
from jax import lax
from jax.experimental import pallas as pl
from jax.experimental.pallas import tpu as pltpu
from jax.sharding import Mesh
from jax.sharding import PartitionSpec as P

MESH = pl.DeviceIdType.MESH
HEAD_DIM = 64
WINDOW = 128
EPS = 1e-05
ROPE_BASE = 10000.0
CLAMP = 7.0
SLOPE = 1.702
SCALE = HEAD_DIM ** (-0.5)
NEG = -1e30
CAP = 272
F32 = jnp.float32
BF16 = jnp.bfloat16
ANY = pl.BlockSpec(memory_space=pl.ANY)
VM = pl.BlockSpec(memory_space=pltpu.VMEM)
SM = pl.BlockSpec(memory_space=pltpu.SMEM)
VMEM_LIMIT = 56 * 1024 * 1024

SIZES = {"xh": 2, "z": 4, "c": 2, "xl": 2, "y": 4, "x": 4}


def coords():
    m, c, t = lax.axis_index("m"), lax.axis_index("core"), lax.axis_index("tp")
    xh, z, xl, y = m // 4, m % 4, t // 4, t % 4
    return {"xh": xh, "z": z, "c": c, "xl": xl, "y": y, "x": 2 * xh + xl}


def moved(place, offset):
    out = dict(place)
    for axis, step in offset.items():
        out[axis] = (place[axis] + step) % SIZES[axis]
        if axis == "x":
            out["xh"], out["xl"] = out["x"] // 2, out["x"] % 2
    return out


def device(place):
    return (place["xh"] * 4 + place["z"], place["c"], place["xl"] * 4 + place["y"])


def offsets(axes):
    ranges = [range(SIZES[a]) for a in axes]
    return [dict(zip(axes, o)) for o in itertools.product(*ranges) if any(o)]


def slot(place, axes):
    out = 0
    for a in axes:
        out = out * SIZES[a] + place[a]
    return out


def greet(peers):
    barrier = pltpu.get_barrier_semaphore()
    for peer in peers:
        pl.semaphore_signal(barrier, inc=1, device_id=device(peer), device_id_type=MESH)
    pl.semaphore_wait(barrier, len(peers))


def remote(src, dst, send, recv, peer):
    return pltpu.make_async_remote_copy(
        src_ref=src,
        dst_ref=dst,
        send_sem=send,
        recv_sem=recv,
        device_id=device(peer),
        device_id_type=MESH,
    )


def comm_params(ident):
    return pltpu.CompilerParams(
        collective_id=ident, has_side_effects=True, vmem_limit_bytes=VMEM_LIMIT
    )


def exchange_kernel(axes, views, *refs):
    count = len(views)
    ins, outs = refs[:count], refs[count : 2 * count]
    bounce = refs[2 * count : 3 * count]
    send, recv, load, store = refs[3 * count :]
    here = coords()
    offs = offsets(axes)
    mine = slot(here, axes)
    loads, stores = [], []
    for i, (src, dst) in enumerate(views):
        loads.append(pltpu.make_async_copy(src(ins[i], mine), bounce[i], load.at[i]))
        stores.append(pltpu.make_async_copy(bounce[i], dst(outs[i], mine), store.at[i]))
        loads[i].start()
    greet([moved(here, o) for o in offs])
    copies = []
    for k, o in enumerate(offs):
        peer = moved(here, o)
        for i, (src, dst) in enumerate(views):
            copy = remote(
                src(ins[i], slot(peer, axes)),
                dst(outs[i], mine),
                send.at[i, k],
                recv.at[i, k],
                peer,
            )
            copy.start()
            copies.append(copy)
    for first, then in zip(loads, stores):
        first.wait()
        then.start()
    for copy in stores + copies:
        copy.wait()


def view_shape(shape, view):
    cut = {whole: None, lead: 0, second: 1, third: 2}[view]
    return tuple(n for d, n in enumerate(shape) if d != cut)


def exchange(items, axes, ident, name):
    views = [(src, dst) for _, _, src, dst in items]
    peers = len(offsets(axes))
    return pl.pallas_call(
        functools.partial(exchange_kernel, axes, views),
        out_shape=[jax.ShapeDtypeStruct(shape, a.dtype) for a, shape, _, _ in items],
        in_specs=[ANY] * len(items),
        out_specs=[ANY] * len(items),
        scratch_shapes=[pltpu.VMEM(view_shape(a.shape, v), a.dtype) for a, _, v, _ in items]
        + [
            pltpu.SemaphoreType.DMA((len(items), peers)),
            pltpu.SemaphoreType.DMA((len(items), peers)),
            pltpu.SemaphoreType.DMA((len(items),)),
            pltpu.SemaphoreType.DMA((len(items),)),
        ],
        compiler_params=comm_params(ident),
        name=name,
    )(*[a for a, _, _, _ in items])


def whole(ref, peer):
    return ref


def lead(ref, peer):
    return ref.at[peer]


def second(ref, peer):
    return ref.at[:, peer]


def third(ref, peer):
    return ref.at[:, :, peer]


class RowGather:
    copies = 8

    def __init__(self, here, src, out, send, recv):
        self.src, self.out, self.send, self.recv, self.here = src, out, send, recv, here
        half = src.shape[-1] // 2
        self.left, self.right = pl.ds(0, half), pl.ds(half, half)
        self.started = []

    def go(self, k, src, dst, offset):
        copy = remote(src, dst, self.send.at[k], self.recv.at[k], moved(self.here, offset))
        copy.start()
        self.started.append(copy)

    def first(self):
        xl, y = self.here["xl"], self.here["y"]
        self.go(0, self.src.at[:, self.left], self.out.at[xl, y, :, self.left], {"xl": 1})
        for k in (1, 3, 2):
            self.go(
                k, self.src.at[:, self.right], self.out.at[xl, y, :, self.right], {"y": k}
            )

    def then(self):
        xl, y = self.here["xl"], self.here["y"]
        self.started[0].wait_recv()
        for k in (1, 3, 2):
            view = self.out.at[:, y, :, self.left]
            self.go(3 + k, view, view, {"y": k})
        for copy in self.started[1:4]:
            copy.wait_recv()
        view = self.out.at[xl, :, :, self.right]
        self.go(7, view, view, {"xl": 1})

    def finish(self):
        for copy in self.started[4:]:
            copy.wait_recv()
        for copy in self.started:
            copy.wait_send()


def rows_kernel(src, out, send, recv, own):
    here = coords()
    local_copy = pltpu.make_async_copy(src, out.at[here["xl"], here["y"]], own)
    local_copy.start()
    greet([moved(here, o) for o in [{"xl": 1}, {"y": 1}, {"y": 2}, {"y": 3}]])
    gather = RowGather(here, src, out, send, recv)
    gather.first()
    local_copy.wait()
    gather.then()
    gather.finish()


def gather_rows(rows, ident, name):
    return pl.pallas_call(
        rows_kernel,
        out_shape=jax.ShapeDtypeStruct((2, 4) + rows.shape, rows.dtype),
        in_specs=[VM],
        out_specs=ANY,
        scratch_shapes=[
            pltpu.SemaphoreType.DMA((8,)),
            pltpu.SemaphoreType.DMA((8,)),
            pltpu.SemaphoreType.DMA,
        ],
        compiler_params=comm_params(ident),
        name=name,
    )(rows)


ORDERS = (("z", "y", "x"), ("y", "x", "z"), ("x", "z", "y"))


def region(ref, p, place, held):
    xl = slice(None) if "x" in held else place["xl"]
    xh = slice(None) if "x" in held else place["xh"]
    z = slice(None) if "z" in held else place["z"]
    y = pl.ds(0, 512) if "y" in held else pl.ds(pl.multiple_of(place["y"] * 128, 128), 128)
    return ref.at[p, xl, xh, z, place["c"], :, y]


def attn_gather_kernel(
    shards, cot, tok, full, cot_full, prev, send, recv, csend, crecv, rsend, rrecv, hsem, own
):
    here = coords()
    local_copies = []
    for p in range(3):
        local_copies.append(
            pltpu.make_async_copy(shards.at[p], region(full, p, here, ()), own.at[p])
        )
    local_copies.append(
        pltpu.make_async_copy(cot, cot_full.at[here["xl"], here["y"]], own.at[3])
    )
    for copy in local_copies:
        copy.start()
    rank = here["xl"] * 4 + here["y"]
    after, before = (rank + 1) % 8, (rank + 7) % 8
    after_place = dict(here, xl=after // 4, y=after % 4)
    before_place = dict(here, xl=before // 4, y=before % 4)
    peers = [moved(here, {a: k}) for a in ("x", "y", "z") for k in (1, 2, 3)]
    peers += [moved(here, {"xl": 1}), moved(here, {"c": 1}), after_place, before_place]
    greet(peers)
    waits = [[None] * 3 for _ in range(3)]

    def start(p, s):
        view = region(full, p, here, ORDERS[p][:s])
        src = shards.at[p] if s == 0 else view
        waits[p][s] = []
        for k in (1, 3, 2):
            copy = remote(
                src,
                view,
                send.at[p, s, k - 1],
                recv.at[p, s, k - 1],
                moved(here, {ORDERS[p][s]: k}),
            )
            copy.start()
            waits[p][s].append(copy)

    for p in range(3):
        start(p, 0)
    halo = remote(tok, prev, hsem.at[0], hsem.at[1], after_place)
    halo.start()
    gather = RowGather(here, cot, cot_full, rsend, rrecv)
    gather.first()
    for copy in local_copies:
        copy.wait()
    for s in (1, 2):
        for p in range(3):
            for copy in waits[p][s - 1]:
                copy.wait_recv()
            start(p, s)
        if s == 1:
            gather.then()
    last = []
    for p in range(3):
        for copy in waits[p][2]:
            copy.wait_recv()
        view = full.at[p, :, :, :, here["c"]]
        copy = remote(view, view, csend.at[p], crecv.at[p], moved(here, {"c": 1}))
        copy.start()
        last.append(copy)
    for copy in last:
        copy.wait()
    halo.wait()
    gather.finish()
    for row in waits:
        for group in row:
            for copy in group:
                copy.wait_send()


def attn_gather(shards, cot, tok, ident):
    dma = pltpu.SemaphoreType.DMA
    return pl.pallas_call(
        attn_gather_kernel,
        out_shape=[
            jax.ShapeDtypeStruct((3, 2, 2, 4, 2, 64, 512), BF16),
            jax.ShapeDtypeStruct((2, 4) + cot.shape, BF16),
            jax.ShapeDtypeStruct(tok.shape, BF16),
        ],
        in_specs=[VM] * 3,
        out_specs=[ANY] * 3,
        scratch_shapes=[
            dma((3, 3, 3)),
            dma((3, 3, 3)),
            dma((3,)),
            dma((3,)),
            dma((8,)),
            dma((8,)),
            dma((2,)),
            dma((4,)),
        ],
        compiler_params=comm_params(ident),
        name="attn_gather",
    )(shards, cot, tok)


def piece(ref, axis, place, dims):
    index = []
    for d in dims:
        if d == "xl":
            index.append(place["xl"] if axis == "x" else slice(None))
        elif d == "xh":
            index.append(place["xh"] if axis == "x" else slice(None))
        elif d == "z":
            index.append(place["z"] if axis == "z" else slice(None))
    index.append(slice(None))
    if axis == "y":
        index.append(pl.ds(pl.multiple_of(place["y"] * 128, 128), 128))
    else:
        index.append(slice(None))
    return tuple(index)


def reduce_shapes(p):
    dims, lanes = ["xl", "xh", "z"], 512
    shapes = [((2, 2, 4, 64, 512), tuple(dims))]
    for axis in ORDERS[p][::-1]:
        if axis == "x":
            dims = [d for d in dims if d not in ("xl", "xh")]
        elif axis == "z":
            dims = [d for d in dims if d != "z"]
        else:
            lanes = 128
        shapes.append((tuple(SIZES[d] for d in dims) + (64, lanes), tuple(dims)))
    return shapes


def attn_reduce_kernel(*refs):
    parts, outs = refs[0], refs[1]
    got0 = refs[2:5]
    sums = [refs[5 + 3 * p : 8 + 3 * p] for p in range(3)]
    gots = [refs[14 + 3 * p : 17 + 3 * p] for p in range(3)]
    csend, crecv, send, recv = refs[23:]
    here = coords()
    other = moved(here, {"c": 1})
    greet([moved(here, {a: k}) for a in ("x", "y", "z") for k in (1, 2, 3)] + [other])
    cores = []
    for p in range(3):
        copy = remote(
            parts.at[p, :, :, :, other["c"]], got0[p], csend.at[p], crecv.at[p], other
        )
        copy.start()
        cores.append(copy)
    shapes = [reduce_shapes(p) for p in range(3)]
    started = []

    def start(p, s):
        axis = ORDERS[p][2 - s]
        dims = shapes[p][s][1]
        group = []
        for k in (1, 3, 2):
            peer = moved(here, {axis: k})
            copy = remote(
                sums[p][s].at[piece(None, axis, peer, dims)],
                gots[p][s].at[k - 1],
                send.at[p, s, k - 1],
                recv.at[p, s, k - 1],
                peer,
            )
            copy.start()
            group.append(copy)
        started.append(group)
        return group

    pending = [None] * 3
    for p in range(3):
        cores[p].wait_recv()
        sums[p][0][...] = (
            parts[p, :, :, :, here["c"]].astype(F32) + got0[p][...].astype(F32)
        ).astype(BF16)
        pending[p] = start(p, 0)
    for s in range(3):
        for p in range(3):
            axis = ORDERS[p][2 - s]
            dims = shapes[p][s][1]
            for copy in pending[p]:
                copy.wait_recv()
            total = sums[p][s][piece(None, axis, here, dims)].astype(F32)
            for k in range(3):
                total = total + gots[p][s][k].astype(F32)
            if s == 2:
                outs[p] = total
            else:
                sums[p][s + 1][...] = total.astype(BF16)
                pending[p] = start(p, s + 1)
    for copy in cores:
        copy.wait_send()
    for group in started:
        for copy in group:
            copy.wait_send()


def attn_reduce(parts, ident):
    dma = pltpu.SemaphoreType.DMA
    shapes = [reduce_shapes(p) for p in range(3)]
    scratch = [pltpu.VMEM((2, 2, 4, 64, 512), BF16) for _ in range(3)]
    for p in range(3):
        scratch += [pltpu.VMEM(shapes[p][s][0], BF16) for s in range(3)]
    for p in range(3):
        scratch += [pltpu.VMEM((3,) + shapes[p][s + 1][0], BF16) for s in range(3)]
    scratch += [dma((3,)), dma((3,)), dma((3, 3, 3)), dma((3, 3, 3))]
    return pl.pallas_call(
        attn_reduce_kernel,
        out_shape=jax.ShapeDtypeStruct((3, 64, 128), F32),
        in_specs=[VM],
        out_specs=VM,
        scratch_shapes=scratch,
        compiler_params=comm_params(ident),
        name="attn_reduce",
    )(parts)


def small_kernel(part, out, got, send, recv, send2, recv2):
    here = coords()
    first, then = offsets(("xh", "z")), offsets(("c", "xl", "y"))
    greet([moved(here, o) for o in first + then])
    copies = []
    for k, o in enumerate(first):
        copy = remote(part, got.at[k], send.at[k], recv.at[k], moved(here, o))
        copy.start()
        copies.append(copy)
    total = part[...]
    for k, copy in enumerate(copies):
        copy.wait_recv()
        total = total + got[k]
    mine = out.at[slot(here, ("c", "xl", "y"))]
    mine[...] = total
    for k, o in enumerate(then):
        copy = remote(mine, mine, send2.at[k], recv2.at[k], moved(here, o))
        copy.start()
        copies.append(copy)
    for copy in copies[len(first) :]:
        copy.wait_recv()
    for copy in copies:
        copy.wait_send()


def small_sums(part, ident):
    dma = pltpu.SemaphoreType.DMA
    return pl.pallas_call(
        small_kernel,
        out_shape=jax.ShapeDtypeStruct((16,) + part.shape, F32),
        in_specs=[VM],
        out_specs=VM,
        scratch_shapes=[
            pltpu.VMEM((7,) + part.shape, F32),
            dma((7,)),
            dma((7,)),
            dma((15,)),
            dma((15,)),
        ],
        compiler_params=comm_params(ident),
        name="small_sums",
    )(part)


def plain(kernel, outs, in_specs, name, *args, grid=None, out_specs=None, scratch=()):
    extra = {} if grid is None else {"grid": grid}
    return pl.pallas_call(
        kernel,
        out_shape=[jax.ShapeDtypeStruct(s, d) for s, d in outs],
        in_specs=in_specs,
        out_specs=out_specs or [VM] * len(outs),
        scratch_shapes=list(scratch),
        compiler_params=pltpu.CompilerParams(vmem_limit_bytes=VMEM_LIMIT),
        name=name,
        **extra,
    )(*args)


def nn(a, b):
    return lax.dot_general(a, b, (((1,), (0,)), ((), ())), preferred_element_type=F32)


def nt(a, b):
    return lax.dot_general(a, b, (((1,), (1,)), ((), ())), preferred_element_type=F32)


def tn(a, b):
    return lax.dot_general(a, b, (((0,), (0,)), ((), ())), preferred_element_type=F32)


def spread(rows, columns, core):
    row = lax.broadcasted_iota(jnp.int32, (rows, columns), 0)
    column = lax.broadcasted_iota(jnp.int32, (rows, columns), 1)
    expert = 4 * (row // 128) + 2 * core + (row // 64) % 2
    return (column == (row % 64) * 32 + expert).astype(F32).astype(BF16)


def sort_kernel(core_ref, w_ref, out_ref):
    hot = spread(1024, 2048, core_ref[0])
    for w in range(3):
        rows = w_ref[:, w].reshape(128, 2048)
        out_ref[:, w] = nt(hot, rows).astype(BF16).reshape(8, 2, 64, 128)


def unsort_kernel(core_ref, g_ref, out_ref):
    hot = spread(1024, 2048, core_ref[0])
    for w in range(3):
        rows = g_ref[:, w].reshape(1024, 128)
        out_ref[:, w] = tn(rows, hot).astype(BF16).reshape(2, 64, 2048)


def rope_partner(values):
    lanes = values.shape[1]
    lane = lax.broadcasted_iota(jnp.int32, values.shape, 1)
    return jnp.where(
        lane % 64 < 32, pltpu.roll(values, lanes - 32, 1), pltpu.roll(values, 32, 1)
    )


def tiled(table):
    return jnp.concatenate([table] * 8, axis=1)


def head_pair(block):
    lane = lax.broadcasted_iota(jnp.int32, block.shape, 1) < 64
    wide = block.astype(F32)
    swapped = pltpu.roll(wide, 64, 1)
    zero = jnp.zeros_like(wide)
    keys = jnp.concatenate([jnp.where(lane, wide, zero), jnp.where(lane, zero, swapped)], 0)
    values = jnp.concatenate([jnp.where(lane, swapped, zero), jnp.where(lane, zero, wide)], 0)
    return keys.astype(BF16), values.astype(BF16)


def window_mask(segq, segk):
    row = lax.broadcasted_iota(jnp.int32, (128, 256), 0)
    column = lax.broadcasted_iota(jnp.int32, (128, 256), 1)
    distance = 128 + row - column
    return (segq == segk) & (distance >= 0) & (distance < WINDOW)


def attn_forward_kernel(
    sinks, tok, prev, full, gain1, gain2, segq, segk, cosq, sinq, cosk, sink_k,
    mid, normed2, normed1, queries, keyvals, attended, logsum,
):
    own = tok[...].astype(F32)
    both = jnp.concatenate([prev[...].astype(F32), own], 0)
    scale = lax.rsqrt(jnp.mean(both * both, -1, keepdims=True) + EPS)
    normed = (both * scale * gain1[...]).astype(BF16)
    normed_own = normed[128:]
    normed1[...] = normed_own
    q = jnp.concatenate([nn(normed_own, full[0, 0]), nn(normed_own, full[0, 1])], 1)
    kv = jnp.concatenate([nn(normed, full[1, 0]), nn(normed, full[1, 1])], 1)
    q = (q * tiled(cosq[...]) + rope_partner(q) * tiled(sinq[...])).astype(BF16)
    kv = (kv * tiled(cosk[...]) + rope_partner(kv) * tiled(sink_k[...])).astype(BF16)
    queries[...] = q
    keyvals[...] = kv
    mask = window_mask(segq[...], segk[...])
    lane = lax.broadcasted_iota(jnp.int32, (128, 128), 1)
    sums = jnp.zeros((128, 128), F32)
    for g in range(8):
        part = slice(128 * g, 128 * g + 128)
        keys, values = head_pair(kv[:, part])
        scores = nt(q[:, part], keys) * SCALE
        shares = []
        for h in range(2):
            masked = jnp.where(mask, scores[:, 256 * h : 256 * h + 256], NEG)
            sink = sinks[2 * g + h]
            peak = jnp.maximum(jnp.max(masked, -1, keepdims=True), sink)
            total = jnp.exp(sink - peak) + jnp.sum(
                jnp.exp(masked - peak), -1, keepdims=True
            )
            log_total = peak + jnp.log(total)
            shares.append(jnp.exp(masked - log_total).astype(BF16))
            sums = jnp.where(lane == 2 * g + h, log_total, sums)
        attended[:, part] = nn(jnp.concatenate(shares, 1), values).astype(BF16)
    logsum[...] = sums
    out = own + nt(attended[:, :512], full[2, 0]) + nt(attended[:, 512:], full[2, 1])
    mid[...] = out
    scale = lax.rsqrt(jnp.mean(out * out, -1, keepdims=True) + EPS)
    normed2[...] = (out * scale * gain2[...]).astype(BF16)


def norm_back(values, gain, grad):
    scale = lax.rsqrt(jnp.mean(values * values, -1, keepdims=True) + EPS)
    normed = values * scale
    weighted = gain * grad
    back = scale * (weighted - normed * jnp.mean(weighted * normed, -1, keepdims=True))
    return back, jnp.sum(grad * normed, 0, keepdims=True)


def attn_backward_kernel(
    sinks, back_parts, out_parts, mid, cot, gain2, full, queries, keyvals, attended, logsum,
    segq, segk,
    layer_out, mid_grad, dq, halo, dkv, grad_wo, grad_gain2, grad_sink,
):
    moved_in = back_parts[0].astype(F32)
    combined = out_parts[0].astype(F32)
    for j in range(1, 8):
        moved_in = moved_in + back_parts[j].astype(F32)
        combined = combined + out_parts[j].astype(F32)
    layer_out[...] = mid[...] + combined
    back, gain_part = norm_back(mid[...], gain2[...], moved_in)
    grad_gain2[...] = gain_part
    grad = cot[...].astype(F32) + back
    mid_grad[...] = grad
    low = grad.astype(BF16)
    for half in range(2):
        grad_wo[half] = tn(low, attended[:, 512 * half : 512 * half + 512]).astype(BF16)
    out_grad = jnp.concatenate([nn(low, full[2, 0]), nn(low, full[2, 1])], 1).astype(BF16)
    mask = window_mask(segq[...], segk[...])
    lane_row = lax.broadcasted_iota(jnp.int32, (1, 128), 1)
    lane = lax.broadcasted_iota(jnp.int32, (256, 128), 1) < 64
    sink_grads = jnp.zeros((1, 128), F32)
    for g in range(8):
        part = slice(128 * g, 128 * g + 128)
        keys, values = head_pair(keyvals[:, part])
        q = queries[:, part]
        grad_block = out_grad[:, part]
        scores = nt(q, keys) * SCALE
        share_grads = nt(grad_block, values)
        shares, score_grads = [], []
        for h in range(2):
            columns = slice(256 * h, 256 * h + 256)
            log_total = logsum[:, 2 * g + h : 2 * g + h + 1]
            share = jnp.exp(jnp.where(mask, scores[:, columns], NEG) - log_total)
            term = jnp.sum(share * share_grads[:, columns], -1, keepdims=True)
            shares.append(share.astype(BF16))
            score_grads.append((share * (share_grads[:, columns] - term)).astype(BF16))
            sink_part = -jnp.sum(jnp.exp(sinks[2 * g + h] - log_total) * term, 0, keepdims=True)
            sink_grads = jnp.where(lane_row == 2 * g + h, sink_part, sink_grads)
        shares = jnp.concatenate(shares, 1)
        score_grads = jnp.concatenate(score_grads, 1)
        dq[:, part] = nn(score_grads, keys) * SCALE
        from_scores = tn(score_grads, q) * SCALE
        from_shares = tn(shares, grad_block)
        joined = jnp.where(
            lane,
            from_scores[:256] + pltpu.roll(from_scores[256:], 64, 1),
            pltpu.roll(from_shares[:256], 64, 1) + from_shares[256:],
        )
        halo[:, part] = joined[:128].astype(BF16)
        dkv[:, part] = joined[128:]
    grad_sink[...] = sink_grads


def attn_finish_kernel(
    dq, dkv, halo, cosq, sinq, cosk, sink_k, normed1, full, tok, gain1, mid_grad,
    grad_tokens, grad_w, grad_gain1,
):
    grad_q = dq[...]
    grad_kv = dkv[...] + halo[...].astype(F32)
    low_q = (grad_q * tiled(cosq[...]) - rope_partner(grad_q) * tiled(sinq[...])).astype(BF16)
    low_kv = (
        grad_kv * tiled(cosk[128:]) - rope_partner(grad_kv) * tiled(sink_k[128:])
    ).astype(BF16)
    normed = normed1[...]
    back = jnp.zeros((128, 1024), F32)
    for half in range(2):
        columns = slice(512 * half, 512 * half + 512)
        grad_w[0, half] = tn(normed, low_q[:, columns]).astype(BF16)
        grad_w[1, half] = tn(normed, low_kv[:, columns]).astype(BF16)
        back = back + nt(low_q[:, columns], full[0, half]) + nt(low_kv[:, columns], full[1, half])
    norm_grad, gain_part = norm_back(tok[...].astype(F32), gain1[...], back)
    grad_gain1[...] = gain_part
    grad_tokens[...] = mid_grad[...] + norm_grad


def expert_kernel(
    rows, cots, gate, weights, bias_gate, bias_up, bias_down,
    out_rows, back_rows, dots, grads, grad_bias,
):
    w_gate = jnp.concatenate([weights[m, 0, 0] for m in range(8)], 1)
    w_up = jnp.concatenate([weights[m, 1, 0] for m in range(8)], 1)
    w_down = jnp.concatenate([weights[m, 2, 0] for m in range(8)], 1)
    x = rows[0].reshape(2 * CAP, 1024)
    tanh_gate = jnp.tanh((nt(x, w_gate) + bias_gate[0]) / CLAMP)
    tanh_up = jnp.tanh((nt(x, w_up) + bias_up[0]) / CLAMP)
    soft_gate, soft_up = CLAMP * tanh_gate, CLAMP * tanh_up
    sig = jax.nn.sigmoid(SLOPE * soft_gate)
    glu = soft_gate * sig
    hidden = (glu * (soft_up + 1.0)).astype(BF16)
    produced = nn(hidden, w_down) + bias_down[0]
    share = gate[0]
    cot = cots[0].reshape(2 * CAP, 1024).astype(F32)
    out_rows[0] = (share * produced).astype(BF16).reshape(2, CAP, 1024)
    products = produced * cot
    partial = products[:, :128]
    for m in range(1, 8):
        partial = partial + products[:, 128 * m : 128 * m + 128]
    dots[0] = partial.reshape(2, CAP, 128)
    scaled = share * cot
    grad_bias[0, :, 1024:] = jnp.sum(scaled, 0, keepdims=True)
    rows_grad = scaled.astype(BF16)
    hidden_grad = nt(rows_grad, w_down)
    gate_grad = (
        hidden_grad
        * (soft_up + 1.0)
        * (sig + SLOPE * glu * (1.0 - sig))
        * (1.0 - tanh_gate * tanh_gate)
    )
    up_grad = hidden_grad * glu * (1.0 - tanh_up * tanh_up)
    grad_bias[0, :, :512] = jnp.sum(gate_grad, 0, keepdims=True)
    grad_bias[0, :, 512:1024] = jnp.sum(up_grad, 0, keepdims=True)
    gate_low, up_low = gate_grad.astype(BF16), up_grad.astype(BF16)
    back_rows[0] = (nn(gate_low, w_gate) + nn(up_low, w_up)).astype(BF16).reshape(2, CAP, 1024)
    for w, (left, right) in enumerate(((gate_low, x), (up_low, x), (hidden, rows_grad))):
        grad = tn(left, right).astype(BF16)
        for m in range(8):
            grads[m, w, 0] = grad[:, 128 * m : 128 * m + 128]


def expert_block(rows, cots, gate, weights, bias_gate, bias_up, bias_down):
    def per(shape, *lead_dims):
        return pl.BlockSpec(lead_dims + shape, lambda e: (e,) + (0,) * len(shape))

    stacked = pl.BlockSpec((8, 3, 1, 512, 128), lambda e: (0, 0, e, 0, 0))
    return plain(
        expert_kernel,
        [
            ((2, 2, CAP, 1024), BF16),
            ((2, 2, CAP, 1024), BF16),
            ((2, 2, CAP, 128), F32),
            ((8, 3, 2, 512, 128), BF16),
            ((2, 1, 2048), F32),
        ],
        [
            per((2, CAP, 1024), 1),
            per((2, CAP, 1024), 1),
            per((2 * CAP, 1), 1),
            stacked,
            per((1, 512), 1),
            per((1, 512), 1),
            per((1, 1024), 1),
        ],
        "experts",
        rows,
        cots,
        gate,
        weights,
        bias_gate,
        bias_up,
        bias_down,
        grid=(2,),
        out_specs=[
            per((2, CAP, 1024), 1),
            per((2, CAP, 1024), 1),
            per((2, CAP, 128), 1),
            stacked,
            per((1, 2048), 1),
        ],
    )


def local(
    tokens, gain_attention, w_query, key_value_weight, w_output, sinks, gain_expert,
    w_gate, w_up, w_down, bias_gate, bias_up, bias_down, gates, routes, segments, cotangent,
):
    core, rank = lax.axis_index("core"), lax.axis_index("tp")
    core_arg = core.reshape(1).astype(jnp.int32)
    gain1, gain2 = gain_attention[None], gain_expert[None]

    raw = jnp.stack([w_gate, w_up, w_down])
    (pair,) = exchange([(raw, (2, 3, 64, 2048), whole, lead)], ("c",), 0, "weights_pair")
    (sorted_w,) = plain(
        sort_kernel, [((8, 3, 2, 64, 128), BF16)], [SM, VM], "weights_sort", core_arg, pair
    )
    (mine,) = exchange(
        [(sorted_w, (3, 2, 8, 64, 128), lead, third)], ("xl", "y"), 1, "weights_deal"
    )
    weights = lax.all_gather(mine.reshape(3, 2, 512, 128), "m", axis=0, tiled=False)

    shards = jnp.stack([w_query, key_value_weight, w_output.T])
    shards, mine = lax.optimization_barrier((shards, mine))
    full, cot_rows, prev = attn_gather(shards, cotangent, tokens, 2)
    full = full.reshape(3, 2, 1024, 512)

    length = routes.shape[0]
    labels = 4 * rank + jnp.arange(4, dtype=jnp.int32)
    named = routes[:, :, None] == labels
    hit = jnp.any(named, 1)
    share = jnp.sum(jnp.where(named, gates[:, :, None], 0.0), 1)
    token = jnp.arange(length, dtype=jnp.int32)
    below = (token[:, None] > token[None, :]).astype(BF16)
    earlier = jnp.dot(below, hit.astype(BF16), preferred_element_type=F32).astype(jnp.int32)
    place = jnp.where(hit, earlier, -1)
    place_t = place.T
    slots = jnp.arange(CAP, dtype=jnp.int32)
    hot = place_t[:, None, :] == slots[None, :, None]
    pick = hot.astype(BF16).reshape(4 * CAP, length)
    slot_share = jnp.sum(jnp.where(hot, share.T[:, None, :], 0.0), -1)

    segq = lax.dynamic_slice_in_dim(segments, rank * 128, 128, 0)
    seg_prev = lax.dynamic_slice_in_dim(segments, jnp.maximum(rank * 128 - 128, 0), 128, 0)
    seg_prev = jnp.where(rank == 0, -1, seg_prev)
    segk = jnp.concatenate([seg_prev, segq])[None]
    segq = segq[:, None]
    frequency = ROPE_BASE ** (-2.0 * jnp.arange(32, dtype=F32) / HEAD_DIM)
    position = (rank * 128 - 128 + jnp.arange(256, dtype=jnp.int32)).astype(F32)
    angles = position[:, None] * frequency[None, :]
    cosine, sine = jnp.cos(angles), jnp.sin(angles)
    one, zero = jnp.ones((256, 64), F32), jnp.zeros((256, 64), F32)
    cosk = jnp.concatenate([cosine, cosine, one], 1)
    sin_k = jnp.concatenate([-sine, sine, zero], 1)
    cosq = jnp.concatenate([cosine] * 4, 1)[128:]
    sinq = jnp.concatenate([-sine, sine] * 2, 1)[128:]
    mid, normed2, normed1, queries, keyvals, attended, logsum = plain(
        attn_forward_kernel,
        [
            ((128, 1024), F32),
            ((128, 1024), BF16),
            ((128, 1024), BF16),
            ((128, 1024), BF16),
            ((256, 1024), BF16),
            ((128, 1024), BF16),
            ((128, 128), F32),
        ],
        [SM] + [VM] * 11,
        "attn_forward",
        sinks, tokens, prev, full, gain1, gain2, segq, segk, cosq, sinq, cosk, sin_k,
    )

    sequence = gather_rows(normed2, 3, "rows_gather").reshape(1024, 1024)
    rows = jnp.dot(pick, sequence, preferred_element_type=F32).astype(BF16)
    cots = jnp.dot(pick, cot_rows.reshape(1024, 1024), preferred_element_type=F32).astype(BF16)
    padded = jnp.pad(slot_share, ((0, 0), (0, 384 - CAP))).reshape(2, 2, 384)
    slot_shape = (2, 2, CAP, 1024)
    rows, cots, padded = exchange(
        [
            (rows.reshape(slot_shape), slot_shape, lead, second),
            (cots.reshape(slot_shape), slot_shape, lead, second),
            (padded, (2, 2, 384), lead, lead),
        ],
        ("c",),
        4,
        "slots_pair",
    )
    slot_gate = padded.transpose(1, 0, 2)[:, :, :CAP].reshape(2, 2 * CAP, 1)
    first = 4 * rank + 2 * core
    expert_bias = [
        lax.dynamic_slice_in_dim(b, first, 2, 0)[:, None] for b in (bias_gate, bias_up, bias_down)
    ]
    out_rows, back_rows, dots, grads, grad_bias = expert_block(
        rows, cots, slot_gate, weights, *expert_bias
    )
    grads = lax.psum_scatter(grads, "m", scatter_dimension=0, tiled=False)

    out_rows, back_rows, dots = exchange(
        [
            (out_rows, slot_shape, second, lead),
            (back_rows, slot_shape, second, lead),
            (dots, (2, 2, CAP, 128), second, lead),
        ],
        ("c",),
        5,
        "slots_back",
    )
    unpick = (place[:, :, None] == slots).astype(BF16).reshape(length, 4 * CAP)
    out_tokens = jnp.dot(
        unpick, out_rows.reshape(4 * CAP, 1024), preferred_element_type=F32
    ).astype(BF16)
    back_tokens = jnp.dot(
        unpick, back_rows.reshape(4 * CAP, 1024), preferred_element_type=F32
    ).astype(BF16)
    slot_dots = jnp.sum(dots, -1).reshape(4, CAP)
    token_dots = jnp.sum(jnp.where(hot, slot_dots[:, :, None], 0.0), 1)
    token_dots = token_dots.reshape(4, 8, 128).transpose(1, 0, 2)
    part_shape = (8, 128, 1024)
    back_parts, out_parts, dot_parts = exchange(
        [
            (back_tokens.reshape(part_shape), part_shape, lead, lead),
            (out_tokens.reshape(part_shape), part_shape, lead, lead),
            (token_dots, (8, 4, 128), lead, lead),
        ],
        ("xl", "y"),
        6,
        "tokens_back",
    )
    own_routes = lax.dynamic_slice_in_dim(routes, rank * 128, 128, 0)
    all_dots = dot_parts.reshape(32, 128).T
    chosen = own_routes[:, :, None] == jnp.arange(32, dtype=jnp.int32)
    grad_gates = jnp.sum(jnp.where(chosen, all_dots[:, None, :], 0.0), -1)

    layer_out, mid_grad, dq, halo, dkv, grad_wo, grad_gain2, grad_sink = plain(
        attn_backward_kernel,
        [
            ((128, 1024), F32),
            ((128, 1024), F32),
            ((128, 1024), F32),
            ((128, 1024), BF16),
            ((128, 1024), F32),
            ((2, 1024, 512), BF16),
            ((1, 1024), F32),
            ((1, 128), F32),
        ],
        [SM] + [VM] * 12,
        "attn_backward",
        sinks, back_parts, out_parts, mid, cotangent, gain2, full, queries, keyvals, attended,
        logsum, segq, segk,
    )
    halo = shift_back(halo, 7)
    grad_tokens, grad_w, grad_gain1 = plain(
        attn_finish_kernel,
        [((128, 1024), F32), ((2, 2, 1024, 512), BF16), ((1, 1024), F32)],
        [VM] * 12,
        "attn_finish",
        dq, dkv, halo, cosq, sinq, cosk, sin_k, normed1, full, tokens, gain1, mid_grad,
    )
    parts = jnp.concatenate([grad_w, grad_wo[None]]).reshape(3, 2, 2, 4, 2, 64, 512)
    owned = attn_reduce(parts, 8)

    (dealt,) = exchange(
        [(grads.reshape(3, 2, 8, 64, 128), (8, 3, 2, 64, 128), third, lead)],
        ("xl", "y"),
        9,
        "grads_deal",
    )
    (unsorted,) = plain(
        unsort_kernel, [((2, 3, 64, 2048), BF16)], [SM, VM], "grads_unsort", core_arg, dealt
    )
    (halves,) = exchange([(unsorted, (2, 3, 64, 2048), lead, lead)], ("c",), 10, "grads_pair")
    grad_experts = halves[0].astype(F32) + halves[1].astype(F32)

    sink_row = jnp.pad(grad_sink, ((0, 0), (0, 896)))
    small = jnp.concatenate(
        [grad_gain1, grad_gain2, sink_row, jnp.zeros_like(sink_row), grad_bias.reshape(4, 1024)]
    )
    totals = small_sums(small, 11)
    sums = jnp.sum(totals[:, :3], 0)
    biases = totals[:, 4:].reshape(2, 8, 2, 2048).transpose(1, 0, 2, 3).reshape(32, 2048)
    return (
        layer_out,
        grad_tokens,
        sums[0],
        owned[0],
        owned[1],
        owned[2].T,
        sums[2, :16],
        sums[1],
        grad_experts[0],
        grad_experts[1],
        grad_experts[2],
        biases[:, :512],
        biases[:, 512:1024],
        biases[:, 1024:],
        grad_gates,
    )


def shift_kernel(src, out, sems):
    here = coords()
    rank = here["xl"] * 4 + here["y"]
    after, before = (rank + 1) % 8, (rank + 7) % 8
    after_place = dict(here, xl=after // 4, y=after % 4)
    before_place = dict(here, xl=before // 4, y=before % 4)
    greet([after_place, before_place])
    copy = remote(src, out, sems.at[0], sems.at[1], before_place)
    copy.start()
    copy.wait()


def shift_back(rows, ident):
    return pl.pallas_call(
        shift_kernel,
        out_shape=jax.ShapeDtypeStruct(rows.shape, rows.dtype),
        in_specs=[ANY],
        out_specs=ANY,
        scratch_shapes=[pltpu.SemaphoreType.DMA((2,))],
        compiler_params=comm_params(ident),
        name="halo_back",
    )(rows)


def solution(mesh):
    fine = Mesh(mesh.devices.reshape(8, 2, 8), ("m", "core", "tp"))
    fsdp = ("m", "core")
    rows = P(("m", "core", "tp"), None)
    return jax.shard_map(
        local,
        mesh=fine,
        in_specs=(
            rows,
            P(),
            P(fsdp, "tp"),
            P(fsdp, "tp"),
            P("tp", fsdp),
            P(),
            P(),
            P(fsdp, "tp"),
            P(fsdp, "tp"),
            P(fsdp, "tp"),
            P(),
            P(),
            P(),
            P(fsdp, None),
            P(fsdp, None),
            P(fsdp),
            rows,
        ),
        out_specs=(
            rows,
            rows,
            P(),
            P(fsdp, "tp"),
            P(fsdp, "tp"),
            P("tp", fsdp),
            P(),
            P(),
            P(fsdp, "tp"),
            P(fsdp, "tp"),
            P(fsdp, "tp"),
            P(),
            P(),
            P(),
            rows,
        ),
        check_vma=False,
    )
```

```python
import functools
import itertools

import jax
import jax.numpy as jnp
from jax import lax
from jax.experimental import pallas as pl
from jax.experimental.pallas import tpu as pltpu
from jax.sharding import Mesh
from jax.sharding import PartitionSpec as P

MESH = pl.DeviceIdType.MESH
HEAD_DIM = 64
WINDOW = 128
EPS = 1e-05
ROPE_BASE = 10000.0
CLAMP = 7.0
SLOPE = 1.702
SCALE = HEAD_DIM ** (-0.5)
NEG = -1e30
CAP = 272
F32 = jnp.float32
BF16 = jnp.bfloat16
ANY = pl.BlockSpec(memory_space=pl.ANY)
VM = pl.BlockSpec(memory_space=pltpu.VMEM)
SM = pl.BlockSpec(memory_space=pltpu.SMEM)
VMEM_LIMIT = 56 * 1024 * 1024

SIZES = {"xh": 2, "z": 4, "c": 2, "xl": 2, "y": 4, "x": 4}


def coords():
    xh, z = lax.axis_index("xh"), lax.axis_index("z")
    c, t = lax.axis_index("core"), lax.axis_index("tp")
    xl, y = t // 4, t % 4
    return {"xh": xh, "z": z, "c": c, "xl": xl, "y": y, "x": 2 * xh + xl}


def moved(place, offset):
    out = dict(place)
    for axis, step in offset.items():
        out[axis] = (place[axis] + step) % SIZES[axis]
        if axis == "x":
            out["xh"], out["xl"] = out["x"] // 2, out["x"] % 2
    return out


def device(place):
    return (place["xh"], place["z"], place["c"], place["xl"] * 4 + place["y"])


def offsets(axes):
    ranges = [range(SIZES[a]) for a in axes]
    return [dict(zip(axes, o)) for o in itertools.product(*ranges) if any(o)]


def slot(place, axes):
    out = 0
    for a in axes:
        out = out * SIZES[a] + place[a]
    return out


def greet(peers):
    barrier = pltpu.get_barrier_semaphore()
    for peer in peers:
        pl.semaphore_signal(barrier, inc=1, device_id=device(peer), device_id_type=MESH)
    pl.semaphore_wait(barrier, len(peers))


def remote(src, dst, send, recv, peer):
    return pltpu.make_async_remote_copy(
        src_ref=src,
        dst_ref=dst,
        send_sem=send,
        recv_sem=recv,
        device_id=device(peer),
        device_id_type=MESH,
    )


def comm_params(ident):
    return pltpu.CompilerParams(
        collective_id=ident, has_side_effects=True, vmem_limit_bytes=VMEM_LIMIT
    )


class Exchange:
    def __init__(self, axes, views, ins, outs, bounce, send, recv, load, store):
        self.here, self.offs, self.views = coords(), offsets(axes), views
        self.ins, self.outs, self.send, self.recv = ins, outs, send, recv
        self.loads, self.stores, self.copies = [], [], []
        for i, (src, dst) in enumerate(views):
            view = dst(outs[i], self.here)
            self.loads.append(
                pltpu.make_async_copy(src(ins[i], self.here), bounce[i], load.at[i])
            )
            self.stores.append(pltpu.make_async_copy(bounce[i], view, store.at[i]))
            self.loads[i].start()

    def peers(self):
        return [moved(self.here, o) for o in self.offs]

    def start(self):
        for k, o in enumerate(self.offs):
            peer = moved(self.here, o)
            for i, (src, dst) in enumerate(self.views):
                copy = remote(
                    src(self.ins[i], peer),
                    dst(self.outs[i], self.here),
                    self.send.at[i, k],
                    self.recv.at[i, k],
                    peer,
                )
                copy.start()
                self.copies.append(copy)
        for first, then in zip(self.loads, self.stores):
            first.wait()
            then.start()

    def finish(self):
        for copy in self.stores + self.copies:
            copy.wait()


def exchange_scratch(items, axes):
    sems = pltpu.SemaphoreType.DMA((len(items), len(offsets(axes))))
    own = pltpu.SemaphoreType.DMA((len(items),))
    return [pltpu.VMEM(shape, a.dtype) for a, _, shape, _, _ in items] + [sems, sems, own, own]


def exchange_kernel(axes, views, *refs):
    n = len(views)
    swap = Exchange(axes, views, refs[:n], refs[n : 2 * n], refs[2 * n : 3 * n], *refs[3 * n :])
    greet(swap.peers())
    swap.start()
    swap.finish()


def exchange(items, axes, ident, name):
    return pl.pallas_call(
        functools.partial(exchange_kernel, axes, [item[3:] for item in items]),
        out_shape=[jax.ShapeDtypeStruct(item[1], item[0].dtype) for item in items],
        in_specs=[ANY] * len(items),
        out_specs=[ANY] * len(items),
        scratch_shapes=exchange_scratch(items, axes),
        compiler_params=comm_params(ident),
        name=name,
    )(*[item[0] for item in items])


def whole(ref, place):
    return ref


def by_core(ref, place):
    return ref.at[place["c"]]


def by_core_second(ref, place):
    return ref.at[:, place["c"]]


def by_rank(ref, place):
    return ref.at[place["xl"] * 4 + place["y"]]


def deal_to(ref, place):
    return ref.at[place["xh"], :, :, place["xl"] * 4 + place["y"]]


def dealt_from(ref, place):
    return ref.at[place["xh"], place["xl"] * 4 + place["y"]]


class RowGather:
    copies = 8

    def __init__(self, here, src, out, send, recv):
        self.src, self.out, self.send, self.recv, self.here = src, out, send, recv, here
        half = src.shape[-1] // 2
        self.left, self.right = pl.ds(0, half), pl.ds(half, half)
        self.started = []

    def go(self, k, src, dst, offset):
        copy = remote(src, dst, self.send.at[k], self.recv.at[k], moved(self.here, offset))
        copy.start()
        self.started.append(copy)

    def first(self):
        xl, y = self.here["xl"], self.here["y"]
        self.go(0, self.src.at[:, self.left], self.out.at[xl, y, :, self.left], {"xl": 1})
        for k in (1, 3, 2):
            self.go(
                k, self.src.at[:, self.right], self.out.at[xl, y, :, self.right], {"y": k}
            )

    def then(self):
        xl, y = self.here["xl"], self.here["y"]
        self.started[0].wait_recv()
        for k in (1, 3, 2):
            view = self.out.at[:, y, :, self.left]
            self.go(3 + k, view, view, {"y": k})
        for copy in self.started[1:4]:
            copy.wait_recv()
        view = self.out.at[xl, :, :, self.right]
        self.go(7, view, view, {"xl": 1})

    def finish(self):
        for copy in self.started[4:]:
            copy.wait_recv()
        for copy in self.started:
            copy.wait_send()


def rows_kernel(src, out, send, recv, own):
    here = coords()
    local_copy = pltpu.make_async_copy(src, out.at[here["xl"], here["y"]], own)
    local_copy.start()
    greet([moved(here, o) for o in [{"xl": 1}, {"y": 1}, {"y": 2}, {"y": 3}]])
    gather = RowGather(here, src, out, send, recv)
    gather.first()
    local_copy.wait()
    gather.then()
    gather.finish()


def gather_rows(rows, ident, name):
    return pl.pallas_call(
        rows_kernel,
        out_shape=jax.ShapeDtypeStruct((2, 4) + rows.shape, rows.dtype),
        in_specs=[VM],
        out_specs=ANY,
        scratch_shapes=[
            pltpu.SemaphoreType.DMA((8,)),
            pltpu.SemaphoreType.DMA((8,)),
            pltpu.SemaphoreType.DMA,
        ],
        compiler_params=comm_params(ident),
        name=name,
    )(rows)


ORDERS = (("z", "y", "x"), ("y", "x", "z"), ("x", "z", "y"))


def region(ref, p, place, held):
    xl = slice(None) if "x" in held else place["xl"]
    xh = slice(None) if "x" in held else place["xh"]
    z = slice(None) if "z" in held else place["z"]
    y = pl.ds(0, 512) if "y" in held else pl.ds(pl.multiple_of(place["y"] * 128, 128), 128)
    return ref.at[p, xl, xh, z, place["c"], :, y]


def attn_gather_kernel(
    shards, cot, tok, full, cot_full, prev, send, recv, csend, crecv, rsend, rrecv, hsem, own
):
    here = coords()
    local_copies = []
    for p in range(3):
        local_copies.append(
            pltpu.make_async_copy(shards.at[p], region(full, p, here, ()), own.at[p])
        )
    local_copies.append(
        pltpu.make_async_copy(cot, cot_full.at[here["xl"], here["y"]], own.at[3])
    )
    for copy in local_copies:
        copy.start()
    rank = here["xl"] * 4 + here["y"]
    after, before = (rank + 1) % 8, (rank + 7) % 8
    after_place = dict(here, xl=after // 4, y=after % 4)
    before_place = dict(here, xl=before // 4, y=before % 4)
    peers = [moved(here, {a: k}) for a in ("x", "y", "z") for k in (1, 2, 3)]
    peers += [moved(here, {"xl": 1}), moved(here, {"c": 1}), after_place, before_place]
    greet(peers)
    waits = [[None] * 3 for _ in range(3)]

    def start(p, s):
        view = region(full, p, here, ORDERS[p][:s])
        src = shards.at[p] if s == 0 else view
        waits[p][s] = []
        for k in (1, 3, 2):
            copy = remote(
                src,
                view,
                send.at[p, s, k - 1],
                recv.at[p, s, k - 1],
                moved(here, {ORDERS[p][s]: k}),
            )
            copy.start()
            waits[p][s].append(copy)

    for p in range(3):
        start(p, 0)
    halo = remote(tok, prev, hsem.at[0], hsem.at[1], after_place)
    halo.start()
    gather = RowGather(here, cot, cot_full, rsend, rrecv)
    gather.first()
    for copy in local_copies:
        copy.wait()
    for s in (1, 2):
        for p in range(3):
            for copy in waits[p][s - 1]:
                copy.wait_recv()
            start(p, s)
        if s == 1:
            gather.then()
    last = []
    for p in range(3):
        for copy in waits[p][2]:
            copy.wait_recv()
        view = full.at[p, :, :, :, here["c"]]
        copy = remote(view, view, csend.at[p], crecv.at[p], moved(here, {"c": 1}))
        copy.start()
        last.append(copy)
    for copy in last:
        copy.wait()
    halo.wait()
    gather.finish()
    for row in waits:
        for group in row:
            for copy in group:
                copy.wait_send()


def attn_gather(shards, cot, tok, ident):
    dma = pltpu.SemaphoreType.DMA
    return pl.pallas_call(
        attn_gather_kernel,
        out_shape=[
            jax.ShapeDtypeStruct((3, 2, 2, 4, 2, 64, 512), BF16),
            jax.ShapeDtypeStruct((2, 4) + cot.shape, BF16),
            jax.ShapeDtypeStruct(tok.shape, BF16),
        ],
        in_specs=[VM] * 3,
        out_specs=[ANY] * 3,
        scratch_shapes=[
            dma((3, 3, 3)),
            dma((3, 3, 3)),
            dma((3,)),
            dma((3,)),
            dma((8,)),
            dma((8,)),
            dma((2,)),
            dma((4,)),
        ],
        compiler_params=comm_params(ident),
        name="attn_gather",
    )(shards, cot, tok)


def piece(axis, place, dims):
    index = []
    for d in dims:
        if d == "xl":
            index.append(place["xl"] if axis == "x" else slice(None))
        elif d == "xh":
            index.append(place["xh"] if axis == "x" else slice(None))
        elif d == "z":
            index.append(place["z"] if axis == "z" else slice(None))
    index.append(slice(None))
    if axis == "y":
        index.append(pl.ds(pl.multiple_of(place["y"] * 128, 128), 128))
    else:
        index.append(slice(None))
    return tuple(index)


def reduce_shapes(p):
    dims, lanes = ["xl", "xh", "z"], 512
    shapes = [((2, 2, 4, 64, 512), tuple(dims))]
    for axis in ORDERS[p][::-1]:
        if axis == "x":
            dims = [d for d in dims if d not in ("xl", "xh")]
        elif axis == "z":
            dims = [d for d in dims if d != "z"]
        else:
            lanes = 128
        shapes.append((tuple(SIZES[d] for d in dims) + (64, lanes), tuple(dims)))
    return shapes


class AttnReduce:
    def __init__(self, here, parts, got0, sums, gots, outs, csend, crecv, send, recv):
        self.here, self.parts, self.got0, self.sums = here, parts, got0, sums
        self.gots, self.outs, self.csend, self.crecv = gots, outs, csend, crecv
        self.send, self.recv = send, recv
        self.other = moved(here, {"c": 1})
        self.shapes = [reduce_shapes(p) for p in range(3)]
        self.started, self.cores, self.pending = [], [], [None] * 3

    def peers(self):
        return [moved(self.here, {a: k}) for a in ("x", "y", "z") for k in (1, 2, 3)] + [self.other]

    def swap(self):
        for p in range(3):
            copy = remote(
                self.parts[p].at[:, :, :, self.other["c"]],
                self.got0[p],
                self.csend.at[p],
                self.crecv.at[p],
                self.other,
            )
            copy.start()
            self.cores.append(copy)

    def go(self, p, s):
        axis = ORDERS[p][2 - s]
        dims = self.shapes[p][s][1]
        group = []
        for k in (1, 3, 2):
            peer = moved(self.here, {axis: k})
            copy = remote(
                self.sums[p][s].at[piece(axis, peer, dims)],
                self.gots[p][s].at[k - 1],
                self.send.at[p, s, k - 1],
                self.recv.at[p, s, k - 1],
                peer,
            )
            copy.start()
            group.append(copy)
        self.started.append(group)
        self.pending[p] = group

    def first(self):
        for p in range(3):
            self.cores[p].wait_recv()
            mine = self.parts[p][:, :, :, self.here["c"]].astype(F32)
            self.sums[p][0][...] = (mine + self.got0[p][...].astype(F32)).astype(BF16)
            self.go(p, 0)

    def step(self, s):
        for p in range(3):
            axis = ORDERS[p][2 - s]
            dims = self.shapes[p][s][1]
            for copy in self.pending[p]:
                copy.wait_recv()
            total = self.sums[p][s][piece(axis, self.here, dims)].astype(F32)
            for k in range(3):
                total = total + self.gots[p][s][k].astype(F32)
            if s == 2:
                self.outs[p][...] = total.T if p == 2 else total
            else:
                self.sums[p][s + 1][...] = total.astype(BF16)
                self.go(p, s + 1)

    def finish(self):
        for copy in self.cores:
            copy.wait_send()
        for group in self.started:
            for copy in group:
                copy.wait_send()


DEAL_AXES = ("xh", "xl", "y")


def final_kernel(*refs):
    grad_w, grad_wo, small, dealt = refs[:4]
    out_q, out_kv, out_o, sums_out, bias_gate, bias_up, bias_down, deal_out = refs[4:12]
    rest = list(refs[12:])

    def take(n):
        got = rest[:n]
        del rest[:n]
        return got

    here = coords()
    deal = Exchange(DEAL_AXES, [(deal_to, dealt_from)], [dealt], [deal_out], take(1), *take(4))
    got0 = take(3)
    sums = [take(3) for _ in range(3)]
    gots = [take(3) for _ in range(3)]
    reduce = AttnReduce(
        here, [grad_w.at[0], grad_w.at[1], grad_wo], got0, sums, gots, (out_q, out_kv, out_o), *take(4)
    )
    small_got, small_all, send1, recv1, send2, recv2 = take(6)
    first, then = offsets(("xh", "z")), offsets(("c", "xl", "y"))
    greet(reduce.peers() + deal.peers() + [moved(here, o) for o in first + then])
    reduce.swap()
    copies = []
    for k, o in enumerate(first):
        copy = remote(small, small_got.at[k], send1.at[k], recv1.at[k], moved(here, o))
        copy.start()
        copies.append(copy)
    reduce.first()
    deal.start()
    total = small[...]
    for k in range(len(first)):
        copies[k].wait_recv()
        total = total + small_got[k]
    mine = small_all.at[here["c"] * 8 + here["xl"] * 4 + here["y"]]
    mine[...] = total
    for k, o in enumerate(then):
        copy = remote(mine, mine, send2.at[k], recv2.at[k], moved(here, o))
        copy.start()
        copies.append(copy)
    reduce.step(0)
    reduce.step(1)
    for copy in copies[len(first) :]:
        copy.wait_recv()
    total = small_all[0, :4]
    for k in range(1, 16):
        total = total + small_all[k, :4]
    sums_out[...] = total
    for c in range(2):
        for j in range(8):
            for e in range(2):
                row = small_all[c * 8 + j, 4 + 2 * e : 6 + 2 * e]
                at = slice(4 * j + 2 * c + e, 4 * j + 2 * c + e + 1)
                bias_gate[at] = row[0:1, :512]
                bias_up[at] = row[0:1, 512:]
                bias_down[at] = row[1:2]
    reduce.step(2)
    reduce.finish()
    deal.finish()
    for copy in copies:
        copy.wait_send()


def final_exchange(grad_w, grad_wo, small, grads, ident):
    dma = pltpu.SemaphoreType.DMA
    shapes = [reduce_shapes(p) for p in range(3)]
    scratch = exchange_scratch([(grads, None, (3, 2, 64, 128), None, None)], DEAL_AXES)
    scratch += [pltpu.VMEM((2, 2, 4, 64, 512), BF16) for _ in range(3)]
    for p in range(3):
        scratch += [pltpu.VMEM(shapes[p][s][0], BF16) for s in range(3)]
    for p in range(3):
        scratch += [pltpu.VMEM((3,) + shapes[p][s + 1][0], BF16) for s in range(3)]
    scratch += [dma((3,)), dma((3,)), dma((3, 3, 3)), dma((3, 3, 3))]
    scratch += [pltpu.VMEM((7, 8, 1024), F32), pltpu.VMEM((16, 8, 1024), F32)]
    scratch += [dma((7,)), dma((7,)), dma((15,)), dma((15,))]
    outs = [(64, 128), (64, 128), (128, 64), (4, 1024), (32, 512), (32, 512), (32, 1024)]
    return pl.pallas_call(
        final_kernel,
        out_shape=[jax.ShapeDtypeStruct(o, F32) for o in outs]
        + [jax.ShapeDtypeStruct((2, 8, 3, 2, 64, 128), BF16)],
        in_specs=[VM, VM, VM, ANY],
        out_specs=[VM] * 7 + [ANY],
        scratch_shapes=scratch,
        compiler_params=comm_params(ident),
        name="final_exchange",
    )(grad_w, grad_wo, small, grads)


def reduce_rows_kernel(count, *refs):
    parts, dots = refs[:count], refs[count]
    outs, dots_out = refs[count + 1 : 2 * count + 1], refs[2 * count + 1]
    rest = list(refs[2 * count + 2 :])
    got_y, sum_y, got_x, sum_x = (rest[i * count : (i + 1) * count] for i in range(4))
    lgot, rgot = (rest[i * count : (i + 1) * count] for i in (4, 5))
    send, recv, dsend, drecv, own = rest[6 * count :]
    here = coords()
    xl, y = here["xl"], here["y"]
    side = moved(here, {"xl": 1})
    ups = [moved(here, {"y": k}) for k in (1, 2, 3)]
    offs = offsets(("xl", "y"))
    keep = pltpu.make_async_copy(dots.at[xl * 4 + y], dots_out.at[xl * 4 + y], own)
    keep.start()
    greet([moved(here, o) for o in offs])
    left, right = pl.ds(0, 512), pl.ds(512, 512)
    copies = []

    def go(src, dst, i, k, peer):
        copy = remote(src, dst, send.at[i, k], recv.at[i, k], peer)
        copy.start()
        copies.append(copy)
        return copy

    ys, xs = [], []
    for i in range(count):
        xs.append(go(parts[i].at[side["xl"], :, :, right], got_x[i], i, 3, side))
        ys.append(
            [
                go(parts[i].at[:, ups[k]["y"], :, left], got_y[i].at[k], i, k, ups[k])
                for k in (0, 2, 1)
            ]
        )
    for k, o in enumerate(offs):
        peer = moved(here, o)
        rank = peer["xl"] * 4 + peer["y"]
        copy = remote(
            dots.at[rank], dots_out.at[xl * 4 + y], dsend.at[k], drecv.at[k], peer
        )
        copy.start()
        copies.append(copy)
    lasts = []
    for i in range(count):
        xs[i].wait_recv()
        sum_x[i][...] = (
            parts[i][xl, :, :, right].astype(F32) + got_x[i][...].astype(F32)
        ).astype(BF16)
        rights = [
            go(sum_x[i].at[ups[k]["y"]], rgot[i].at[k], i, 5 + k, ups[k]) for k in (0, 2, 1)
        ]
        for copy in ys[i]:
            copy.wait_recv()
        total = parts[i][:, y, :, left].astype(F32)
        for k in range(3):
            total = total + got_y[i][k].astype(F32)
        sum_y[i][...] = total.astype(BF16)
        lasts.append((go(sum_y[i].at[side["xl"]], lgot[i], i, 4, side), rights))
    for i in range(count):
        lasts[i][0].wait_recv()
        outs[i][:, left] = sum_y[i][xl].astype(F32) + lgot[i][...].astype(F32)
        for copy in lasts[i][1]:
            copy.wait_recv()
        total = sum_x[i][y].astype(F32)
        for k in range(3):
            total = total + rgot[i][k].astype(F32)
        outs[i][:, right] = total
    for k in range(len(offs)):
        copies[4 * count + k].wait_recv()
    for copy in copies:
        copy.wait_send()
    keep.wait()


def reduce_rows(parts, dots, ident, name):
    dma = pltpu.SemaphoreType.DMA
    n = len(parts)
    scratch = []
    for shape in ((3, 2, 128, 512), (2, 128, 512), (4, 128, 512), (4, 128, 512)):
        scratch += [pltpu.VMEM(shape, BF16) for _ in range(n)]
    scratch += [pltpu.VMEM((128, 512), BF16) for _ in range(n)]
    scratch += [pltpu.VMEM((3, 128, 512), BF16) for _ in range(n)]
    scratch += [dma((n, 8)), dma((n, 8)), dma((7,)), dma((7,)), dma]
    return pl.pallas_call(
        functools.partial(reduce_rows_kernel, n),
        out_shape=[jax.ShapeDtypeStruct((128, 1024), F32) for _ in range(n)]
        + [jax.ShapeDtypeStruct(dots.shape, F32)],
        in_specs=[VM] * (n + 1),
        out_specs=[VM] * (n + 1),
        scratch_shapes=scratch,
        compiler_params=comm_params(ident),
        name=name,
    )(*parts, dots)


def plain(kernel, outs, in_specs, name, *args, grid=None, out_specs=None, scratch=()):
    extra = {} if grid is None else {"grid": grid}
    return pl.pallas_call(
        kernel,
        out_shape=[jax.ShapeDtypeStruct(s, d) for s, d in outs],
        in_specs=in_specs,
        out_specs=out_specs or [VM] * len(outs),
        scratch_shapes=list(scratch),
        compiler_params=pltpu.CompilerParams(vmem_limit_bytes=VMEM_LIMIT),
        name=name,
        **extra,
    )(*args)


def nn(a, b):
    return lax.dot_general(a, b, (((1,), (0,)), ((), ())), preferred_element_type=F32)


def nt(a, b):
    return lax.dot_general(a, b, (((1,), (1,)), ((), ())), preferred_element_type=F32)


def tn(a, b):
    return lax.dot_general(a, b, (((0,), (0,)), ((), ())), preferred_element_type=F32)


def spread(rows, columns, core):
    row = lax.broadcasted_iota(jnp.int32, (rows, columns), 0)
    column = lax.broadcasted_iota(jnp.int32, (rows, columns), 1)
    expert = 4 * (row // 128) + 2 * core + (row // 64) % 2
    return (column == (row % 64) * 32 + expert).astype(F32).astype(BF16)


def sort_kernel(core_ref, gate_ref, up_ref, down_ref, out_ref):
    hot = spread(1024, 2048, core_ref[0])
    for w, ref in enumerate((gate_ref, up_ref, down_ref)):
        rows = ref[...].reshape(128, 2048)
        out_ref[:, w] = nt(hot, rows).astype(BF16).reshape(8, 2, 64, 128)


def unsort_kernel(core_ref, g_ref, out_ref):
    hot = spread(1024, 2048, core_ref[0])
    for w in range(3):
        rows = (g_ref[0, :, w].astype(F32) + g_ref[1, :, w].astype(F32)).astype(BF16)
        rows = rows.reshape(1024, 128)
        out_ref[:, w] = tn(rows, hot).astype(BF16).reshape(2, 64, 2048)


def rope_partner(values):
    lanes = values.shape[1]
    lane = lax.broadcasted_iota(jnp.int32, values.shape, 1)
    return jnp.where(
        lane % 64 < 32, pltpu.roll(values, lanes - 32, 1), pltpu.roll(values, 32, 1)
    )


def tiled(table):
    return jnp.concatenate([table] * 8, axis=1)


def head_pair(block):
    lane = lax.broadcasted_iota(jnp.int32, block.shape, 1) < 64
    wide = block.astype(F32)
    swapped = pltpu.roll(wide, 64, 1)
    zero = jnp.zeros_like(wide)
    keys = jnp.concatenate([jnp.where(lane, wide, zero), jnp.where(lane, zero, swapped)], 0)
    values = jnp.concatenate([jnp.where(lane, swapped, zero), jnp.where(lane, zero, wide)], 0)
    return keys.astype(BF16), values.astype(BF16)


def window_mask(segq, segk):
    row = lax.broadcasted_iota(jnp.int32, (128, 256), 0)
    column = lax.broadcasted_iota(jnp.int32, (128, 256), 1)
    distance = 128 + row - column
    return (segq == segk) & (distance >= 0) & (distance < WINDOW)


def attn_forward_kernel(
    sinks, tok, prev, full, gain1, gain2, segq, segk, cosq, sinq, cosk, sink_k,
    mid, normed2, normed1, queries, keyvals, attended, logsum,
):
    own = tok[...].astype(F32)
    both = jnp.concatenate([prev[...].astype(F32), own], 0)
    scale = lax.rsqrt(jnp.mean(both * both, -1, keepdims=True) + EPS)
    normed = (both * scale * gain1[...]).astype(BF16)
    normed_own = normed[128:]
    normed1[...] = normed_own
    q = jnp.concatenate([nn(normed_own, full[0, 0]), nn(normed_own, full[0, 1])], 1)
    kv = jnp.concatenate([nn(normed, full[1, 0]), nn(normed, full[1, 1])], 1)
    q = (q * tiled(cosq[...]) + rope_partner(q) * tiled(sinq[...])).astype(BF16)
    kv = (kv * tiled(cosk[...]) + rope_partner(kv) * tiled(sink_k[...])).astype(BF16)
    queries[...] = q
    keyvals[...] = kv
    mask = window_mask(segq[...], segk[...])
    lane = lax.broadcasted_iota(jnp.int32, (128, 128), 1)
    sums = jnp.zeros((128, 128), F32)
    for g in range(8):
        part = slice(128 * g, 128 * g + 128)
        keys, values = head_pair(kv[:, part])
        scores = nt(q[:, part], keys) * SCALE
        shares = []
        for h in range(2):
            masked = jnp.where(mask, scores[:, 256 * h : 256 * h + 256], NEG)
            sink = sinks[2 * g + h]
            peak = jnp.maximum(jnp.max(masked, -1, keepdims=True), sink)
            total = jnp.exp(sink - peak) + jnp.sum(
                jnp.exp(masked - peak), -1, keepdims=True
            )
            log_total = peak + jnp.log(total)
            shares.append(jnp.exp(masked - log_total).astype(BF16))
            sums = jnp.where(lane == 2 * g + h, log_total, sums)
        attended[:, part] = nn(jnp.concatenate(shares, 1), values).astype(BF16)
    logsum[...] = sums
    out = own + nt(attended[:, :512], full[2, 0]) + nt(attended[:, 512:], full[2, 1])
    mid[...] = out
    scale = lax.rsqrt(jnp.mean(out * out, -1, keepdims=True) + EPS)
    normed2[...] = (out * scale * gain2[...]).astype(BF16)


def norm_back(values, gain, grad):
    scale = lax.rsqrt(jnp.mean(values * values, -1, keepdims=True) + EPS)
    normed = values * scale
    weighted = gain * grad
    back = scale * (weighted - normed * jnp.mean(weighted * normed, -1, keepdims=True))
    return back, jnp.sum(grad * normed, 0, keepdims=True)


def attn_backward_kernel(
    sinks, moved_in, combined, mid, cot, gain2, full, queries, keyvals, attended, logsum,
    segq, segk,
    layer_out, mid_grad, dq, halo, dkv, grad_wo, grad_gain2, grad_sink,
):
    layer_out[...] = mid[...] + combined[...]
    back, gain_part = norm_back(mid[...], gain2[...], moved_in[...])
    grad_gain2[...] = gain_part
    grad = cot[...].astype(F32) + back
    mid_grad[...] = grad
    low = grad.astype(BF16)
    for half in range(2):
        grad_wo[half] = tn(low, attended[:, 512 * half : 512 * half + 512]).astype(BF16)
    out_grad = jnp.concatenate([nn(low, full[2, 0]), nn(low, full[2, 1])], 1).astype(BF16)
    mask = window_mask(segq[...], segk[...])
    lane_row = lax.broadcasted_iota(jnp.int32, (1, 128), 1)
    lane = lax.broadcasted_iota(jnp.int32, (256, 128), 1) < 64
    sink_grads = jnp.zeros((1, 128), F32)
    for g in range(8):
        part = slice(128 * g, 128 * g + 128)
        keys, values = head_pair(keyvals[:, part])
        q = queries[:, part]
        grad_block = out_grad[:, part]
        scores = nt(q, keys) * SCALE
        share_grads = nt(grad_block, values)
        shares, score_grads = [], []
        for h in range(2):
            columns = slice(256 * h, 256 * h + 256)
            log_total = logsum[:, 2 * g + h : 2 * g + h + 1]
            share = jnp.exp(jnp.where(mask, scores[:, columns], NEG) - log_total)
            term = jnp.sum(share * share_grads[:, columns], -1, keepdims=True)
            shares.append(share.astype(BF16))
            score_grads.append((share * (share_grads[:, columns] - term)).astype(BF16))
            sink_part = -jnp.sum(jnp.exp(sinks[2 * g + h] - log_total) * term, 0, keepdims=True)
            sink_grads = jnp.where(lane_row == 2 * g + h, sink_part, sink_grads)
        shares = jnp.concatenate(shares, 1)
        score_grads = jnp.concatenate(score_grads, 1)
        dq[:, part] = nn(score_grads, keys) * SCALE
        from_scores = tn(score_grads, q) * SCALE
        from_shares = tn(shares, grad_block)
        joined = jnp.where(
            lane,
            from_scores[:256] + pltpu.roll(from_scores[256:], 64, 1),
            pltpu.roll(from_shares[:256], 64, 1) + from_shares[256:],
        )
        halo[:, part] = joined[:128].astype(BF16)
        dkv[:, part] = joined[128:]
    grad_sink[...] = sink_grads


def attn_finish_kernel(
    dq, dkv, halo, cosq, sinq, cosk, sink_k, normed1, full, tok, gain1, mid_grad,
    grad_tokens, grad_w, grad_gain1, arrived, sems,
):
    here = coords()
    rank = here["xl"] * 4 + here["y"]
    after, before = (rank + 1) % 8, (rank + 7) % 8
    after_place = dict(here, xl=after // 4, y=after % 4)
    before_place = dict(here, xl=before // 4, y=before % 4)
    greet([after_place, before_place])
    copy = remote(halo, arrived, sems.at[0], sems.at[1], before_place)
    copy.start()
    normed = normed1[...]
    grad_q = dq[...]
    low = (grad_q * tiled(cosq[...]) - rope_partner(grad_q) * tiled(sinq[...])).astype(BF16)
    back = jnp.zeros((128, 1024), F32)
    for half in range(2):
        columns = slice(512 * half, 512 * half + 512)
        grad_w[0, half] = tn(normed, low[:, columns]).astype(BF16)
        back = back + nt(low[:, columns], full[0, half])
    copy.wait_recv()
    grad_kv = dkv[...] + arrived[...].astype(F32)
    low = (
        grad_kv * tiled(cosk[128:]) - rope_partner(grad_kv) * tiled(sink_k[128:])
    ).astype(BF16)
    for half in range(2):
        columns = slice(512 * half, 512 * half + 512)
        grad_w[1, half] = tn(normed, low[:, columns]).astype(BF16)
        back = back + nt(low[:, columns], full[1, half])
    norm_grad, gain_part = norm_back(tok[...].astype(F32), gain1[...], back)
    grad_gain1[...] = gain_part
    grad_tokens[...] = mid_grad[...] + norm_grad
    copy.wait_send()


def expert_kernel(
    rows, cots, gate, weights, bias_gate, bias_up, bias_down,
    out_rows, back_rows, dots, grads, grad_bias,
):
    w_gate = jnp.concatenate([weights[m % 4, m // 4, 0, 0] for m in range(8)], 1)
    w_up = jnp.concatenate([weights[m % 4, m // 4, 1, 0] for m in range(8)], 1)
    w_down = jnp.concatenate([weights[m % 4, m // 4, 2, 0] for m in range(8)], 1)
    x = rows[0].reshape(2 * CAP, 1024)
    tanh_gate = jnp.tanh((nt(x, w_gate) + bias_gate[0]) / CLAMP)
    tanh_up = jnp.tanh((nt(x, w_up) + bias_up[0]) / CLAMP)
    soft_gate, soft_up = CLAMP * tanh_gate, CLAMP * tanh_up
    sig = jax.nn.sigmoid(SLOPE * soft_gate)
    glu = soft_gate * sig
    hidden = (glu * (soft_up + 1.0)).astype(BF16)
    produced = nn(hidden, w_down) + bias_down[0]
    share = gate[0]
    cot = cots[0].reshape(2 * CAP, 1024).astype(F32)
    out_rows[0] = (share * produced).astype(BF16).reshape(2, CAP, 1024)
    products = produced * cot
    partial = products[:, :128]
    for m in range(1, 8):
        partial = partial + products[:, 128 * m : 128 * m + 128]
    dots[0] = partial.reshape(2, CAP, 128)
    scaled = share * cot
    grad_bias[0, :, 1024:] = jnp.sum(scaled, 0, keepdims=True)
    rows_grad = scaled.astype(BF16)
    hidden_grad = nt(rows_grad, w_down)
    gate_grad = (
        hidden_grad
        * (soft_up + 1.0)
        * (sig + SLOPE * glu * (1.0 - sig))
        * (1.0 - tanh_gate * tanh_gate)
    )
    up_grad = hidden_grad * glu * (1.0 - tanh_up * tanh_up)
    grad_bias[0, :, :512] = jnp.sum(gate_grad, 0, keepdims=True)
    grad_bias[0, :, 512:1024] = jnp.sum(up_grad, 0, keepdims=True)
    gate_low, up_low = gate_grad.astype(BF16), up_grad.astype(BF16)
    back_rows[0] = (nn(gate_low, w_gate) + nn(up_low, w_up)).astype(BF16).reshape(2, CAP, 1024)
    for w, (left, right) in enumerate(((gate_low, x), (up_low, x), (hidden, rows_grad))):
        grad = tn(left, right).astype(BF16)
        for m in range(8):
            grads[m % 4, m // 4, w, 0] = grad[:, 128 * m : 128 * m + 128]


def expert_block(rows, cots, gate, weights, bias_gate, bias_up, bias_down):
    def per(shape, *lead_dims):
        return pl.BlockSpec(lead_dims + shape, lambda e: (e,) + (0,) * len(shape))

    stacked = pl.BlockSpec((4, 2, 3, 1, 512, 128), lambda e: (0, 0, 0, e, 0, 0))
    return plain(
        expert_kernel,
        [
            ((2, 2, CAP, 1024), BF16),
            ((2, 2, CAP, 1024), BF16),
            ((2, 2, CAP, 128), F32),
            ((4, 2, 3, 2, 512, 128), BF16),
            ((2, 1, 2048), F32),
        ],
        [
            per((2, CAP, 1024), 1),
            per((2, CAP, 1024), 1),
            per((2 * CAP, 1), 1),
            stacked,
            per((1, 512), 1),
            per((1, 512), 1),
            per((1, 1024), 1),
        ],
        "experts",
        rows,
        cots,
        gate,
        weights,
        bias_gate,
        bias_up,
        bias_down,
        grid=(2,),
        out_specs=[
            per((2, CAP, 1024), 1),
            per((2, CAP, 1024), 1),
            per((2, CAP, 128), 1),
            stacked,
            per((1, 2048), 1),
        ],
    )


def local(
    tokens, gain_attention, w_query, key_value_weight, w_output, sinks, gain_expert,
    w_gate, w_up, w_down, bias_gate, bias_up, bias_down, gates, routes, segments, cotangent,
):
    core, rank = lax.axis_index("core"), lax.axis_index("tp")
    core_arg = core.reshape(1).astype(jnp.int32)
    gain1, gain2 = gain_attention[None], gain_expert[None]

    pairs = exchange(
        [(w, (2, 64, 2048), (64, 2048), whole, by_core) for w in (w_gate, w_up, w_down)],
        ("c",),
        0,
        "weights_pair",
    )
    (sorted_w,) = plain(
        sort_kernel, [((8, 3, 2, 64, 128), BF16)], [SM] + [VM] * 3, "weights_sort", core_arg, *pairs
    )
    (mine,) = exchange(
        [(sorted_w, (2, 3, 2, 8, 64, 128), (3, 2, 64, 128), by_rank, deal_to)],
        DEAL_AXES,
        1,
        "weights_deal",
    )
    weights = lax.all_gather(mine.reshape(2, 3, 2, 512, 128), "z", axis=0, tiled=False)

    shards = jnp.stack([w_query, key_value_weight, w_output.T])
    shards, mine = lax.optimization_barrier((shards, mine))
    full, cot_rows, prev = attn_gather(shards, cotangent, tokens, 2)
    full = full.reshape(3, 2, 1024, 512)

    length = routes.shape[0]
    labels = 4 * rank + jnp.arange(4, dtype=jnp.int32)
    named = routes[:, :, None] == labels
    hit = jnp.any(named, 1)
    share = jnp.sum(jnp.where(named, gates[:, :, None], 0.0), 1)
    token = jnp.arange(length, dtype=jnp.int32)
    below = (token[:, None] > token[None, :]).astype(BF16)
    earlier = jnp.dot(below, hit.astype(BF16), preferred_element_type=F32).astype(jnp.int32)
    place = jnp.where(hit, earlier, -1)
    place_t = place.T
    slots = jnp.arange(CAP, dtype=jnp.int32)
    hot = place_t[:, None, :] == slots[None, :, None]
    pick = hot.astype(BF16).reshape(4 * CAP, length)
    slot_share = jnp.sum(jnp.where(hot, share.T[:, None, :], 0.0), -1)

    segq = lax.dynamic_slice_in_dim(segments, rank * 128, 128, 0)
    seg_prev = lax.dynamic_slice_in_dim(segments, jnp.maximum(rank * 128 - 128, 0), 128, 0)
    seg_prev = jnp.where(rank == 0, -1, seg_prev)
    segk = jnp.concatenate([seg_prev, segq])[None]
    segq = segq[:, None]
    frequency = ROPE_BASE ** (-2.0 * jnp.arange(32, dtype=F32) / HEAD_DIM)
    position = (rank * 128 - 128 + jnp.arange(256, dtype=jnp.int32)).astype(F32)
    angles = position[:, None] * frequency[None, :]
    cosine, sine = jnp.cos(angles), jnp.sin(angles)
    one, zero = jnp.ones((256, 64), F32), jnp.zeros((256, 64), F32)
    cosk = jnp.concatenate([cosine, cosine, one], 1)
    sin_k = jnp.concatenate([-sine, sine, zero], 1)
    cosq = jnp.concatenate([cosine] * 4, 1)[128:]
    sinq = jnp.concatenate([-sine, sine] * 2, 1)[128:]
    mid, normed2, normed1, queries, keyvals, attended, logsum = plain(
        attn_forward_kernel,
        [
            ((128, 1024), F32),
            ((128, 1024), BF16),
            ((128, 1024), BF16),
            ((128, 1024), BF16),
            ((256, 1024), BF16),
            ((128, 1024), BF16),
            ((128, 128), F32),
        ],
        [SM] + [VM] * 11,
        "attn_forward",
        sinks, tokens, prev, full, gain1, gain2, segq, segk, cosq, sinq, cosk, sin_k,
    )

    sequence = gather_rows(normed2, 3, "rows_gather").reshape(1024, 1024)
    rows = jnp.dot(pick, sequence, preferred_element_type=F32).astype(BF16)
    cots = jnp.dot(pick, cot_rows.reshape(1024, 1024), preferred_element_type=F32).astype(BF16)
    padded = jnp.pad(slot_share, ((0, 0), (0, 384 - CAP))).reshape(2, 2, 384)
    slot_shape = (2, 2, CAP, 1024)
    part = (2, CAP, 1024)
    rows, cots, padded = exchange(
        [
            (rows.reshape(slot_shape), slot_shape, part, by_core, by_core_second),
            (cots.reshape(slot_shape), slot_shape, part, by_core, by_core_second),
            (padded, (2, 2, 384), (2, 384), by_core, by_core),
        ],
        ("c",),
        4,
        "slots_pair",
    )
    slot_gate = padded.transpose(1, 0, 2)[:, :, :CAP].reshape(2, 2 * CAP, 1)
    first = 4 * rank + 2 * core
    expert_bias = [
        lax.dynamic_slice_in_dim(b, first, 2, 0)[:, None] for b in (bias_gate, bias_up, bias_down)
    ]
    out_rows, back_rows, dots, grads, grad_bias = expert_block(
        rows, cots, slot_gate, weights, *expert_bias
    )
    grads = lax.psum_scatter(grads, "z", scatter_dimension=0, tiled=False)

    out_rows, back_rows, dots = exchange(
        [
            (out_rows, slot_shape, part, by_core_second, by_core),
            (back_rows, slot_shape, part, by_core_second, by_core),
            (dots, (2, 2, CAP, 128), (2, CAP, 128), by_core_second, by_core),
        ],
        ("c",),
        5,
        "slots_back",
    )
    unpick = (place[:, :, None] == slots).astype(BF16).reshape(length, 4 * CAP)
    out_tokens = jnp.dot(
        unpick, out_rows.reshape(4 * CAP, 1024), preferred_element_type=F32
    ).astype(BF16)
    back_tokens = jnp.dot(
        unpick, back_rows.reshape(4 * CAP, 1024), preferred_element_type=F32
    ).astype(BF16)
    slot_dots = jnp.sum(dots, -1).reshape(4, CAP)
    token_dots = jnp.sum(jnp.where(hot, slot_dots[:, :, None], 0.0), 1)
    token_dots = token_dots.reshape(4, 8, 128).transpose(1, 0, 2)
    part_shape = (2, 4, 128, 1024)
    moved_in, combined, dot_parts = reduce_rows(
        [back_tokens.reshape(part_shape), out_tokens.reshape(part_shape)], token_dots, 6, "tokens_back"
    )
    own_routes = lax.dynamic_slice_in_dim(routes, rank * 128, 128, 0)
    all_dots = dot_parts.reshape(32, 128).T
    chosen = own_routes[:, :, None] == jnp.arange(32, dtype=jnp.int32)
    grad_gates = jnp.sum(jnp.where(chosen, all_dots[:, None, :], 0.0), -1)

    layer_out, mid_grad, dq, halo, dkv, grad_wo, grad_gain2, grad_sink = plain(
        attn_backward_kernel,
        [
            ((128, 1024), F32),
            ((128, 1024), F32),
            ((128, 1024), F32),
            ((128, 1024), BF16),
            ((128, 1024), F32),
            ((2, 1024, 512), BF16),
            ((1, 1024), F32),
            ((1, 128), F32),
        ],
        [SM] + [VM] * 12,
        "attn_backward",
        sinks, moved_in, combined, mid, cotangent, gain2, full, queries, keyvals, attended,
        logsum, segq, segk,
    )
    grad_tokens, grad_w, grad_gain1 = pl.pallas_call(
        attn_finish_kernel,
        out_shape=[
            jax.ShapeDtypeStruct((128, 1024), F32),
            jax.ShapeDtypeStruct((2, 2, 1024, 512), BF16),
            jax.ShapeDtypeStruct((1, 1024), F32),
        ],
        in_specs=[VM] * 12,
        out_specs=[VM] * 3,
        scratch_shapes=[pltpu.VMEM((128, 1024), BF16), pltpu.SemaphoreType.DMA((2,))],
        compiler_params=comm_params(7),
        name="attn_finish",
    )(dq, dkv, halo, cosq, sinq, cosk, sin_k, normed1, full, tokens, gain1, mid_grad)

    sink_row = jnp.pad(grad_sink, ((0, 0), (0, 896)))
    small = jnp.concatenate(
        [grad_gain1, grad_gain2, sink_row, jnp.zeros_like(sink_row), grad_bias.reshape(4, 1024)]
    )
    split = (2, 2, 4, 2, 64, 512)
    grad_q, grad_kv, grad_o, sums, grad_bg, grad_bu, grad_bd, dealt = final_exchange(
        grad_w.reshape((2,) + split),
        grad_wo.reshape(split),
        small,
        grads.reshape(2, 3, 2, 8, 64, 128),
        8,
    )
    (unsorted,) = plain(
        unsort_kernel, [((2, 3, 64, 2048), BF16)], [SM, VM], "grads_unsort", core_arg, dealt
    )
    (halves,) = exchange(
        [(unsorted, (2, 3, 64, 2048), (3, 64, 2048), by_core, by_core)], ("c",), 9, "grads_pair"
    )
    grad_experts = halves[0].astype(F32) + halves[1].astype(F32)
    return (
        layer_out,
        grad_tokens,
        sums[0],
        grad_q,
        grad_kv,
        grad_o,
        sums[2, :16],
        sums[1],
        grad_experts[0],
        grad_experts[1],
        grad_experts[2],
        grad_bg,
        grad_bu,
        grad_bd,
        grad_gates,
    )


def solution(mesh):
    fine = Mesh(mesh.devices.reshape(2, 4, 2, 8), ("xh", "z", "core", "tp"))
    fsdp = ("xh", "z", "core")
    rows = P(("xh", "z", "core", "tp"), None)
    return jax.shard_map(
        local,
        mesh=fine,
        in_specs=(
            rows,
            P(),
            P(fsdp, "tp"),
            P(fsdp, "tp"),
            P("tp", fsdp),
            P(),
            P(),
            P(fsdp, "tp"),
            P(fsdp, "tp"),
            P(fsdp, "tp"),
            P(),
            P(),
            P(),
            P(fsdp, None),
            P(fsdp, None),
            P(fsdp),
            rows,
        ),
        out_specs=(
            rows,
            rows,
            P(),
            P(fsdp, "tp"),
            P(fsdp, "tp"),
            P("tp", fsdp),
            P(),
            P(),
            P(fsdp, "tp"),
            P(fsdp, "tp"),
            P(fsdp, "tp"),
            P(),
            P(),
            P(),
            rows,
        ),
        check_vma=False,
    )
```

```python
import itertools
import types

import jax
import jax.numpy as jnp
from jax import lax
from jax.experimental import pallas as pl
from jax.experimental.pallas import tpu as pltpu
from jax.sharding import Mesh
from jax.sharding import PartitionSpec as P

MESH = pl.DeviceIdType.MESH
HEAD_DIM = 64
WINDOW = 128
EPS = 1e-05
ROPE_BASE = 10000.0
CLAMP = 7.0
SLOPE = 1.702
SCALE = HEAD_DIM ** (-0.5)
NEG = -1e30
CAP = 272
F32 = jnp.float32
BF16 = jnp.bfloat16
ANY = pl.BlockSpec(memory_space=pl.ANY)
DMA = pltpu.SemaphoreType.DMA
VM = pl.BlockSpec(memory_space=pltpu.VMEM)
SM = pl.BlockSpec(memory_space=pltpu.SMEM)
VMEM_LIMIT = 58 * 1024 * 1024

SIZES = {"xh": 2, "z": 4, "c": 2, "xl": 2, "y": 4, "x": 4}


def coords():
    xh, z = lax.axis_index("xh"), lax.axis_index("z")
    c, t = lax.axis_index("core"), lax.axis_index("tp")
    xl, y = t // 4, t % 4
    return {"xh": xh, "z": z, "c": c, "xl": xl, "y": y, "x": 2 * xh + xl}


def moved(place, offset):
    out = dict(place)
    for axis, step in offset.items():
        out[axis] = (place[axis] + step) % SIZES[axis]
        if axis == "x":
            out["xh"], out["xl"] = out["x"] // 2, out["x"] % 2
    return out


def device(place):
    return (place["xh"], place["z"], place["c"], place["xl"] * 4 + place["y"])


def offsets(axes):
    ranges = [range(SIZES[a]) for a in axes]
    return [dict(zip(axes, o)) for o in itertools.product(*ranges) if any(o)]


def slot(place, axes):
    out = 0
    for a in axes:
        out = out * SIZES[a] + place[a]
    return out


def greet(peers):
    barrier = pltpu.get_barrier_semaphore()
    for peer in peers:
        pl.semaphore_signal(barrier, inc=1, device_id=device(peer), device_id_type=MESH)
    pl.semaphore_wait(barrier, len(peers))


def remote(src, dst, send, recv, peer):
    return pltpu.make_async_remote_copy(
        src_ref=src,
        dst_ref=dst,
        send_sem=send,
        recv_sem=recv,
        device_id=device(peer),
        device_id_type=MESH,
    )


def comm_params(ident):
    return pltpu.CompilerParams(
        collective_id=ident, has_side_effects=True, vmem_limit_bytes=VMEM_LIMIT
    )


def call(kernel, name, ident, ins, outs, scratch, **extra):
    names = list(ins) + list(outs) + list(scratch)

    def body(*refs):
        kernel(types.SimpleNamespace(**dict(zip(names, refs))))

    if ident is None:
        params = pltpu.CompilerParams(vmem_limit_bytes=VMEM_LIMIT)
    else:
        params = comm_params(ident)
    results = pl.pallas_call(
        body,
        out_shape=[jax.ShapeDtypeStruct(o[0], o[1]) for o in outs.values()],
        in_specs=[i[1] for i in ins.values()],
        out_specs=[o[2] for o in outs.values()],
        scratch_shapes=list(scratch.values()),
        compiler_params=params,
        name=name,
        **extra,
    )(*[i[0] for i in ins.values()])
    return types.SimpleNamespace(**dict(zip(outs, results)))


def given(spec, **arrays):
    return {name: (a, spec) for name, a in arrays.items()}


def f32(*shape):
    return pltpu.VMEM(shape, F32)


def bf16(*shape):
    return pltpu.VMEM(shape, BF16)


class Copies:
    def __init__(self, send, recv):
        self.send, self.recv, self.all = send, recv, []

    def go(self, src, dst, peer):
        k = len(self.all)
        copy = remote(src, dst, self.send.at[k], self.recv.at[k], peer)
        copy.start()
        self.all.append(copy)
        return copy

    def sent(self):
        for copy in self.all:
            copy.wait_send()


def arrived(copies):
    for copy in copies:
        copy.wait_recv()


def along(here, axis):
    return [moved(here, {axis: k}) for k in (1, 3, 2)]


def sequence_neighbours(here):
    rank = here["xl"] * 4 + here["y"]
    after, before = (rank + 1) % 8, (rank + 7) % 8
    return dict(here, xl=after // 4, y=after % 4), dict(here, xl=before // 4, y=before % 4)


def lanes_of(place):
    return pl.ds(pl.multiple_of(place["y"] * 128, 128), 128)


LEFT, RIGHT = pl.ds(0, 512), pl.ds(512, 512)


class RowGather:
    def __init__(self, here, src, out, send, recv):
        self.here, self.src, self.out = here, src, out
        self.net = Copies(send, recv)
        self.side, self.ups = moved(here, {"xl": 1}), along(here, "y")

    def first(self):
        xl, y = self.here["xl"], self.here["y"]
        go = self.net.go
        self.x = go(self.src.at[:, LEFT], self.out.at[xl, y, :, LEFT], self.side)
        self.y = [go(self.src.at[:, RIGHT], self.out.at[xl, y, :, RIGHT], p) for p in self.ups]

    def then(self):
        xl, y = self.here["xl"], self.here["y"]
        self.x.wait_recv()
        view = self.out.at[:, y, :, LEFT]
        self.last = [self.net.go(view, view, p) for p in self.ups]
        arrived(self.y)
        view = self.out.at[xl, :, :, RIGHT]
        self.last.append(self.net.go(view, view, self.side))

    def finish(self):
        arrived(self.last)
        self.net.sent()


class RowReduce:
    def __init__(self, here, parts, bufs, send, recv):
        self.here, self.parts = here, parts
        self.got_y, self.sum_y, self.got_x, self.sum_x, self.end_y, self.end_x = bufs
        self.net = Copies(send, recv)
        self.side, self.ups = moved(here, {"xl": 1}), along(here, "y")

    def right(self):
        self.x = self.net.go(self.parts.at[self.side["xl"], :, :, RIGHT], self.got_x, self.side)

    def left(self):
        self.y = [
            self.net.go(self.parts.at[:, p["y"], :, LEFT], self.got_y.at[k], p)
            for k, p in enumerate(self.ups)
        ]

    def then_right(self):
        self.x.wait_recv()
        mine = self.parts[self.here["xl"], :, :, RIGHT].astype(F32)
        self.sum_x[...] = (mine + self.got_x[...].astype(F32)).astype(BF16)
        self.last_x = [
            self.net.go(self.sum_x.at[p["y"]], self.end_x.at[k], p) for k, p in enumerate(self.ups)
        ]

    def then_left(self):
        arrived(self.y)
        total = self.parts[:, self.here["y"], :, LEFT].astype(F32)
        for k in range(3):
            total = total + self.got_y[k].astype(F32)
        self.sum_y[...] = total.astype(BF16)
        self.last_y = self.net.go(self.sum_y.at[self.side["xl"]], self.end_y, self.side)

    def result(self):
        self.last_y.wait_recv()
        left = self.sum_y[self.here["xl"]].astype(F32) + self.end_y[...].astype(F32)
        arrived(self.last_x)
        right = self.sum_x[self.here["y"]].astype(F32)
        for k in range(3):
            right = right + self.end_x[k].astype(F32)
        return jnp.concatenate([left, right], 1)


def row_reduce_scratch():
    return [
        bf16(3, 2, 128, 512),
        bf16(2, 128, 512),
        bf16(4, 128, 512),
        bf16(4, 128, 512),
        bf16(128, 512),
        bf16(3, 128, 512),
        DMA((8,)),
        DMA((8,)),
    ]


FULL = (2, 2, 4, 2, 64, 512)


def region(ref, place, held):
    xl = slice(None) if "x" in held else place["xl"]
    xh = slice(None) if "x" in held else place["xh"]
    z = slice(None) if "z" in held else place["z"]
    y = pl.ds(0, 512) if "y" in held else lanes_of(place)
    return ref.at[xl, xh, z, place["c"], :, y]


class Spread:
    def __init__(self, here, full, net):
        self.here, self.full, self.net = here, full, net

    def step(self, axis, held, src=None):
        view = region(self.full, self.here, held)
        src = view if src is None else src
        self.group = [self.net.go(src, view, p) for p in along(self.here, axis)]

    def swap(self):
        view = self.full.at[:, :, :, self.here["c"]]
        self.group = [self.net.go(view, view, moved(self.here, {"c": 1}))]

    def wait(self):
        arrived(self.group)


def matrix(ref, half):
    return ref[half].reshape(1024, 512)


def piece(axis, place, dims):
    index = []
    for d in dims:
        if d in ("xl", "xh"):
            index.append(place[d] if axis == "x" else slice(None))
        else:
            index.append(place["z"] if axis == "z" else slice(None))
    index.append(slice(None))
    index.append(lanes_of(place) if axis == "y" else slice(None))
    return tuple(index)


def reduce_shapes(order):
    dims, lanes = ["xl", "xh", "z"], 512
    shapes = [((2, 2, 4, 64, 512), tuple(dims))]
    for axis in order:
        if axis == "x":
            dims = [d for d in dims if d not in ("xl", "xh")]
        elif axis == "z":
            dims = [d for d in dims if d != "z"]
        else:
            lanes = 128
        shapes.append((tuple(SIZES[d] for d in dims) + (64, lanes), tuple(dims)))
    return shapes


class Reduce:
    def __init__(self, here, parts, order, bufs, send, recv):
        self.here, self.parts, self.order = here, parts, order
        self.got0, self.sums, self.gots = bufs[0], bufs[1:4], bufs[4:7]
        self.net = Copies(send, recv)
        self.other = moved(here, {"c": 1})
        self.shapes = reduce_shapes(order)

    def swap(self):
        self.group = [self.net.go(self.parts.at[:, :, :, self.other["c"]], self.got0, self.other)]

    def go(self, s):
        axis, dims = self.order[s], self.shapes[s][1]
        self.group = [
            self.net.go(self.sums[s].at[piece(axis, p, dims)], self.gots[s].at[k], p)
            for k, p in enumerate(along(self.here, axis))
        ]

    def first(self):
        arrived(self.group)
        mine = self.parts[:, :, :, self.here["c"]].astype(F32)
        self.sums[0][...] = (mine + self.got0[...].astype(F32)).astype(BF16)
        self.go(0)

    def step(self, s):
        arrived(self.group)
        total = self.sums[s][piece(self.order[s], self.here, self.shapes[s][1])].astype(F32)
        for k in range(3):
            total = total + self.gots[s][k].astype(F32)
        if s < 2:
            self.sums[s + 1][...] = total.astype(BF16)
            self.go(s + 1)
        return total


def reduce_scratch(order):
    shapes = reduce_shapes(order)
    bufs = [bf16(*shapes[0][0])]
    bufs += [bf16(*shapes[s][0]) for s in range(3)]
    bufs += [bf16(3, *shapes[s + 1][0]) for s in range(3)]
    return bufs + [DMA((10,)), DMA((10,))]


def nn(a, b):
    return lax.dot_general(a, b, (((1,), (0,)), ((), ())), preferred_element_type=F32)


def nt(a, b):
    return lax.dot_general(a, b, (((1,), (1,)), ((), ())), preferred_element_type=F32)


def tn(a, b):
    return lax.dot_general(a, b, (((0,), (0,)), ((), ())), preferred_element_type=F32)


def one_hot_columns(start, core):
    row = lax.broadcasted_iota(jnp.int32, (1024, 1024), 0)
    column = lax.broadcasted_iota(jnp.int32, (1024, 1024), 1) + start
    expert = 4 * (row // 128) + 2 * core + (row // 64) % 2
    return (column == (row % 64) * 32 + expert).astype(F32).astype(BF16)


def rope_partner(values):
    lanes = values.shape[1]
    lane = lax.broadcasted_iota(jnp.int32, values.shape, 1)
    return jnp.where(
        lane % 64 < 32, pltpu.roll(values, lanes - 32, 1), pltpu.roll(values, 32, 1)
    )


def tiled(table):
    return jnp.concatenate([table] * 8, axis=1)


def head_pair(block):
    lane = lax.broadcasted_iota(jnp.int32, block.shape, 1) < 64
    wide = block.astype(F32)
    swapped = pltpu.roll(wide, 64, 1)
    zero = jnp.zeros_like(wide)
    keys = jnp.concatenate([jnp.where(lane, wide, zero), jnp.where(lane, zero, swapped)], 0)
    values = jnp.concatenate([jnp.where(lane, swapped, zero), jnp.where(lane, zero, wide)], 0)
    return keys.astype(BF16), values.astype(BF16)


def window_mask(segq, segk):
    row = lax.broadcasted_iota(jnp.int32, (128, 256), 0)
    column = lax.broadcasted_iota(jnp.int32, (128, 256), 1)
    distance = 128 + row - column
    return (segq == segk) & (distance >= 0) & (distance < WINDOW)


def rope_at(start, rows, freq):
    row = lax.broadcasted_iota(jnp.int32, (rows, 128), 0)
    lane = lax.broadcasted_iota(jnp.int32, (rows, 128), 1)
    angles = (row + start).astype(F32) * freq
    cosine, sine = jnp.cos(angles), jnp.sin(angles)
    return cosine, jnp.where(lane % 64 < 32, -sine, sine), lane < 64


def rope_queries(rank, freq):
    cosine, sine, _ = rope_at(128 * rank, 128, freq)
    return tiled(cosine), tiled(sine)


def rope_keyvals(start, rows, freq):
    cosine, sine, keys = rope_at(start, rows, freq)
    return tiled(jnp.where(keys, cosine, 1.0)), tiled(jnp.where(keys, sine, 0.0))


def mask_at(segments, rank):
    own = segments[:, pl.ds(pl.multiple_of(128 * rank, 128), 128)]
    prev = segments[:, pl.ds(pl.multiple_of(128 * ((rank + 7) % 8), 128), 128)]
    prev = jnp.where(rank == 0, -1, prev)
    row = lax.broadcasted_iota(jnp.int32, (128, 128), 0)
    column = lax.broadcasted_iota(jnp.int32, (128, 128), 1)
    segq = jnp.sum(jnp.where(row == column, own.astype(F32), 0.0), 1, keepdims=True)
    return window_mask(segq, jnp.concatenate([prev, own], 1).astype(F32))


def slot_tables(r, rank):
    row = lax.broadcasted_iota(jnp.int32, (1024, 1024), 0)
    column = lax.broadcasted_iota(jnp.int32, (1024, 1024), 1)
    before = (row < column).astype(F32).astype(BF16)
    routes_t, gates_t = r.routes_t[...], r.gates_t[...]
    hits, shares = [], []
    for el in range(4):
        named = routes_t == 4 * rank + el
        hits.append(jnp.sum(named.astype(F32), 0, keepdims=True))
        shares.append(jnp.sum(jnp.where(named, gates_t, 0.0), 0, keepdims=True))
    earlier = nn(jnp.concatenate(hits + [jnp.zeros((12, 1024), F32)], 0).astype(BF16), before)
    places = [jnp.where(hits[el] > 0, earlier[el : el + 1], -1.0) for el in range(4)]
    columns = jnp.concatenate(places + [jnp.zeros((124, 1024), F32)], 0).T
    slot = lax.broadcasted_iota(jnp.int32, (CAP, 1024), 0).astype(F32)
    wide = lax.broadcasted_iota(jnp.int32, (1024, 2 * CAP), 1).astype(F32)
    for c in range(2):
        for e in range(2):
            el = 2 * c + e
            r.place_t[c, e : e + 1] = places[el]
            hot = slot == places[el]
            r.pick[c, CAP * e : CAP * e + CAP] = hot.astype(F32).astype(BF16)
            share = jnp.sum(jnp.where(hot, shares[el], 0.0), 1, keepdims=True)
            r.slot_gate[c, e] = jnp.broadcast_to(share, (CAP, 128))
        low = (wide == columns[:, 2 * c : 2 * c + 1]) & (wide < CAP)
        high = (wide - CAP == columns[:, 2 * c + 1 : 2 * c + 2]) & (wide >= CAP)
        r.unpick_v[c] = (low | high).astype(F32).astype(BF16)


DEAL_AXES = ("xh", "xl", "y")


def front_kernel(r):
    here = coords()
    c, xh, z, xl, y = (here[a] for a in ("c", "xh", "z", "xl", "y"))
    rank = xl * 4 + y
    other = moved(here, {"c": 1})
    after, before = sequence_neighbours(here)
    dealt = [moved(here, o) for o in offsets(DEAL_AXES)]
    up, down = moved(here, {"z": 1}), moved(here, {"z": 3})
    parts = (r.w_gate, r.w_up, r.w_down)
    fulls = (r.full0_v, r.full1_v, r.full2_v)
    for w, ref in enumerate(parts):
        r.pairs[w, c] = ref[...]
    for p, ref in enumerate((r.w_query, r.w_keyval, r.w_output_t)):
        r.shards[p] = ref[...]
    own = [
        pltpu.make_async_copy(r.shards.at[p], region(fulls[p], here, ""), r.own.at[p])
        for p in range(3)
    ]
    for copy in own:
        copy.start()
    greet([other, after, before] + [p for a in "xyz" for p in along(here, a)] + dealt)
    net = Copies(r.send, r.recv)
    swaps = [net.go(ref, r.pairs.at[w, c], other) for w, ref in enumerate(parts)]
    halo = net.go(r.tok, r.prev, after)
    q_full, kv_full, o_full = (Spread(here, full, net) for full in fulls)
    kv_full.step("y", "", r.shards.at[1])
    q_full.step("z", "", r.shards.at[0])
    o_full.step("z", "", r.shards.at[2])
    cots = RowGather(here, r.cot, r.cot_all, r.cot_send, r.cot_recv)
    cots.first()
    r.cot_all[xl, y] = r.cot[...]
    first = 4 * rank + 2 * c
    for e in range(2):
        r.bias[e, :, :512] = r.bias_gate[pl.ds(first + e, 1)]
        r.bias[e, :, 512:1024] = r.bias_up[pl.ds(first + e, 1)]
        r.bias[e, :, 1024:] = r.bias_down[pl.ds(first + e, 1)]
    hot = jnp.concatenate([one_hot_columns(0, c), one_hot_columns(1024, c)], 1)
    for copy in own:
        copy.wait()
    kv_full.wait()
    kv_full.step("x", "y")
    deals, keeps = [], []
    for w in range(3):
        arrived([swaps[w]])
        rows = r.pairs[w].reshape(128, 2048)
        r.sorted[w] = nt(hot, rows).astype(BF16).reshape(8, 2, 64, 128)
        mine = r.weights.at[w, z, xh, :, rank]
        keeps.append(pltpu.make_async_copy(r.sorted.at[w, rank], mine, r.keep.at[w]))
        keeps[w].start()
        deals.append(
            [net.go(r.sorted.at[w, p["xl"] * 4 + p["y"]], mine, p) for p in dealt]
        )
        if w == 0:
            q_full.wait()
            q_full.step("y", "z")
            o_full.wait()
            o_full.step("x", "z")
    kv_full.wait()
    kv_full.step("z", "yx")
    q_full.wait()
    q_full.step("x", "zy")
    o_full.wait()
    o_full.step("y", "zx")
    cots.then()
    slot_tables(r, rank)
    stores = [pltpu.make_async_copy(r.unpick_v, r.unpick, r.store.at[0])]
    stores[0].start()
    gates = net.go(r.slot_gate.at[other["c"]], r.gate_rows.at[c], other)
    r.gate_rows[c] = r.slot_gate[c]
    ring = []
    for w in range(3):
        arrived(deals[w])
        keeps[w].wait()
        view = r.weights.at[w, z]
        ring.append([net.go(view, view, up), net.go(view, view, down)])
    last_ring = []

    def pass_on(w):
        arrived(ring[w])
        view = r.weights.at[w, down["z"], 0]
        last_ring.append(net.go(view, view, up))
        view = r.weights.at[w, up["z"], 1]
        last_ring.append(net.go(view, view, down))

    def save(k, full, result):
        stores.append(pltpu.make_async_copy(full, result, r.store.at[k]))
        stores[k].start()

    kv_full.wait()
    kv_full.swap()
    halo.wait_recv()
    tok = r.tok[...].astype(F32)
    both = jnp.concatenate([r.prev[...].astype(F32), tok], 0)
    scale = lax.rsqrt(jnp.mean(both * both, -1, keepdims=True) + EPS)
    normed = (both * scale * r.gain1[...]).astype(BF16)
    normed_own = normed[128:]
    r.normed1[...] = normed_own
    q_full.wait()
    q_full.swap()
    o_full.wait()
    o_full.swap()
    kv_full.wait()
    save(1, r.full1_v, r.full1)
    kv = jnp.concatenate([nn(normed, matrix(r.full1_v, 0)), nn(normed, matrix(r.full1_v, 1))], 1)
    cosine, sine = rope_keyvals(128 * rank - 128, 256, r.freq[...])
    kv = (kv * cosine + rope_partner(kv) * sine).astype(BF16)
    r.keyvals[...] = kv
    mask = mask_at(r.segments, rank)
    lane = lax.broadcasted_iota(jnp.int32, (128, 128), 1)
    q_full.wait()
    save(2, r.full0_v, r.full0)
    q = jnp.concatenate(
        [nn(normed_own, matrix(r.full0_v, 0)), nn(normed_own, matrix(r.full0_v, 1))], 1
    )
    cosine, sine = rope_queries(rank, r.freq[...])
    q = (q * cosine + rope_partner(q) * sine).astype(BF16)
    r.queries[...] = q
    pass_on(0)
    sums = jnp.zeros((128, 128), F32)
    for g in range(8):
        part = slice(128 * g, 128 * g + 128)
        keys, values = head_pair(kv[:, part])
        scores = nt(q[:, part], keys) * SCALE
        shares = []
        for h in range(2):
            masked = jnp.where(mask, scores[:, 256 * h : 256 * h + 256], NEG)
            sink = r.sinks[2 * g + h]
            peak = jnp.maximum(jnp.max(masked, -1, keepdims=True), sink)
            total = jnp.exp(sink - peak) + jnp.sum(jnp.exp(masked - peak), -1, keepdims=True)
            log_total = peak + jnp.log(total)
            shares.append(jnp.exp(masked - log_total).astype(BF16))
            sums = jnp.where(lane == 2 * g + h, log_total, sums)
        r.attended[:, part] = nn(jnp.concatenate(shares, 1), values).astype(BF16)
    r.logsum[...] = sums
    o_full.wait()
    save(3, r.full2_v, r.full2)
    out = (
        tok
        + nt(r.attended[:, :512], matrix(r.full2_v, 0))
        + nt(r.attended[:, 512:], matrix(r.full2_v, 1))
    )
    r.mid[...] = out
    scale = lax.rsqrt(jnp.mean(out * out, -1, keepdims=True) + EPS)
    r.normed2[...] = (out * scale * r.gain2[...]).astype(BF16)

    rows = RowGather(here, r.normed2, r.row_all, r.row_send, r.row_recv)
    rows.first()
    r.row_all[xl, y] = r.normed2[...]
    pass_on(1)
    cots.finish()

    def to_slots(gathered, outgoing, result):
        tokens = gathered[...].reshape(1024, 1024)
        outgoing[...] = nn(r.pick[other["c"]], tokens).astype(BF16).reshape(2, CAP, 1024)
        copy = net.go(outgoing, result.at[c], other)
        result[c] = nn(r.pick[c], tokens).astype(BF16).reshape(2, CAP, 1024)
        return copy

    rows.then()
    cot_copy = to_slots(r.cot_all, r.cot_out, r.cot_rows)
    pass_on(2)
    rows.finish()
    row_copy = to_slots(r.row_all, r.row_out, r.rows)
    arrived([gates, cot_copy, row_copy])
    arrived(last_ring)
    for copy in stores:
        copy.wait()
    net.sent()


def expert_kernel(r):
    turn = pl.program_id(0)
    here = coords()
    xl, y = here["xl"], here["y"]
    side, ups = moved(here, {"xl": 1}), along(here, "y")
    own = pltpu.make_async_copy(r.normed1, r.normed_all.at[xl, y], r.own)
    src, out = r.normed1, r.normed_all

    def copy(k, src_view, dst_view, peer):
        return remote(src_view, dst_view, r.send.at[k], r.recv.at[k], peer)

    start = [copy(0, src.at[:, LEFT], out.at[xl, y, :, LEFT], side)]
    start += [
        copy(1 + k, src.at[:, RIGHT], out.at[xl, y, :, RIGHT], p) for k, p in enumerate(ups)
    ]
    column, line = out.at[:, y, :, LEFT], out.at[xl, :, :, RIGHT]
    then = [copy(4 + k, column, column, p) for k, p in enumerate(ups)]
    then.append(copy(7, line, line, side))

    @pl.when(turn == 0)
    def _():
        own.start()
        greet([side] + ups)
        for item in start:
            item.start()

    @pl.when(turn == 1)
    def _():
        own.wait()
        for item in start:
            item.wait()
        for item in then:
            item.start()

    def stacked(w):
        return jnp.concatenate(
            [r.weights[w, m % 4, m // 4, 0].reshape(512, 128) for m in range(8)], 1
        )

    w_gate, w_up, w_down = stacked(0), stacked(1), stacked(2)
    bias = r.bias[0]
    x = r.rows[:, 0].reshape(2 * CAP, 1024)
    tanh_gate = jnp.tanh((nt(x, w_gate) + bias[:, :512]) / CLAMP)
    tanh_up = jnp.tanh((nt(x, w_up) + bias[:, 512:1024]) / CLAMP)
    soft_gate, soft_up = CLAMP * tanh_gate, CLAMP * tanh_up
    sig = jax.nn.sigmoid(SLOPE * soft_gate)
    glu = soft_gate * sig
    hidden = (glu * (soft_up + 1.0)).astype(BF16)
    produced = nn(hidden, w_down) + bias[:, 1024:]
    share = r.gate_rows[:, 0].reshape(2 * CAP, 128)[:, :1]
    cot = r.cot_rows[:, 0].reshape(2 * CAP, 1024).astype(F32)
    r.out_rows[:, 0] = (share * produced).astype(BF16).reshape(2, CAP, 1024)
    products = produced * cot
    partial = products[:, :128]
    for m in range(1, 8):
        partial = partial + products[:, 128 * m : 128 * m + 128]
    r.dots[:, 0] = partial.reshape(2, CAP, 128)
    scaled = share * cot
    r.grad_bias[0, :, 1024:] = jnp.sum(scaled, 0, keepdims=True)
    rows_grad = scaled.astype(BF16)
    hidden_grad = nt(rows_grad, w_down)
    gate_grad = (
        hidden_grad
        * (soft_up + 1.0)
        * (sig + SLOPE * glu * (1.0 - sig))
        * (1.0 - tanh_gate * tanh_gate)
    )
    up_grad = hidden_grad * glu * (1.0 - tanh_up * tanh_up)
    r.grad_bias[0, :, :512] = jnp.sum(gate_grad, 0, keepdims=True)
    r.grad_bias[0, :, 512:1024] = jnp.sum(up_grad, 0, keepdims=True)
    gate_low, up_low = gate_grad.astype(BF16), up_grad.astype(BF16)
    back = (nn(gate_low, w_gate) + nn(up_low, w_up)).astype(BF16)
    r.back_rows[:, 0] = back.reshape(2, CAP, 1024)
    for w, (left, right) in enumerate(((gate_low, x), (up_low, x), (hidden, rows_grad))):
        grad = tn(left, right).astype(BF16)
        for m in range(8):
            r.grads[m % 4, m // 4, w, 0] = grad[:, 128 * m : 128 * m + 128]

    @pl.when(turn == 1)
    def _():
        for item in then:
            item.wait()


def expert_block(front):
    def at(dim, *shape):
        return pl.BlockSpec(
            shape[:dim] + (1,) + shape[dim:],
            lambda e: (0,) * dim + (e,) + (0,) * (len(shape) - dim),
        )

    per_row, per_slot = at(1, 2, CAP, 1024), at(1, 2, CAP, 128)
    stacked, vector = at(3, 4, 2, 3, 512, 128), at(0, 1, 2048)
    return call(
        expert_kernel,
        "experts",
        1,
        dict(
            rows=(front.rows, per_row),
            cot_rows=(front.cot_rows, per_row),
            gate_rows=(front.gate_rows, per_slot),
            weights=(front.weights, at(3, 3, 4, 2, 8, 64, 128)),
            bias=(front.bias, vector),
            normed1=(front.normed1, VM),
        ),
        dict(
            out_rows=((2, 2, CAP, 1024), BF16, per_row),
            back_rows=((2, 2, CAP, 1024), BF16, per_row),
            dots=((2, 2, CAP, 128), F32, per_slot),
            grads=((4, 2, 3, 2, 512, 128), BF16, stacked),
            grad_bias=((2, 1, 2048), F32, vector),
            normed_all=((2, 4, 128, 1024), BF16, ANY),
        ),
        dict(send=DMA((8,)), recv=DMA((8,)), own=DMA),
        grid=(2,),
    )


def norm_back(values, gain, grad):
    scale = lax.rsqrt(jnp.mean(values * values, -1, keepdims=True) + EPS)
    normed = values * scale
    weighted = gain * grad
    back = scale * (weighted - normed * jnp.mean(weighted * normed, -1, keepdims=True))
    return back, jnp.sum(grad * normed, 0, keepdims=True)


WO_ORDER = ("x", "y", "z")


class ZSum:
    def __init__(self, r, here, net):
        self.r, self.net, self.z = r, net, here["z"]
        self.up, self.down = moved(here, {"z": 1}), moved(here, {"z": 3})
        far = (self.z + 2) % 4
        up, down = self.up["z"], self.down["z"]
        self.far, self.solo, self.both = [], [], [None] * 3
        for w in range(3):
            self.far.append(
                [
                    net.go(r.grads.at[far, 0, w], r.z_far.at[0, w], self.up),
                    net.go(r.grads.at[far, 1, w], r.z_far.at[1, w], self.down),
                ]
            )
        for w in range(3):
            self.solo.append(
                [
                    net.go(r.grads.at[up, 1, w], r.z_solo.at[1, w], self.up),
                    net.go(r.grads.at[down, 0, w], r.z_solo.at[0, w], self.down),
                ]
            )

    def add(self, w):
        r = self.r
        arrived(self.far[w])
        for half in range(2):
            r.z_send[half, w] = (
                r.z_near[half, w].astype(F32) + r.z_far[half, w].astype(F32)
            ).astype(BF16)
        self.both[w] = [
            self.net.go(r.z_send.at[0, w], r.z_got.at[0, w], self.up),
            self.net.go(r.z_send.at[1, w], r.z_got.at[1, w], self.down),
        ]

    def total(self, w, half):
        r = self.r
        return (
            r.z_own[half, w].astype(F32)
            + r.z_got[half, w].astype(F32)
            + r.z_solo[half, w].astype(F32)
        ).astype(BF16)

    def wait(self, w):
        arrived(self.solo[w] + self.both[w])


def back_kernel(r):
    here = coords()
    c, xh, z, xl, y = (here[a] for a in ("c", "xh", "z", "xl", "y"))
    rank = xl * 4 + y
    other = moved(here, {"c": 1})
    after, before = sequence_neighbours(here)
    everyone = [moved(here, o) for o in offsets(("xl", "y"))]
    dealt = [moved(here, o) for o in offsets(DEAL_AXES)]
    owners = [moved(here, o) for o in offsets(("xh", "z", "c"))]
    planes = [moved(here, o) for o in offsets(("xh", "z"))]
    places = [moved(here, o) for o in offsets(("c", "xl", "y"))]
    loads = []

    def load(src, dst):
        copy = pltpu.make_async_copy(src, dst, r.load.at[len(loads)])
        copy.start()
        loads.append(copy)
        return copy

    get_unpick = load(r.unpick, r.unpick_v)
    get_back = load(r.back_rows.at[c], r.back_own)
    get_dots = load(r.dots.at[c], r.dot_own)
    get_near = [
        load(r.grads.at[(z + 1) % 4, 0], r.z_near.at[0]),
        load(r.grads.at[(z + 3) % 4, 1], r.z_near.at[1]),
    ]
    get_full2 = load(r.full2, r.full2_v)
    get_z = load(r.grads.at[z], r.z_own)
    get_full0 = load(r.full0, r.full0_v)
    get_full1 = load(r.full1, r.full1_v)
    get_normed = load(r.normed_all, r.normed_v)
    greet(
        [other, after, before]
        + [p for a in "xyz" for p in along(here, a)]
        + everyone + dealt + owners + planes + places
    )
    net = Copies(r.send, r.recv)
    back_swap = net.go(r.back_rows.at[other["c"]], r.back_got, other)
    zsum = ZSum(r, here, net)

    def to_tokens(own, got, parts, columns):
        mine = nn(r.unpick_v[c], own[:, :, columns].reshape(2 * CAP, 512))
        theirs = nn(r.unpick_v[other["c"]], got[:, :, columns].reshape(2 * CAP, 512))
        parts[:, :, :, columns] = (mine + theirs).astype(BF16).reshape(2, 4, 128, 512)

    back = RowReduce(here, r.back_parts, r.back_bufs[:6], *r.back_bufs[6:])
    out = RowReduce(here, r.out_parts, r.out_bufs[:6], *r.out_bufs[6:])
    get_unpick.wait()
    get_back.wait()
    back_swap.wait_recv()
    dot_swap = net.go(r.dots.at[other["c"]], r.dot_got, other)
    out_swap = net.go(r.out_rows.at[other["c"]], r.out_got, other)
    to_tokens(r.back_own, r.back_got, r.back_parts, RIGHT)
    back.right()
    to_tokens(r.back_own, r.back_got, r.back_parts, LEFT)
    back.left()
    get_out = load(r.out_rows.at[c], r.back_own)

    get_dots.wait()
    dot_swap.wait_recv()
    slot = lax.broadcasted_iota(jnp.int32, (CAP, 1024), 0).astype(F32)
    for source, core in ((r.dot_own, c), (r.dot_got, other["c"])):
        for e in range(2):
            totals = jnp.sum(source[e], 1, keepdims=True)
            hot = slot == r.place_t[core, e : e + 1]
            line = jnp.sum(jnp.where(hot, totals, 0.0), 0, keepdims=True)
            for j in range(8):
                r.token_dots[j, core, e : e + 1] = line[:, 128 * j : 128 * j + 128]
    r.dots_all[rank] = r.token_dots[rank]
    dot_copies = [
        net.go(r.token_dots.at[p["xl"] * 4 + p["y"]], r.dots_all.at[rank], p) for p in everyone
    ]
    for copy in get_near:
        copy.wait()
    zsum.add(0)
    back.then_right()
    back.then_left()
    zsum.add(1)
    zsum.add(2)
    get_out.wait()
    out_swap.wait_recv()
    to_tokens(r.back_own, r.out_got, r.out_parts, RIGHT)
    to_tokens(r.back_own, r.out_got, r.out_parts, LEFT)
    moved_in = back.result()
    out.right()
    out.left()

    step, gain_part = norm_back(r.mid[...], r.gain2[...], moved_in)
    r.small[1:2] = gain_part
    mid_grad = r.cot[...].astype(F32) + step
    low = mid_grad.astype(BF16)
    for half in range(2):
        columns = slice(512 * half, 512 * half + 512)
        r.grad_wo[half] = tn(low, r.attended[:, columns]).astype(BF16).reshape(FULL[1:])
    wo = Reduce(here, r.grad_wo, WO_ORDER, r.wo_bufs[:7], *r.wo_bufs[7:])
    wo.swap()
    get_full2.wait()
    out_grad = jnp.concatenate([nn(low, matrix(r.full2_v, 0)), nn(low, matrix(r.full2_v, 1))], 1)
    out_grad = out_grad.astype(BF16)
    mask = mask_at(r.segments, rank)
    lane_row = lax.broadcasted_iota(jnp.int32, (1, 128), 1)
    lane = lax.broadcasted_iota(jnp.int32, (256, 128), 1) < 64
    sink_grads = jnp.zeros((1, 128), F32)
    for g in range(8):
        part = slice(128 * g, 128 * g + 128)
        keys, values = head_pair(r.keyvals[:, part])
        q = r.queries[:, part]
        grad_block = out_grad[:, part]
        scores = nt(q, keys) * SCALE
        share_grads = nt(grad_block, values)
        shares, score_grads = [], []
        for h in range(2):
            columns = slice(256 * h, 256 * h + 256)
            log_total = r.logsum[:, 2 * g + h : 2 * g + h + 1]
            share = jnp.exp(jnp.where(mask, scores[:, columns], NEG) - log_total)
            term = jnp.sum(share * share_grads[:, columns], -1, keepdims=True)
            shares.append(share.astype(BF16))
            score_grads.append((share * (share_grads[:, columns] - term)).astype(BF16))
            sink_part = -jnp.sum(jnp.exp(r.sinks[2 * g + h] - log_total) * term, 0, keepdims=True)
            sink_grads = jnp.where(lane_row == 2 * g + h, sink_part, sink_grads)
        shares = jnp.concatenate(shares, 1)
        score_grads = jnp.concatenate(score_grads, 1)
        r.dq[:, part] = nn(score_grads, keys) * SCALE
        from_scores = tn(score_grads, q) * SCALE
        from_shares = tn(shares, grad_block)
        joined = jnp.where(
            lane,
            from_scores[:256] + pltpu.roll(from_scores[256:], 64, 1),
            pltpu.roll(from_shares[:256], 64, 1) + from_shares[256:],
        )
        r.halo[:, part] = joined[:128].astype(BF16)
        r.dkv[:, part] = joined[128:]
        if g == 1:
            wo.first()
    halo = net.go(r.halo, r.halo_got, before)
    out.then_right()
    out.then_left()

    def to_columns(low, k):
        r.low[k] = low
        r.low_all[k, rank] = r.low[k, :, lanes_at(rank)]
        return [net.go(r.low.at[k, :, lanes_at(p["xl"] * 4 + p["y"])], r.low_all.at[k, rank], p) for p in everyone]

    grad_q = r.dq[...]
    cosine, sine = rope_queries(rank, r.freq[...])
    low = (grad_q * cosine - rope_partner(grad_q) * sine).astype(BF16)
    q_copies = to_columns(low, 0)
    get_full0.wait()
    first_back = nt(low[:, :512], matrix(r.full0_v, 0)) + nt(low[:, 512:], matrix(r.full0_v, 1))

    get_z.wait()
    deals = []

    def deal(w):
        zsum.wait(w)
        for half in range(2):
            r.deal_out[w, half] = zsum.total(w, half).reshape(2, 8, 64, 128)
        r.deal_got[w, xh, rank] = r.deal_out[w, xh, :, rank]
        deals.append(
            [
                net.go(
                    r.deal_out.at[w, p["xh"], :, p["xl"] * 4 + p["y"]], r.deal_got.at[w, xh, rank], p
                )
                for p in dealt
            ]
        )

    deal(0)
    halo.wait_recv()
    grad_kv = r.dkv[...] + r.halo_got[...].astype(F32)
    cosine, sine = rope_keyvals(128 * rank, 128, r.freq[...])
    low = (grad_kv * cosine - rope_partner(grad_kv) * sine).astype(BF16)
    kv_copies = to_columns(low, 1)
    deal(1)
    get_full1.wait()
    first_back = (
        first_back + nt(low[:, :512], matrix(r.full1_v, 0)) + nt(low[:, 512:], matrix(r.full1_v, 1))
    )
    norm_grad, gain_part = norm_back(r.tok[...].astype(F32), r.gain1[...], first_back)
    r.grad_tokens[...] = mid_grad + norm_grad
    r.small[0:1] = gain_part
    r.small[2:3] = jnp.concatenate([sink_grads, jnp.zeros((1, 896), F32)], 1)
    r.small[3:4] = jnp.zeros((1, 1024), F32)
    for e in range(2):
        r.small[4 + 2 * e : 5 + 2 * e] = r.grad_bias[e, :, :1024]
        r.small[5 + 2 * e : 6 + 2 * e] = r.grad_bias[e, :, 1024:]
    small = [net.go(r.small, r.small_got.at[k], p) for k, p in enumerate(planes)]
    deal(2)
    wo.step(0)

    get_normed.wait()
    normed = r.normed_v[...].reshape(1024, 1024)
    mine = (xh * 4 + z) * 2 + c
    sums = []
    for k, copies in enumerate((q_copies, kv_copies)):
        arrived(copies)
        product = tn(normed, r.low_all[k].reshape(1024, 128))
        r.grad_w[k] = product.astype(BF16).reshape(16, 64, 128)
        r.grad_w_got[k, mine] = r.grad_w[k, mine]
        sums.append(
            [
                net.go(
                    r.grad_w.at[k, (p["xh"] * 4 + p["z"]) * 2 + p["c"]], r.grad_w_got.at[k, mine], p
                )
                for p in owners
            ]
        )
    wo.step(1)
    arrived(small)
    total = r.small[...]
    for k in range(7):
        total = total + r.small_got[k]
    spot = r.small_all.at[c * 8 + rank]
    spot[...] = total
    small = [net.go(spot, spot, p) for p in places]
    unsorted, rows = [], []
    for half in range(2):
        hot = one_hot_columns(1024 * half, c)
        for w in range(3):
            if half == 0:
                arrived(deals[w])
                summed = r.deal_got[w, 0].astype(F32) + r.deal_got[w, 1].astype(F32)
                rows.append(summed.astype(BF16).reshape(1024, 128))
            wide = tn(rows[w], hot).astype(BF16)
            r.unsorted[w, :, :, 1024 * half : 1024 * half + 1024] = wide.reshape(2, 64, 1024)
            if half == 1:
                unsorted.append(net.go(r.unsorted.at[w, other["c"]], r.unsorted_got.at[w], other))
    r.layer_out[...] = r.mid[...] + out.result()
    arrived(dot_copies)
    own_routes = r.routes_t[:, lanes_at(rank)]
    chosen = jnp.zeros((8, 128), F32)
    for j in range(8):
        for core in range(2):
            for e in range(2):
                line = r.dots_all[j, core, e : e + 1]
                chosen = jnp.where(own_routes == 4 * j + 2 * core + e, line, chosen)
    r.grad_gates[...] = chosen
    for k, copies in enumerate(sums):
        arrived(copies)
        total = r.grad_w_got[k, 0].astype(F32)
        for m in range(1, 16):
            total = total + r.grad_w_got[k, m].astype(F32)
        r.grad_qkv[k] = total
    r.grad_o[...] = wo.step(2)
    arrived(small)
    for w in range(3):
        arrived([unsorted[w]])
        r.grad_experts[w] = r.unsorted[w, c].astype(F32) + r.unsorted_got[w].astype(F32)
    r.totals[...] = r.small_all[...]
    for sent in (net, back.net, out.net, wo.net):
        sent.sent()


def lanes_at(rank):
    return pl.ds(pl.multiple_of(rank * 128, 128), 128)


def finish_kernel(r):
    r.layer_out[...] = r.layer_in[...]
    r.grad_tokens[...] = r.tokens_in[...]
    r.w_query[...] = r.qkv[0]
    r.w_keyval[...] = r.qkv[1]
    r.w_output_t[...] = r.wo_in[...]
    r.w_gate[...] = r.experts[0]
    r.w_up[...] = r.experts[1]
    r.w_down[...] = r.experts[2]
    r.gates_t[...] = r.gates_in[...]
    total = r.totals[0, :3]
    for k in range(1, 16):
        total = total + r.totals[k, :3]
    r.gain1[...] = total[0:1]
    r.gain2[...] = total[1:2]
    r.sinks[...] = total[2:3, :16]
    for core in range(2):
        for j in range(8):
            for e in range(2):
                at = slice(4 * j + 2 * core + e, 4 * j + 2 * core + e + 1)
                row = r.totals[core * 8 + j, 4 + 2 * e : 6 + 2 * e]
                r.bias_gate[at] = row[0:1, :512]
                r.bias_up[at] = row[0:1, 512:]
                r.bias_down[at] = row[1:2]


def local(
    tokens, gain_attention, w_query, key_value_weight, w_output, sinks, gain_expert,
    w_gate, w_up, w_down, bias_gate, bias_up, bias_down, gates, routes, segments, cotangent,
):
    frequency = ROPE_BASE ** (-2.0 * jnp.arange(32, dtype=F32) / HEAD_DIM)
    common = dict(sinks=(sinks, SM)) | given(
        VM,
        gain1=gain_attention[None],
        gain2=gain_expert[None],
        routes_t=routes.T,
        tok=tokens,
        cot=cotangent,
        segments=segments[None],
        freq=jnp.tile(frequency, 4)[None],
    )
    rows = (128, 1024)
    slots = (2, 2, CAP, 1024)
    wide = (2, 1024, 2 * CAP)
    front = call(
        front_kernel,
        "front",
        0,
        common
        | given(
            VM, w_gate=w_gate, w_up=w_up, w_down=w_down, w_query=w_query,
            w_keyval=key_value_weight, w_output_t=w_output.T, gates_t=gates.T,
            bias_gate=bias_gate, bias_up=bias_up, bias_down=bias_down,
        ),
        dict(
            weights=((3, 4, 2, 2, 8, 64, 128), BF16, ANY),
            full0=(FULL, BF16, ANY),
            full1=(FULL, BF16, ANY),
            full2=(FULL, BF16, ANY),
            unpick=(wide, BF16, ANY),
            mid=(rows, F32, VM),
            normed1=(rows, BF16, VM),
            queries=(rows, BF16, VM),
            keyvals=((256, 1024), BF16, VM),
            attended=(rows, BF16, VM),
            logsum=((128, 128), F32, VM),
            rows=(slots, BF16, VM),
            cot_rows=(slots, BF16, VM),
            gate_rows=((2, 2, CAP, 128), F32, VM),
            place_t=((2, 2, 1024), F32, VM),
            bias=((2, 1, 2048), F32, VM),
        ),
        dict(
            pairs=bf16(3, 2, 64, 2048),
            shards=bf16(3, 64, 128),
            sorted=bf16(3, 8, 2, 64, 128),
            full0_v=bf16(*FULL),
            full1_v=bf16(*FULL),
            full2_v=bf16(*FULL),
            unpick_v=bf16(*wide),
            pick=bf16(2, 2 * CAP, 1024),
            slot_gate=f32(2, 2, CAP, 128),
            prev=bf16(*rows),
            normed2=bf16(*rows),
            row_all=bf16(2, 4, 128, 1024),
            cot_all=bf16(2, 4, 128, 1024),
            row_out=bf16(2, CAP, 1024),
            cot_out=bf16(2, CAP, 1024),
            send=DMA((94,)),
            recv=DMA((94,)),
            cot_send=DMA((8,)),
            cot_recv=DMA((8,)),
            row_send=DMA((8,)),
            row_recv=DMA((8,)),
            own=DMA((3,)),
            keep=DMA((3,)),
            store=DMA((4,)),
        ),
    )
    experts = expert_block(front)
    bufs = dict(
        back_bufs=row_reduce_scratch(), out_bufs=row_reduce_scratch(), wo_bufs=reduce_scratch(WO_ORDER)
    )
    flat = {}
    for name, items in bufs.items():
        flat |= {name + str(k): item for k, item in enumerate(items)}

    def kernel(r):
        for name, items in bufs.items():
            setattr(r, name, [getattr(r, name + str(k)) for k in range(len(items))])
        back_kernel(r)

    half = (2, 3, 2, 512, 128)
    back = call(
        kernel,
        "back",
        2,
        common
        | given(
            VM, place_t=front.place_t, mid=front.mid, queries=front.queries,
            keyvals=front.keyvals, attended=front.attended, logsum=front.logsum,
            grad_bias=experts.grad_bias,
        )
        | given(
            ANY, out_rows=experts.out_rows, back_rows=experts.back_rows, dots=experts.dots,
            grads=experts.grads, normed_all=experts.normed_all, unpick=front.unpick,
            full0=front.full0, full1=front.full1, full2=front.full2,
        ),
        dict(
            layer_out=(rows, F32, VM),
            grad_tokens=(rows, F32, VM),
            grad_gates=((8, 128), F32, VM),
            grad_qkv=((2, 64, 128), F32, VM),
            grad_o=((64, 128), F32, VM),
            grad_experts=((3, 64, 2048), F32, VM),
            totals=((16, 8, 1024), F32, VM),
        ),
        dict(
            unpick_v=bf16(*wide),
            back_own=bf16(2, CAP, 1024),
            back_got=bf16(2, CAP, 1024),
            out_got=bf16(2, CAP, 1024),
            dot_own=f32(2, CAP, 128),
            dot_got=f32(2, CAP, 128),
            back_parts=bf16(2, 4, 128, 1024),
            out_parts=bf16(2, 4, 128, 1024),
            token_dots=f32(8, 2, 2, 128),
            dots_all=f32(8, 2, 2, 128),
            z_own=bf16(*half),
            z_near=bf16(*half),
            z_far=bf16(*half),
            z_solo=bf16(*half),
            z_send=bf16(*half),
            z_got=bf16(*half),
            deal_out=bf16(3, 2, 2, 8, 64, 128),
            deal_got=bf16(3, 2, 8, 2, 64, 128),
            unsorted=bf16(3, 2, 64, 2048),
            unsorted_got=bf16(3, 64, 2048),
            full0_v=bf16(*FULL),
            full1_v=bf16(*FULL),
            full2_v=bf16(*FULL),
            normed_v=bf16(2, 4, 128, 1024),
            grad_wo=bf16(*FULL),
            dq=f32(*rows),
            dkv=f32(*rows),
            halo=bf16(*rows),
            halo_got=bf16(*rows),
            low=bf16(2, 128, 1024),
            low_all=bf16(2, 8, 128, 128),
            grad_w=bf16(2, 16, 64, 128),
            grad_w_got=bf16(2, 16, 64, 128),
            small=f32(8, 1024),
            small_got=f32(7, 8, 1024),
            small_all=f32(16, 8, 1024),
            send=DMA((143,)),
            recv=DMA((143,)),
            load=DMA((11,)),
        )
        | flat,
    )
    done = call(
        finish_kernel,
        "finish",
        None,
        given(
            VM, layer_in=back.layer_out, tokens_in=back.grad_tokens, qkv=back.grad_qkv,
            wo_in=back.grad_o, experts=back.grad_experts, gates_in=back.grad_gates,
            totals=back.totals,
        ),
        dict(
            layer_out=(rows, F32, VM),
            grad_tokens=(rows, F32, VM),
            w_query=((64, 128), F32, VM),
            w_keyval=((64, 128), F32, VM),
            w_output_t=((64, 128), F32, VM),
            w_gate=((64, 2048), F32, VM),
            w_up=((64, 2048), F32, VM),
            w_down=((64, 2048), F32, VM),
            gates_t=((8, 128), F32, VM),
            gain1=((1, 1024), F32, VM),
            gain2=((1, 1024), F32, VM),
            sinks=((1, 16), F32, VM),
            bias_gate=((32, 512), F32, VM),
            bias_up=((32, 512), F32, VM),
            bias_down=((32, 1024), F32, VM),
        ),
        {},
    )
    return (
        done.layer_out,
        done.grad_tokens,
        done.gain1[0],
        done.w_query,
        done.w_keyval,
        done.w_output_t.T,
        done.sinks[0],
        done.gain2[0],
        done.w_gate,
        done.w_up,
        done.w_down,
        done.bias_gate,
        done.bias_up,
        done.bias_down,
        done.gates_t.T,
    )


def solution(mesh):
    fine = Mesh(mesh.devices.reshape(2, 4, 2, 8), ("xh", "z", "core", "tp"))
    fsdp = ("xh", "z", "core")
    rows = P(("xh", "z", "core", "tp"), None)
    return jax.shard_map(
        local,
        mesh=fine,
        in_specs=(
            rows,
            P(),
            P(fsdp, "tp"),
            P(fsdp, "tp"),
            P("tp", fsdp),
            P(),
            P(),
            P(fsdp, "tp"),
            P(fsdp, "tp"),
            P(fsdp, "tp"),
            P(),
            P(),
            P(),
            P(fsdp, None),
            P(fsdp, None),
            P(fsdp),
            rows,
        ),
        out_specs=(
            rows,
            rows,
            P(),
            P(fsdp, "tp"),
            P(fsdp, "tp"),
            P("tp", fsdp),
            P(),
            P(),
            P(fsdp, "tp"),
            P(fsdp, "tp"),
            P(fsdp, "tp"),
            P(),
            P(),
            P(),
            rows,
        ),
        check_vma=False,
    )
```

```python
import itertools
import types

import jax
import jax.numpy as jnp
from jax import lax
from jax.experimental import pallas as pl
from jax.experimental.pallas import tpu as pltpu
from jax.sharding import Mesh
from jax.sharding import PartitionSpec as P

MESH = pl.DeviceIdType.MESH
HEAD_DIM = 64
WINDOW = 128
EPS = 1e-05
ROPE_BASE = 10000.0
CLAMP = 7.0
SLOPE = 1.702
SCALE = HEAD_DIM ** (-0.5)
NEG = -1e30
CAP = 272
F32 = jnp.float32
BF16 = jnp.bfloat16
ANY = pl.BlockSpec(memory_space=pl.ANY)
DMA = pltpu.SemaphoreType.DMA
VM = pl.BlockSpec(memory_space=pltpu.VMEM)
SM = pl.BlockSpec(memory_space=pltpu.SMEM)
VMEM_LIMIT = 58 * 1024 * 1024

SIZES = {"xh": 2, "z": 4, "c": 2, "xl": 2, "y": 4, "x": 4}


def coords():
    xh, z = lax.axis_index("xh"), lax.axis_index("z")
    c, t = lax.axis_index("core"), lax.axis_index("tp")
    xl, y = t // 4, t % 4
    return {"xh": xh, "z": z, "c": c, "xl": xl, "y": y, "x": 2 * xh + xl}


def moved(place, offset):
    out = dict(place)
    for axis, step in offset.items():
        out[axis] = (place[axis] + step) % SIZES[axis]
        if axis == "x":
            out["xh"], out["xl"] = out["x"] // 2, out["x"] % 2
    return out


def device(place):
    return (place["xh"], place["z"], place["c"], place["xl"] * 4 + place["y"])


def offsets(axes):
    ranges = [range(SIZES[a]) for a in axes]
    return [dict(zip(axes, o)) for o in itertools.product(*ranges) if any(o)]


def slot(place, axes):
    out = 0
    for a in axes:
        out = out * SIZES[a] + place[a]
    return out


def greet(peers):
    barrier = pltpu.get_barrier_semaphore()
    for peer in peers:
        pl.semaphore_signal(barrier, inc=1, device_id=device(peer), device_id_type=MESH)
    pl.semaphore_wait(barrier, len(peers))


def remote(src, dst, send, recv, peer):
    return pltpu.make_async_remote_copy(
        src_ref=src,
        dst_ref=dst,
        send_sem=send,
        recv_sem=recv,
        device_id=device(peer),
        device_id_type=MESH,
    )


def comm_params(ident):
    return pltpu.CompilerParams(
        collective_id=ident, has_side_effects=True, vmem_limit_bytes=VMEM_LIMIT
    )


def call(kernel, name, ident, ins, outs, scratch, **extra):
    names = list(ins) + list(outs) + list(scratch)

    def body(*refs):
        kernel(types.SimpleNamespace(**dict(zip(names, refs))))

    if ident is None:
        params = pltpu.CompilerParams(vmem_limit_bytes=VMEM_LIMIT)
    else:
        params = comm_params(ident)
    results = pl.pallas_call(
        body,
        out_shape=[jax.ShapeDtypeStruct(o[0], o[1]) for o in outs.values()],
        in_specs=[i[1] for i in ins.values()],
        out_specs=[o[2] for o in outs.values()],
        scratch_shapes=list(scratch.values()),
        compiler_params=params,
        name=name,
        **extra,
    )(*[i[0] for i in ins.values()])
    return types.SimpleNamespace(**dict(zip(outs, results)))


def given(spec, **arrays):
    return {name: (a, spec) for name, a in arrays.items()}


def f32(*shape):
    return pltpu.VMEM(shape, F32)


def bf16(*shape):
    return pltpu.VMEM(shape, BF16)


class Copies:
    def __init__(self, send, recv):
        self.send, self.recv, self.all = send, recv, []

    def go(self, src, dst, peer):
        k = len(self.all)
        copy = remote(src, dst, self.send.at[k], self.recv.at[k], peer)
        copy.start()
        self.all.append(copy)
        return copy

    def sent(self):
        for copy in self.all:
            copy.wait_send()


def arrived(copies):
    for copy in copies:
        copy.wait_recv()


def along(here, axis):
    return [moved(here, {axis: k}) for k in (1, 3, 2)]


def sequence_neighbours(here):
    rank = here["xl"] * 4 + here["y"]
    after, before = (rank + 1) % 8, (rank + 7) % 8
    return dict(here, xl=after // 4, y=after % 4), dict(here, xl=before // 4, y=before % 4)


def lanes_of(place):
    return pl.ds(pl.multiple_of(place["y"] * 128, 128), 128)


LEFT, RIGHT = pl.ds(0, 512), pl.ds(512, 512)


class RowGather:
    def __init__(self, here, src, out, send, recv):
        self.here, self.src, self.out = here, src, out
        self.net = Copies(send, recv)
        self.side, self.ups = moved(here, {"xl": 1}), along(here, "y")

    def first(self):
        xl, y = self.here["xl"], self.here["y"]
        go = self.net.go
        self.x = go(self.src.at[:, LEFT], self.out.at[xl, y, :, LEFT], self.side)
        self.y = [go(self.src.at[:, RIGHT], self.out.at[xl, y, :, RIGHT], p) for p in self.ups]

    def then(self):
        xl, y = self.here["xl"], self.here["y"]
        self.x.wait_recv()
        view = self.out.at[:, y, :, LEFT]
        self.beside = [self.net.go(view, view, p) for p in self.ups[:2]]
        arrived(self.y)
        view = self.out.at[xl, :, :, RIGHT]
        self.last = [self.net.go(view, view, self.side)]

    def relay(self):
        arrived(self.beside)
        up, down = self.ups[:2]
        view = self.out.at[0, down["y"], :, LEFT]
        self.last.append(self.net.go(view, view, up))
        view = self.out.at[1, up["y"], :, LEFT]
        self.last.append(self.net.go(view, view, down))

    def finish(self):
        arrived(self.last)
        self.net.sent()


class RowReduce:
    def __init__(self, here, parts, bufs, send, recv):
        self.here, self.parts = here, parts
        self.got_y, self.sum_y, self.got_x, self.sum_x, self.end_y, self.end_x = bufs
        self.net = Copies(send, recv)
        self.side, self.ups = moved(here, {"xl": 1}), along(here, "y")

    def right(self):
        self.x = self.net.go(self.parts.at[self.side["xl"], :, :, RIGHT], self.got_x, self.side)

    def left(self):
        self.y = [
            self.net.go(self.parts.at[:, p["y"], :, LEFT], self.got_y.at[k], p)
            for k, p in enumerate(self.ups)
        ]

    def then_right(self):
        self.x.wait_recv()
        mine = self.parts[self.here["xl"], :, :, RIGHT].astype(F32)
        self.sum_x[...] = (mine + self.got_x[...].astype(F32)).astype(BF16)
        self.last_x = [
            self.net.go(self.sum_x.at[p["y"]], self.end_x.at[k], p) for k, p in enumerate(self.ups)
        ]

    def then_left(self):
        arrived(self.y)
        total = self.parts[:, self.here["y"], :, LEFT].astype(F32)
        for k in range(3):
            total = total + self.got_y[k].astype(F32)
        self.sum_y[...] = total.astype(BF16)
        self.last_y = self.net.go(self.sum_y.at[self.side["xl"]], self.end_y, self.side)

    def result(self):
        self.last_y.wait_recv()
        left = self.sum_y[self.here["xl"]].astype(F32) + self.end_y[...].astype(F32)
        arrived(self.last_x)
        right = self.sum_x[self.here["y"]].astype(F32)
        for k in range(3):
            right = right + self.end_x[k].astype(F32)
        return jnp.concatenate([left, right], 1)


def row_reduce_scratch():
    return [
        bf16(3, 2, 128, 512),
        bf16(2, 128, 512),
        bf16(4, 128, 512),
        bf16(4, 128, 512),
        bf16(128, 512),
        bf16(3, 128, 512),
        DMA((8,)),
        DMA((8,)),
    ]


FULL = (2, 2, 4, 2, 64, 512)


def region(ref, place, held):
    xl = slice(None) if "x" in held else place["xl"]
    xh = slice(None) if "x" in held else place["xh"]
    z = slice(None) if "z" in held else place["z"]
    y = pl.ds(0, 512) if "y" in held else lanes_of(place)
    return ref.at[xl, xh, z, place["c"], :, y]


class Spread:
    def __init__(self, here, full, net):
        self.here, self.full, self.net = here, full, net

    def step(self, axis, held, src=None):
        view = region(self.full, self.here, held)
        src = view if src is None else src
        self.group = [self.net.go(src, view, p) for p in along(self.here, axis)]

    def step_beside(self, held):
        view = region(self.full, self.here, held)
        self.group = [self.net.go(view, view, p) for p in along(self.here, "y")[:2]]

    def relay(self):
        arrived(self.group)
        up, down = along(self.here, "y")[:2]
        c = self.here["c"]
        self.group = []
        for half, source, target in ((0, down, up), (1, up, down)):
            view = self.full.at[half, :, :, c, :, lanes_of(source)]
            self.group.append(self.net.go(view, view, target))

    def swap(self):
        view = self.full.at[:, :, :, self.here["c"]]
        self.group = [self.net.go(view, view, moved(self.here, {"c": 1}))]

    def wait(self):
        arrived(self.group)


def matrix(ref, half):
    return ref[half].reshape(1024, 512)


def piece(axis, place, dims):
    index = []
    for d in dims:
        if d in ("xl", "xh"):
            index.append(place[d] if axis == "x" else slice(None))
        else:
            index.append(place["z"] if axis == "z" else slice(None))
    index.append(slice(None))
    index.append(lanes_of(place) if axis == "y" else slice(None))
    return tuple(index)


def reduce_shapes(order):
    dims, lanes = ["xl", "xh", "z"], 512
    shapes = [((2, 2, 4, 64, 512), tuple(dims))]
    for axis in order:
        if axis == "x":
            dims = [d for d in dims if d not in ("xl", "xh")]
        elif axis == "z":
            dims = [d for d in dims if d != "z"]
        else:
            lanes = 128
        shapes.append((tuple(SIZES[d] for d in dims) + (64, lanes), tuple(dims)))
    return shapes


class Reduce:
    def __init__(self, here, parts, order, bufs, send, recv):
        self.here, self.parts, self.order = here, parts, order
        self.got0, self.sums, self.gots = bufs[0], bufs[1:4], bufs[4:7]
        self.net = Copies(send, recv)
        self.other = moved(here, {"c": 1})
        self.shapes = reduce_shapes(order)

    def swap(self):
        self.group = [self.net.go(self.parts.at[:, :, :, self.other["c"]], self.got0, self.other)]

    def go(self, s):
        axis, dims = self.order[s], self.shapes[s][1]
        self.group = [
            self.net.go(self.sums[s].at[piece(axis, p, dims)], self.gots[s].at[k], p)
            for k, p in enumerate(along(self.here, axis))
        ]

    def first(self):
        arrived(self.group)
        mine = self.parts[:, :, :, self.here["c"]].astype(F32)
        self.sums[0][...] = (mine + self.got0[...].astype(F32)).astype(BF16)
        self.go(0)

    def step(self, s):
        arrived(self.group)
        total = self.sums[s][piece(self.order[s], self.here, self.shapes[s][1])].astype(F32)
        for k in range(3):
            total = total + self.gots[s][k].astype(F32)
        if s < 2:
            self.sums[s + 1][...] = total.astype(BF16)
            self.go(s + 1)
        return total


def reduce_scratch(order):
    shapes = reduce_shapes(order)
    bufs = [bf16(*shapes[0][0])]
    bufs += [bf16(*shapes[s][0]) for s in range(3)]
    bufs += [bf16(3, *shapes[s + 1][0]) for s in range(3)]
    return bufs + [DMA((10,)), DMA((10,))]


def nn(a, b):
    return lax.dot_general(a, b, (((1,), (0,)), ((), ())), preferred_element_type=F32)


def nt(a, b):
    return lax.dot_general(a, b, (((1,), (1,)), ((), ())), preferred_element_type=F32)


def tn(a, b):
    return lax.dot_general(a, b, (((0,), (0,)), ((), ())), preferred_element_type=F32)


def one_hot_columns(start, core):
    row = lax.broadcasted_iota(jnp.int32, (1024, 1024), 0)
    column = lax.broadcasted_iota(jnp.int32, (1024, 1024), 1) + start
    expert = 4 * (row // 128) + 2 * core + (row // 64) % 2
    return (column == (row % 64) * 32 + expert).astype(F32).astype(BF16)


def rope_partner(values):
    lanes = values.shape[1]
    lane = lax.broadcasted_iota(jnp.int32, values.shape, 1)
    return jnp.where(
        lane % 64 < 32, pltpu.roll(values, lanes - 32, 1), pltpu.roll(values, 32, 1)
    )


def tiled(table):
    return jnp.concatenate([table] * 8, axis=1)


def head_pair(block):
    lane = lax.broadcasted_iota(jnp.int32, block.shape, 1) < 64
    wide = block.astype(F32)
    swapped = pltpu.roll(wide, 64, 1)
    zero = jnp.zeros_like(wide)
    keys = jnp.concatenate([jnp.where(lane, wide, zero), jnp.where(lane, zero, swapped)], 0)
    values = jnp.concatenate([jnp.where(lane, swapped, zero), jnp.where(lane, zero, wide)], 0)
    return keys.astype(BF16), values.astype(BF16)


def window_mask(segq, segk):
    row = lax.broadcasted_iota(jnp.int32, (128, 256), 0)
    column = lax.broadcasted_iota(jnp.int32, (128, 256), 1)
    distance = 128 + row - column
    return (segq == segk) & (distance >= 0) & (distance < WINDOW)


def rope_at(start, rows, freq):
    row = lax.broadcasted_iota(jnp.int32, (rows, 128), 0)
    lane = lax.broadcasted_iota(jnp.int32, (rows, 128), 1)
    angles = (row + start).astype(F32) * freq
    cosine, sine = jnp.cos(angles), jnp.sin(angles)
    return cosine, jnp.where(lane % 64 < 32, -sine, sine), lane < 64


def rope_queries(rank, freq):
    cosine, sine, _ = rope_at(128 * rank, 128, freq)
    return tiled(cosine), tiled(sine)


def rope_keyvals(start, rows, freq):
    cosine, sine, keys = rope_at(start, rows, freq)
    return tiled(jnp.where(keys, cosine, 1.0)), tiled(jnp.where(keys, sine, 0.0))


def mask_at(segments, rank):
    own = segments[:, pl.ds(pl.multiple_of(128 * rank, 128), 128)]
    prev = segments[:, pl.ds(pl.multiple_of(128 * ((rank + 7) % 8), 128), 128)]
    prev = jnp.where(rank == 0, -1, prev)
    row = lax.broadcasted_iota(jnp.int32, (128, 128), 0)
    column = lax.broadcasted_iota(jnp.int32, (128, 128), 1)
    segq = jnp.sum(jnp.where(row == column, own.astype(F32), 0.0), 1, keepdims=True)
    return window_mask(segq, jnp.concatenate([prev, own], 1).astype(F32))


def slot_tables(r, rank):
    row = lax.broadcasted_iota(jnp.int32, (1024, 1024), 0)
    column = lax.broadcasted_iota(jnp.int32, (1024, 1024), 1)
    before = (row < column).astype(F32).astype(BF16)
    routes_t, gates_t = r.routes_t[...], r.gates_t[...]
    hits, shares = [], []
    for el in range(4):
        named = routes_t == 4 * rank + el
        hits.append(jnp.sum(named.astype(F32), 0, keepdims=True))
        shares.append(jnp.sum(jnp.where(named, gates_t, 0.0), 0, keepdims=True))
    earlier = nn(jnp.concatenate(hits + [jnp.zeros((12, 1024), F32)], 0).astype(BF16), before)
    places = [jnp.where(hits[el] > 0, earlier[el : el + 1], -1.0) for el in range(4)]
    columns = jnp.concatenate(places + [jnp.zeros((124, 1024), F32)], 0).T
    slot = lax.broadcasted_iota(jnp.int32, (CAP, 1024), 0).astype(F32)
    wide = lax.broadcasted_iota(jnp.int32, (1024, 2 * CAP), 1).astype(F32)
    for c in range(2):
        for e in range(2):
            el = 2 * c + e
            r.place_t[c, e : e + 1] = places[el]
            hot = slot == places[el]
            r.pick[c, CAP * e : CAP * e + CAP] = hot.astype(F32).astype(BF16)
            share = jnp.sum(jnp.where(hot, shares[el], 0.0), 1, keepdims=True)
            r.slot_gate[c, e] = jnp.broadcast_to(share, (CAP, 128))
        low = (wide == columns[:, 2 * c : 2 * c + 1]) & (wide < CAP)
        high = (wide - CAP == columns[:, 2 * c + 1 : 2 * c + 2]) & (wide >= CAP)
        r.unpick_v[c] = (low | high).astype(F32).astype(BF16)


DEAL_AXES = ("xh", "xl", "y")


def front_kernel(r):
    here = coords()
    c, xh, z, xl, y = (here[a] for a in ("c", "xh", "z", "xl", "y"))
    rank = xl * 4 + y
    other = moved(here, {"c": 1})
    after, before = sequence_neighbours(here)
    dealt = [moved(here, o) for o in offsets(DEAL_AXES)]
    up, down = moved(here, {"z": 1}), moved(here, {"z": 3})
    parts = (r.w_gate, r.w_up, r.w_down)
    fulls = (r.full0_v, r.full1_v, r.full2_v)
    for w, ref in enumerate(parts):
        r.pairs[w, c] = ref[...]
    for p, ref in enumerate((r.w_query, r.w_keyval, r.w_output_t)):
        r.shards[p] = ref[...]
    own = [
        pltpu.make_async_copy(r.shards.at[p], region(fulls[p], here, ""), r.own.at[p])
        for p in range(3)
    ]
    for copy in own:
        copy.start()
    greet([other, after, before] + [p for a in "xyz" for p in along(here, a)] + dealt)
    net = Copies(r.send, r.recv)
    swaps = [net.go(ref, r.pairs.at[w, c], other) for w, ref in enumerate(parts)]
    q_full, kv_full, o_full = (Spread(here, full, net) for full in fulls)
    kv_full.step("y", "", r.shards.at[1])
    q_full.step("z", "", r.shards.at[0])
    o_full.step("z", "", r.shards.at[2])
    cots = RowGather(here, r.cot, r.cot_all, r.cot_send, r.cot_recv)
    first = 4 * rank + 2 * c
    for e in range(2):
        r.bias[e, :, :512] = r.bias_gate[pl.ds(first + e, 1)]
        r.bias[e, :, 512:1024] = r.bias_up[pl.ds(first + e, 1)]
        r.bias[e, :, 1024:] = r.bias_down[pl.ds(first + e, 1)]
    r.cot_all[xl, y] = r.cot[...]
    hot_left = one_hot_columns(0, c)
    for copy in own:
        copy.wait()
    kv_full.wait()
    kv_full.step("x", "y")
    q_full.wait()
    q_full.step("y", "z")
    o_full.wait()
    o_full.step("x", "z")
    halo = net.go(r.tok, r.prev, after)
    hot = jnp.concatenate([hot_left, one_hot_columns(1024, c)], 1)
    deals, keeps = [], []

    def sort(w):
        arrived([swaps[w]])
        rows = r.pairs[w].reshape(128, 2048)
        r.sorted[w] = nt(hot, rows).astype(BF16).reshape(8, 2, 64, 128)
        mine = r.weights.at[w, z, xh, :, rank]
        keeps.append(pltpu.make_async_copy(r.sorted.at[w, rank], mine, r.keep.at[w]))
        keeps[w].start()

    def deal(w):
        mine = r.weights.at[w, z, xh, :, rank]
        deals.append([net.go(r.sorted.at[w, p["xl"] * 4 + p["y"]], mine, p) for p in dealt])

    ring, last_ring = [], []

    def send_on(w):
        arrived(deals[w])
        keeps[w].wait()
        view = r.weights.at[w, z]
        ring.append([net.go(view, view, up), net.go(view, view, down)])

    def pass_on(w):
        arrived(ring[w])
        view = r.weights.at[w, down["z"], 0]
        last_ring.append(net.go(view, view, up))
        view = r.weights.at[w, up["z"], 1]
        last_ring.append(net.go(view, view, down))

    sort(0)
    deal(0)
    kv_full.wait()
    kv_full.step("z", "yx")
    q_full.wait()
    q_full.step("x", "zy")
    o_full.wait()
    o_full.step_beside("zx")
    sort(1)
    sort(2)
    slot_tables(r, rank)
    stores = [pltpu.make_async_copy(r.unpick_v, r.unpick, r.store.at[0])]
    stores[0].start()

    def save(k, full, result):
        stores.append(pltpu.make_async_copy(full, result, r.store.at[k]))
        stores[k].start()

    send_on(0)
    deal(1)
    o_full.relay()
    kv_full.wait()
    kv_full.swap()
    halo.wait_recv()
    tok = r.tok[...].astype(F32)
    both = jnp.concatenate([r.prev[...].astype(F32), tok], 0)
    scale = lax.rsqrt(jnp.mean(both * both, -1, keepdims=True) + EPS)
    normed = (both * scale * r.gain1[...]).astype(BF16)
    normed_own = normed[128:]
    r.normed1[...] = normed_own
    keep_normed = pltpu.make_async_copy(r.normed1, r.normed_all.at[xl, y], r.own.at[3])
    keep_normed.start()
    q_full.wait()
    q_full.swap()
    kv_full.wait()
    deal(2)
    cots.first()
    save(1, r.full1_v, r.full1)
    kv = jnp.concatenate([nn(normed, matrix(r.full1_v, 0)), nn(normed, matrix(r.full1_v, 1))], 1)
    cosine, sine = rope_keyvals(128 * rank - 128, 256, r.freq[...])
    kv = (kv * cosine + rope_partner(kv) * sine).astype(BF16)
    r.keyvals[...] = kv
    o_full.wait()
    o_full.swap()
    pass_on(0)
    gates = net.go(r.slot_gate.at[other["c"]], r.gate_rows.at[c], other)
    r.gate_rows[c] = r.slot_gate[c]
    mask = mask_at(r.segments, rank)
    lane = lax.broadcasted_iota(jnp.int32, (128, 128), 1)
    q_full.wait()
    save(2, r.full0_v, r.full0)
    q = jnp.concatenate(
        [nn(normed_own, matrix(r.full0_v, 0)), nn(normed_own, matrix(r.full0_v, 1))], 1
    )
    cosine, sine = rope_queries(rank, r.freq[...])
    q = (q * cosine + rope_partner(q) * sine).astype(BF16)
    r.queries[...] = q
    send_on(1)
    sums = jnp.zeros((128, 128), F32)
    for g in range(8):
        part = slice(128 * g, 128 * g + 128)
        keys, values = head_pair(kv[:, part])
        scores = nt(q[:, part], keys) * SCALE
        shares = []
        for h in range(2):
            masked = jnp.where(mask, scores[:, 256 * h : 256 * h + 256], NEG)
            sink = r.sinks[2 * g + h]
            peak = jnp.maximum(jnp.max(masked, -1, keepdims=True), sink)
            total = jnp.exp(sink - peak) + jnp.sum(jnp.exp(masked - peak), -1, keepdims=True)
            log_total = peak + jnp.log(total)
            shares.append(jnp.exp(masked - log_total).astype(BF16))
            sums = jnp.where(lane == 2 * g + h, log_total, sums)
        r.attended[:, part] = nn(jnp.concatenate(shares, 1), values).astype(BF16)
        if g == 4:
            send_on(2)
    r.logsum[...] = sums
    cots.then()
    o_full.wait()
    save(3, r.full2_v, r.full2)
    out = (
        tok
        + nt(r.attended[:, :512], matrix(r.full2_v, 0))
        + nt(r.attended[:, 512:], matrix(r.full2_v, 1))
    )
    r.mid[...] = out
    scale = lax.rsqrt(jnp.mean(out * out, -1, keepdims=True) + EPS)
    r.normed2[...] = (out * scale * r.gain2[...]).astype(BF16)

    rows = RowGather(here, r.normed2, r.row_all, r.row_send, r.row_recv)
    rows.first()
    r.row_all[xl, y] = r.normed2[...]
    cots.relay()

    def to_slots(gathered, outgoing, result):
        tokens = gathered[...].reshape(1024, 1024)
        outgoing[...] = nn(r.pick[other["c"]], tokens).astype(BF16).reshape(2, CAP, 1024)
        copy = net.go(outgoing, result.at[c], other)
        result[c] = nn(r.pick[c], tokens).astype(BF16).reshape(2, CAP, 1024)
        return copy

    rows.then()
    pass_on(1)
    cots.finish()
    cot_copy = to_slots(r.cot_all, r.cot_out, r.cot_rows)
    rows.relay()
    pass_on(2)
    rows.finish()
    near = [
        net.go(r.normed1.at[:, LEFT], r.normed_all.at[xl, y, :, LEFT], moved(here, {"xl": 1}))
    ]
    view = r.normed_all.at[xl, y, :, RIGHT]
    near += [net.go(r.normed1.at[:, RIGHT], view, p) for p in along(here, "y")]
    row_copy = to_slots(r.row_all, r.row_out, r.rows)
    arrived([gates, cot_copy, row_copy])
    arrived(near)
    arrived(last_ring)
    for copy in stores:
        copy.wait()
    keep_normed.wait()
    net.sent()


def expert_kernel(r):
    turn = pl.program_id(0)
    here = coords()
    xl, y = here["xl"], here["y"]
    side, ups = moved(here, {"xl": 1}), along(here, "y")
    out = r.normed_all
    column, line = out.at[:, y, :, LEFT], out.at[xl, :, :, RIGHT]
    then = [
        remote(column, column, r.send.at[k], r.recv.at[k], p) for k, p in enumerate(ups)
    ]
    then.append(remote(line, line, r.send.at[3], r.recv.at[3], side))

    @pl.when(turn == 0)
    def _():
        greet([side] + ups)
        for item in then:
            item.start()

    def stacked(w):
        return jnp.concatenate(
            [r.weights[w, m % 4, m // 4, 0].reshape(512, 128) for m in range(8)], 1
        )

    w_gate, w_up, w_down = stacked(0), stacked(1), stacked(2)
    bias = r.bias[0]
    x = r.rows[:, 0].reshape(2 * CAP, 1024)
    tanh_gate = jnp.tanh((nt(x, w_gate) + bias[:, :512]) / CLAMP)
    tanh_up = jnp.tanh((nt(x, w_up) + bias[:, 512:1024]) / CLAMP)
    soft_gate, soft_up = CLAMP * tanh_gate, CLAMP * tanh_up
    sig = jax.nn.sigmoid(SLOPE * soft_gate)
    glu = soft_gate * sig
    hidden = (glu * (soft_up + 1.0)).astype(BF16)
    produced = nn(hidden, w_down) + bias[:, 1024:]
    share = r.gate_rows[:, 0].reshape(2 * CAP, 128)[:, :1]
    cot = r.cot_rows[:, 0].reshape(2 * CAP, 1024).astype(F32)
    r.out_rows[:, 0] = (share * produced).astype(BF16).reshape(2, CAP, 1024)

    products = produced * cot
    partial = products[:, :128]
    for m in range(1, 8):
        partial = partial + products[:, 128 * m : 128 * m + 128]
    r.dots[:, 0] = partial.reshape(2, CAP, 128)
    scaled = share * cot
    r.grad_bias[0, :, 1024:] = jnp.sum(scaled, 0, keepdims=True)
    rows_grad = scaled.astype(BF16)
    hidden_grad = nt(rows_grad, w_down)
    gate_grad = (
        hidden_grad
        * (soft_up + 1.0)
        * (sig + SLOPE * glu * (1.0 - sig))
        * (1.0 - tanh_gate * tanh_gate)
    )
    up_grad = hidden_grad * glu * (1.0 - tanh_up * tanh_up)
    r.grad_bias[0, :, :512] = jnp.sum(gate_grad, 0, keepdims=True)
    r.grad_bias[0, :, 512:1024] = jnp.sum(up_grad, 0, keepdims=True)
    gate_low, up_low = gate_grad.astype(BF16), up_grad.astype(BF16)
    back = (nn(gate_low, w_gate) + nn(up_low, w_up)).astype(BF16)
    r.back_rows[:, 0] = back.reshape(2, CAP, 1024)
    for w, (left, right) in enumerate(((gate_low, x), (up_low, x), (hidden, rows_grad))):
        grad = tn(left, right).astype(BF16)
        for m in range(8):
            r.grads[m % 4, m // 4, w, 0] = grad[:, 128 * m : 128 * m + 128]

    @pl.when(turn == 1)
    def _():
        for item in then:
            item.wait()


def expert_block(front):
    def at(dim, *shape):
        return pl.BlockSpec(
            shape[:dim] + (1,) + shape[dim:],
            lambda e: (0,) * dim + (e,) + (0,) * (len(shape) - dim),
        )

    per_row, per_slot = at(1, 2, CAP, 1024), at(1, 2, CAP, 128)
    stacked, vector = at(3, 4, 2, 3, 512, 128), at(0, 1, 2048)
    return call(
        expert_kernel,
        "experts",
        1,
        dict(
            rows=(front.rows, per_row),
            cot_rows=(front.cot_rows, per_row),
            gate_rows=(front.gate_rows, per_slot),
            weights=(front.weights, at(3, 3, 4, 2, 8, 64, 128)),
            bias=(front.bias, vector),
            normed_near=(front.normed_all, ANY),
        ),
        dict(
            out_rows=((2, 2, CAP, 1024), BF16, per_row),
            back_rows=((2, 2, CAP, 1024), BF16, per_row),
            dots=((2, 2, CAP, 128), F32, per_slot),
            grads=((4, 2, 3, 2, 512, 128), BF16, stacked),
            grad_bias=((2, 1, 2048), F32, vector),
            normed_all=((2, 4, 128, 1024), BF16, ANY),
        ),
        dict(send=DMA((4,)), recv=DMA((4,))),
        grid=(2,),
        input_output_aliases={5: 5},
    )


def norm_back(values, gain, grad):
    scale = lax.rsqrt(jnp.mean(values * values, -1, keepdims=True) + EPS)
    normed = values * scale
    weighted = gain * grad
    back = scale * (weighted - normed * jnp.mean(weighted * normed, -1, keepdims=True))
    return back, jnp.sum(grad * normed, 0, keepdims=True)


WO_ORDER = ("z", "x", "y")


class ZSum:
    def __init__(self, r, here, net):
        self.r, self.net, self.z = r, net, here["z"]
        self.up, self.down = moved(here, {"z": 1}), moved(here, {"z": 3})
        far = (self.z + 2) % 4
        self.solo, self.both = [None] * 3, [None] * 3
        self.far = [
            [
                net.go(r.grads.at[far, 0, w], r.z_far.at[0, w], self.up),
                net.go(r.grads.at[far, 1, w], r.z_far.at[1, w], self.down),
            ]
            for w in range(3)
        ]

    def alone(self, w):
        r, up, down = self.r, self.up, self.down
        self.solo[w] = [
            self.net.go(r.grads.at[up["z"], 1, w], r.z_solo.at[1, w], up),
            self.net.go(r.grads.at[down["z"], 0, w], r.z_solo.at[0, w], down),
        ]

    def add(self, w):
        r = self.r
        arrived(self.far[w])
        for half in range(2):
            r.z_send[half, w] = (
                r.z_near[half, w].astype(F32) + r.z_far[half, w].astype(F32)
            ).astype(BF16)
        self.both[w] = [
            self.net.go(r.z_send.at[0, w], r.z_got.at[0, w], self.up),
            self.net.go(r.z_send.at[1, w], r.z_got.at[1, w], self.down),
        ]

    def total(self, w, half):
        r = self.r
        return (
            r.z_own[half, w].astype(F32)
            + r.z_got[half, w].astype(F32)
            + r.z_solo[half, w].astype(F32)
        ).astype(BF16)

    def wait(self, w):
        arrived(self.solo[w] + self.both[w])


def back_kernel(r):
    here = coords()
    c, xh, z, xl, y = (here[a] for a in ("c", "xh", "z", "xl", "y"))
    rank = xl * 4 + y
    other = moved(here, {"c": 1})
    after, before = sequence_neighbours(here)
    everyone = [moved(here, o) for o in offsets(("xl", "y"))]
    dealt = [moved(here, o) for o in offsets(DEAL_AXES)]
    owners = [moved(here, o) for o in offsets(("xh", "z", "c"))]
    planes = [moved(here, o) for o in offsets(("xh", "z"))]
    places = [moved(here, o) for o in offsets(("c", "xl", "y"))]
    loads = []

    def load(src, dst):
        copy = pltpu.make_async_copy(src, dst, r.load.at[len(loads)])
        copy.start()
        loads.append(copy)
        return copy

    get_unpick = load(r.unpick, r.unpick_v)
    get_back = load(r.back_rows.at[c], r.back_own)
    get_dots = load(r.dots.at[c], r.dot_own)
    get_near = [
        load(r.grads.at[(z + 1) % 4, 0], r.z_near.at[0]),
        load(r.grads.at[(z + 3) % 4, 1], r.z_near.at[1]),
    ]
    get_full2 = load(r.full2, r.full2_v)
    get_z = load(r.grads.at[z], r.z_own)
    get_full0 = load(r.full0, r.full0_v)
    get_full1 = load(r.full1, r.full1_v)
    get_normed = load(r.normed_all, r.normed_v)
    greet(
        [other, after, before]
        + [p for a in "xyz" for p in along(here, a)]
        + everyone + dealt + owners + planes + places
    )
    net = Copies(r.send, r.recv)
    back_swap = net.go(r.back_rows.at[other["c"]], r.back_got, other)
    for e in range(2):
        r.bias_sum[2 * e : 2 * e + 1] = r.grad_bias[e, :, :1024]
        r.bias_sum[2 * e + 1 : 2 * e + 2] = r.grad_bias[e, :, 1024:]
    biases = [net.go(r.bias_sum, r.bias_got.at[k], p) for k, p in enumerate(planes)]
    zsum = ZSum(r, here, net)

    def to_tokens(own, got, parts, columns):
        mine = nn(r.unpick_v[c], own[:, :, columns].reshape(2 * CAP, 512))
        theirs = nn(r.unpick_v[other["c"]], got[:, :, columns].reshape(2 * CAP, 512))
        parts[:, :, :, columns] = (mine + theirs).astype(BF16).reshape(2, 4, 128, 512)

    back = RowReduce(here, r.back_parts, r.back_bufs[:6], *r.back_bufs[6:])
    out = RowReduce(here, r.out_parts, r.out_bufs[:6], *r.out_bufs[6:])
    get_unpick.wait()
    get_back.wait()
    back_swap.wait_recv()
    dot_swap = net.go(r.dots.at[other["c"]], r.dot_got, other)
    out_swap = net.go(r.out_rows.at[other["c"]], r.out_got, other)
    to_tokens(r.back_own, r.back_got, r.back_parts, RIGHT)
    back.right()
    to_tokens(r.back_own, r.back_got, r.back_parts, LEFT)
    back.left()
    get_out = load(r.out_rows.at[c], r.back_own)

    get_dots.wait()
    dot_swap.wait_recv()
    slot = lax.broadcasted_iota(jnp.int32, (CAP, 1024), 0).astype(F32)
    for source, core in ((r.dot_own, c), (r.dot_got, other["c"])):
        for e in range(2):
            totals = jnp.sum(source[e], 1, keepdims=True)
            hot = slot == r.place_t[core, e : e + 1]
            line = jnp.sum(jnp.where(hot, totals, 0.0), 0, keepdims=True)
            for j in range(8):
                r.token_dots[j, core, e : e + 1] = line[:, 128 * j : 128 * j + 128]
    r.dots_all[rank] = r.token_dots[rank]
    dot_copies = [
        net.go(r.token_dots.at[p["xl"] * 4 + p["y"]], r.dots_all.at[rank], p) for p in everyone
    ]
    for copy in get_near:
        copy.wait()
    zsum.add(0)
    zsum.alone(0)
    get_out.wait()
    out_swap.wait_recv()
    to_tokens(r.back_own, r.out_got, r.out_parts, RIGHT)
    to_tokens(r.back_own, r.out_got, r.out_parts, LEFT)
    back.then_right()
    back.then_left()
    out.right()
    out.left()
    for w in (1, 2):
        zsum.add(w)
        zsum.alone(w)
    spot = c * 8 + rank
    arrived(biases)
    total = r.bias_sum[...]
    for k in range(7):
        total = total + r.bias_got[k]
    r.bias_all[spot] = total
    biases = [net.go(r.bias_all.at[spot], r.bias_all.at[spot], p) for p in places]
    moved_in = back.result()

    step, gain_part = norm_back(r.mid[...], r.gain2[...], moved_in)
    for k in range(8):
        r.small[8 + k : 9 + k] = gain_part[:, 128 * k : 128 * k + 128]
    mid_grad = r.cot[...].astype(F32) + step
    low = mid_grad.astype(BF16)
    for half in range(2):
        columns = slice(512 * half, 512 * half + 512)
        r.grad_wo[half] = tn(low, r.attended[:, columns]).astype(BF16).reshape(FULL[1:])
    wo = Reduce(here, r.grad_wo, WO_ORDER, r.wo_bufs[:7], *r.wo_bufs[7:])
    wo.swap()
    get_full2.wait()
    out_grad = jnp.concatenate([nn(low, matrix(r.full2_v, 0)), nn(low, matrix(r.full2_v, 1))], 1)
    out_grad = out_grad.astype(BF16)
    mask = mask_at(r.segments, rank)
    lane_row = lax.broadcasted_iota(jnp.int32, (1, 128), 1)
    lane = lax.broadcasted_iota(jnp.int32, (256, 128), 1) < 64
    sink_grads = jnp.zeros((1, 128), F32)
    halos = []
    for g in range(8):
        part = slice(128 * g, 128 * g + 128)
        keys, values = head_pair(r.keyvals[:, part])
        q = r.queries[:, part]
        grad_block = out_grad[:, part]
        scores = nt(q, keys) * SCALE
        share_grads = nt(grad_block, values)
        shares, score_grads = [], []
        for h in range(2):
            columns = slice(256 * h, 256 * h + 256)
            log_total = r.logsum[:, 2 * g + h : 2 * g + h + 1]
            share = jnp.exp(jnp.where(mask, scores[:, columns], NEG) - log_total)
            term = jnp.sum(share * share_grads[:, columns], -1, keepdims=True)
            shares.append(share.astype(BF16))
            score_grads.append((share * (share_grads[:, columns] - term)).astype(BF16))
            sink_part = -jnp.sum(jnp.exp(r.sinks[2 * g + h] - log_total) * term, 0, keepdims=True)
            sink_grads = jnp.where(lane_row == 2 * g + h, sink_part, sink_grads)
        shares = jnp.concatenate(shares, 1)
        score_grads = jnp.concatenate(score_grads, 1)
        r.dq[:, part] = nn(score_grads, keys) * SCALE
        from_scores = tn(score_grads, q) * SCALE
        from_shares = tn(shares, grad_block)
        joined = jnp.where(
            lane,
            from_scores[:256] + pltpu.roll(from_scores[256:], 64, 1),
            pltpu.roll(from_shares[:256], 64, 1) + from_shares[256:],
        )
        r.halo[:, part] = joined[:128].astype(BF16)
        r.dkv[:, part] = joined[128:]
        if g == 3:
            wo.first()
        if g % 4 == 3:
            view = slice(512 * (g // 4), 512 * (g // 4) + 512)
            halos.append(net.go(r.halo.at[:, view], r.halo_got.at[:, view], before))

    get_z.wait()
    deals = []

    def deal(w):
        zsum.wait(w)
        for half in range(2):
            r.deal_out[w, half] = zsum.total(w, half).reshape(2, 8, 64, 128)
        r.deal_got[w, xh, rank] = r.deal_out[w, xh, :, rank]
        deals.append(
            [
                net.go(
                    r.deal_out.at[w, p["xh"], :, p["xl"] * 4 + p["y"]], r.deal_got.at[w, xh, rank], p
                )
                for p in dealt
            ]
        )

    def to_columns(low, k):
        r.low[k] = low
        r.low_all[k, rank] = r.low[k, :, lanes_at(rank)]
        return [net.go(r.low.at[k, :, lanes_at(p["xl"] * 4 + p["y"])], r.low_all.at[k, rank], p) for p in everyone]

    grad_q = r.dq[...]
    cosine, sine = rope_queries(rank, r.freq[...])
    low = (grad_q * cosine - rope_partner(grad_q) * sine).astype(BF16)
    q_copies = to_columns(low, 0)
    get_full0.wait()
    first_back = nt(low[:, :512], matrix(r.full0_v, 0)) + nt(low[:, 512:], matrix(r.full0_v, 1))

    hot = one_hot_columns(0, c)
    r.full2_v[0] = hot[:, :512].reshape(FULL[1:])
    r.full2_v[1] = hot[:, 512:].reshape(FULL[1:])
    hot = one_hot_columns(1024, c)
    r.full0_v[0] = hot[:, :512].reshape(FULL[1:])
    r.full0_v[1] = hot[:, 512:].reshape(FULL[1:])
    arrived(halos)
    grad_kv = r.dkv[...] + r.halo_got[...].astype(F32)
    cosine, sine = rope_keyvals(128 * rank, 128, r.freq[...])
    low = (grad_kv * cosine - rope_partner(grad_kv) * sine).astype(BF16)
    kv_copies = to_columns(low, 1)
    deal(0)
    get_full1.wait()
    first_back = (
        first_back + nt(low[:, :512], matrix(r.full1_v, 0)) + nt(low[:, 512:], matrix(r.full1_v, 1))
    )
    norm_grad, gain_part = norm_back(r.tok[...].astype(F32), r.gain1[...], first_back)
    r.grad_tokens[...] = mid_grad + norm_grad
    for k in range(8):
        r.small[k : k + 1] = gain_part[:, 128 * k : 128 * k + 128]
    r.small[16:24] = jnp.concatenate([sink_grads, jnp.zeros((7, 128), F32)], 0)
    small = [net.go(r.small, r.small_got.at[k], p) for k, p in enumerate(planes)]

    get_normed.wait()
    normed = r.normed_v[...].reshape(1024, 1024)
    mine = (xh * 4 + z) * 2 + c
    sums = []

    def product(k, copies):
        arrived(copies)
        block = tn(normed, r.low_all[k].reshape(1024, 128))
        r.grad_w[k] = block.astype(BF16).reshape(16, 64, 128)
        r.grad_w_got[k, mine] = r.grad_w[k, mine]
        sums.append(
            [
                net.go(
                    r.grad_w.at[k, (p["xh"] * 4 + p["z"]) * 2 + p["c"]], r.grad_w_got.at[k, mine], p
                )
                for p in owners
            ]
        )

    deal(1)
    product(0, q_copies)
    out.then_right()
    out.then_left()
    product(1, kv_copies)
    deal(2)
    unsorted = []

    def unsort(w):
        arrived(deals[w])
        summed = r.deal_got[w, 0].astype(F32) + r.deal_got[w, 1].astype(F32)
        lines = summed.reshape(1024, 128).T.astype(BF16)
        for k in range(4):
            wide = nn(lines, matrix(r.full2_v if k < 2 else r.full0_v, k % 2)).astype(BF16)
            r.unsorted[w, :, :, 512 * k : 512 * k + 512] = wide.reshape(2, 64, 512)
        unsorted.append(net.go(r.unsorted.at[w, other["c"]], r.unsorted_got.at[w], other))

    unsort(0)
    wo.step(0)
    unsort(1)
    arrived(small)
    total = r.small[...]
    for k in range(7):
        total = total + r.small_got[k]
    r.small_all[spot] = total
    small = [net.go(r.small_all.at[spot], r.small_all.at[spot], p) for p in places]
    r.layer_out[...] = r.mid[...] + out.result()
    arrived(dot_copies)
    own_routes = r.routes_t[:, lanes_at(rank)]
    chosen = jnp.zeros((8, 128), F32)
    for j in range(8):
        for core in range(2):
            for e in range(2):
                line = r.dots_all[j, core, e : e + 1]
                chosen = jnp.where(own_routes == 4 * j + 2 * core + e, line, chosen)
    r.grad_gates[...] = chosen
    wo.step(1)
    unsort(2)
    for k, copies in enumerate(sums):
        arrived(copies)
        total = r.grad_w_got[k, 0].astype(F32)
        for m in range(1, 16):
            total = total + r.grad_w_got[k, m].astype(F32)
        r.grad_qkv[k] = total
    r.grad_o[...] = wo.step(2)
    arrived(small)
    arrived(biases)
    for w in range(3):
        arrived([unsorted[w]])
        r.grad_experts[w] = r.unsorted[w, c].astype(F32) + r.unsorted_got[w].astype(F32)
    r.totals[...] = r.small_all[...]
    r.biases[...] = r.bias_all[...]
    for sent in (net, back.net, out.net, wo.net):
        sent.sent()


def lanes_at(rank):
    return pl.ds(pl.multiple_of(rank * 128, 128), 128)


def finish_kernel(r):
    r.layer_out[...] = r.layer_in[...]
    r.grad_tokens[...] = r.tokens_in[...]
    r.w_query[...] = r.qkv[0]
    r.w_keyval[...] = r.qkv[1]
    r.w_output_t[...] = r.wo_in[...]
    r.w_gate[...] = r.experts[0]
    r.w_up[...] = r.experts[1]
    r.w_down[...] = r.experts[2]
    r.gates_t[...] = r.gates_in[...]
    total = r.totals[0]
    for k in range(1, 16):
        total = total + r.totals[k]
    for k in range(8):
        r.gain1[:, 128 * k : 128 * k + 128] = total[k : k + 1]
        r.gain2[:, 128 * k : 128 * k + 128] = total[8 + k : 9 + k]
    r.sinks[...] = total[16:17, :16]
    for core in range(2):
        for j in range(8):
            for e in range(2):
                at = slice(4 * j + 2 * core + e, 4 * j + 2 * core + e + 1)
                row = r.biases[core * 8 + j, 2 * e : 2 * e + 2]
                r.bias_gate[at] = row[0:1, :512]
                r.bias_up[at] = row[0:1, 512:]
                r.bias_down[at] = row[1:2]


def local(
    tokens, gain_attention, w_query, key_value_weight, w_output, sinks, gain_expert,
    w_gate, w_up, w_down, bias_gate, bias_up, bias_down, gates, routes, segments, cotangent,
):
    frequency = ROPE_BASE ** (-2.0 * jnp.arange(32, dtype=F32) / HEAD_DIM)
    common = dict(sinks=(sinks, SM)) | given(
        VM,
        gain1=gain_attention[None],
        gain2=gain_expert[None],
        routes_t=routes.T,
        tok=tokens,
        cot=cotangent,
        segments=segments[None],
        freq=jnp.tile(frequency, 4)[None],
    )
    rows = (128, 1024)
    slots = (2, 2, CAP, 1024)
    wide = (2, 1024, 2 * CAP)
    front = call(
        front_kernel,
        "front",
        0,
        common
        | given(
            VM, w_gate=w_gate, w_up=w_up, w_down=w_down, w_query=w_query,
            w_keyval=key_value_weight, w_output_t=w_output.T, gates_t=gates.T,
            bias_gate=bias_gate, bias_up=bias_up, bias_down=bias_down,
        ),
        dict(
            weights=((3, 4, 2, 2, 8, 64, 128), BF16, ANY),
            full0=(FULL, BF16, ANY),
            full1=(FULL, BF16, ANY),
            full2=(FULL, BF16, ANY),
            unpick=(wide, BF16, ANY),
            mid=(rows, F32, VM),
            normed_all=((2, 4, 128, 1024), BF16, ANY),
            queries=(rows, BF16, VM),
            keyvals=((256, 1024), BF16, VM),
            attended=(rows, BF16, VM),
            logsum=((128, 128), F32, VM),
            rows=(slots, BF16, VM),
            cot_rows=(slots, BF16, VM),
            gate_rows=((2, 2, CAP, 128), F32, VM),
            place_t=((2, 2, 1024), F32, VM),
            bias=((2, 1, 2048), F32, VM),
        ),
        dict(
            pairs=bf16(3, 2, 64, 2048),
            shards=bf16(3, 64, 128),
            normed1=bf16(*rows),
            sorted=bf16(3, 8, 2, 64, 128),
            full0_v=bf16(*FULL),
            full1_v=bf16(*FULL),
            full2_v=bf16(*FULL),
            unpick_v=bf16(*wide),
            pick=bf16(2, 2 * CAP, 1024),
            slot_gate=f32(2, 2, CAP, 128),
            prev=bf16(*rows),
            normed2=bf16(*rows),
            row_all=bf16(2, 4, 128, 1024),
            cot_all=bf16(2, 4, 128, 1024),
            row_out=bf16(2, CAP, 1024),
            cot_out=bf16(2, CAP, 1024),
            send=DMA((99,)),
            recv=DMA((99,)),
            cot_send=DMA((9,)),
            cot_recv=DMA((9,)),
            row_send=DMA((9,)),
            row_recv=DMA((9,)),
            own=DMA((4,)),
            keep=DMA((3,)),
            store=DMA((4,)),
        ),
    )
    experts = expert_block(front)
    bufs = dict(
        back_bufs=row_reduce_scratch(), out_bufs=row_reduce_scratch(), wo_bufs=reduce_scratch(WO_ORDER)
    )
    flat = {}
    for name, items in bufs.items():
        flat |= {name + str(k): item for k, item in enumerate(items)}

    def kernel(r):
        for name, items in bufs.items():
            setattr(r, name, [getattr(r, name + str(k)) for k in range(len(items))])
        back_kernel(r)

    half = (2, 3, 2, 512, 128)
    back = call(
        kernel,
        "back",
        2,
        common
        | given(
            VM, place_t=front.place_t, mid=front.mid, queries=front.queries,
            keyvals=front.keyvals, attended=front.attended, logsum=front.logsum,
            grad_bias=experts.grad_bias,
        )
        | given(
            ANY, out_rows=experts.out_rows, back_rows=experts.back_rows, dots=experts.dots,
            grads=experts.grads, normed_all=experts.normed_all, unpick=front.unpick,
            full0=front.full0, full1=front.full1, full2=front.full2,
        ),
        dict(
            layer_out=(rows, F32, VM),
            grad_tokens=(rows, F32, VM),
            grad_gates=((8, 128), F32, VM),
            grad_qkv=((2, 64, 128), F32, VM),
            grad_o=((64, 128), F32, VM),
            grad_experts=((3, 64, 2048), F32, VM),
            totals=((16, 24, 128), F32, VM),
            biases=((16, 4, 1024), F32, VM),
        ),
        dict(
            unpick_v=bf16(*wide),
            back_own=bf16(2, CAP, 1024),
            back_got=bf16(2, CAP, 1024),
            out_got=bf16(2, CAP, 1024),
            dot_own=f32(2, CAP, 128),
            dot_got=f32(2, CAP, 128),
            back_parts=bf16(2, 4, 128, 1024),
            out_parts=bf16(2, 4, 128, 1024),
            token_dots=f32(8, 2, 2, 128),
            dots_all=f32(8, 2, 2, 128),
            z_own=bf16(*half),
            z_near=bf16(*half),
            z_far=bf16(*half),
            z_solo=bf16(*half),
            z_send=bf16(*half),
            z_got=bf16(*half),
            deal_out=bf16(3, 2, 2, 8, 64, 128),
            deal_got=bf16(3, 2, 8, 2, 64, 128),
            unsorted=bf16(3, 2, 64, 2048),
            unsorted_got=bf16(3, 64, 2048),
            full0_v=bf16(*FULL),
            full1_v=bf16(*FULL),
            full2_v=bf16(*FULL),
            normed_v=bf16(2, 4, 128, 1024),
            grad_wo=bf16(*FULL),
            dq=f32(*rows),
            dkv=f32(*rows),
            halo=bf16(*rows),
            halo_got=bf16(*rows),
            low=bf16(2, 128, 1024),
            low_all=bf16(2, 8, 128, 128),
            grad_w=bf16(2, 16, 64, 128),
            grad_w_got=bf16(2, 16, 64, 128),
            small=f32(24, 128),
            small_got=f32(7, 24, 128),
            small_all=f32(16, 24, 128),
            bias_sum=f32(4, 1024),
            bias_got=f32(7, 4, 1024),
            bias_all=f32(16, 4, 1024),
            send=DMA((166,)),
            recv=DMA((166,)),
            load=DMA((11,)),
        )
        | flat,
    )
    done = call(
        finish_kernel,
        "finish",
        None,
        given(
            VM, layer_in=back.layer_out, tokens_in=back.grad_tokens, qkv=back.grad_qkv,
            wo_in=back.grad_o, experts=back.grad_experts, gates_in=back.grad_gates,
            totals=back.totals, biases=back.biases,
        ),
        dict(
            layer_out=(rows, F32, VM),
            grad_tokens=(rows, F32, VM),
            w_query=((64, 128), F32, VM),
            w_keyval=((64, 128), F32, VM),
            w_output_t=((64, 128), F32, VM),
            w_gate=((64, 2048), F32, VM),
            w_up=((64, 2048), F32, VM),
            w_down=((64, 2048), F32, VM),
            gates_t=((8, 128), F32, VM),
            gain1=((1, 1024), F32, VM),
            gain2=((1, 1024), F32, VM),
            sinks=((1, 16), F32, VM),
            bias_gate=((32, 512), F32, VM),
            bias_up=((32, 512), F32, VM),
            bias_down=((32, 1024), F32, VM),
        ),
        {},
    )
    return (
        done.layer_out,
        done.grad_tokens,
        done.gain1[0],
        done.w_query,
        done.w_keyval,
        done.w_output_t.T,
        done.sinks[0],
        done.gain2[0],
        done.w_gate,
        done.w_up,
        done.w_down,
        done.bias_gate,
        done.bias_up,
        done.bias_down,
        done.gates_t.T,
    )


def solution(mesh):
    fine = Mesh(mesh.devices.reshape(2, 4, 2, 8), ("xh", "z", "core", "tp"))
    fsdp = ("xh", "z", "core")
    rows = P(("xh", "z", "core", "tp"), None)
    return jax.shard_map(
        local,
        mesh=fine,
        in_specs=(
            rows,
            P(),
            P(fsdp, "tp"),
            P(fsdp, "tp"),
            P("tp", fsdp),
            P(),
            P(),
            P(fsdp, "tp"),
            P(fsdp, "tp"),
            P(fsdp, "tp"),
            P(),
            P(),
            P(),
            P(fsdp, None),
            P(fsdp, None),
            P(fsdp),
            rows,
        ),
        out_specs=(
            rows,
            rows,
            P(),
            P(fsdp, "tp"),
            P(fsdp, "tp"),
            P("tp", fsdp),
            P(),
            P(),
            P(fsdp, "tp"),
            P(fsdp, "tp"),
            P(fsdp, "tp"),
            P(),
            P(),
            P(),
            rows,
        ),
        check_vma=False,
    )
```

```python
import itertools
import types

import jax
import jax.numpy as jnp
from jax import lax
from jax.experimental import pallas as pl
from jax.experimental.pallas import tpu as pltpu
from jax.sharding import Mesh
from jax.sharding import PartitionSpec as P

MESH = pl.DeviceIdType.MESH
HEAD_DIM = 64
WINDOW = 128
EPS = 1e-05
ROPE_BASE = 10000.0
CLAMP = 7.0
SLOPE = 1.702
SCALE = HEAD_DIM ** (-0.5)
NEG = -1e30
CAP = 272
F32 = jnp.float32
BF16 = jnp.bfloat16
ANY = pl.BlockSpec(memory_space=pl.ANY)
DMA = pltpu.SemaphoreType.DMA
VM = pl.BlockSpec(memory_space=pltpu.VMEM)
SM = pl.BlockSpec(memory_space=pltpu.SMEM)
VMEM_LIMIT = 58 * 1024 * 1024

SIZES = {"xh": 2, "z": 4, "c": 2, "xl": 2, "y": 4, "x": 4}


def coords():
    xh, z = lax.axis_index("xh"), lax.axis_index("z")
    c, t = lax.axis_index("core"), lax.axis_index("tp")
    xl, y = t // 4, t % 4
    return {"xh": xh, "z": z, "c": c, "xl": xl, "y": y, "x": 2 * xh + xl}


def moved(place, offset):
    out = dict(place)
    for axis, step in offset.items():
        out[axis] = (place[axis] + step) % SIZES[axis]
        if axis == "x":
            out["xh"], out["xl"] = out["x"] // 2, out["x"] % 2
    return out


def device(place):
    return (place["xh"], place["z"], place["c"], place["xl"] * 4 + place["y"])


def offsets(axes):
    ranges = [range(SIZES[a]) for a in axes]
    return [dict(zip(axes, o)) for o in itertools.product(*ranges) if any(o)]


def slot(place, axes):
    out = 0
    for a in axes:
        out = out * SIZES[a] + place[a]
    return out


def greet(peers):
    barrier = pltpu.get_barrier_semaphore()
    for peer in peers:
        pl.semaphore_signal(barrier, inc=1, device_id=device(peer), device_id_type=MESH)
    pl.semaphore_wait(barrier, len(peers))


def remote(src, dst, send, recv, peer):
    return pltpu.make_async_remote_copy(
        src_ref=src,
        dst_ref=dst,
        send_sem=send,
        recv_sem=recv,
        device_id=device(peer),
        device_id_type=MESH,
    )


def comm_params(ident):
    return pltpu.CompilerParams(
        collective_id=ident, has_side_effects=True, vmem_limit_bytes=VMEM_LIMIT
    )


def call(kernel, name, ident, ins, outs, scratch, **extra):
    names = list(ins) + list(outs) + list(scratch)

    def body(*refs):
        kernel(types.SimpleNamespace(**dict(zip(names, refs))))

    if ident is None:
        params = pltpu.CompilerParams(vmem_limit_bytes=VMEM_LIMIT)
    else:
        params = comm_params(ident)
    results = pl.pallas_call(
        body,
        out_shape=[jax.ShapeDtypeStruct(o[0], o[1]) for o in outs.values()],
        in_specs=[i[1] for i in ins.values()],
        out_specs=[o[2] for o in outs.values()],
        scratch_shapes=list(scratch.values()),
        compiler_params=params,
        name=name,
        **extra,
    )(*[i[0] for i in ins.values()])
    return types.SimpleNamespace(**dict(zip(outs, results)))


def given(spec, **arrays):
    return {name: (a, spec) for name, a in arrays.items()}


def f32(*shape):
    return pltpu.VMEM(shape, F32)


def bf16(*shape):
    return pltpu.VMEM(shape, BF16)


class Copies:
    def __init__(self, send, recv):
        self.send, self.recv, self.all = send, recv, []

    def go(self, src, dst, peer):
        k = len(self.all)
        copy = remote(src, dst, self.send.at[k], self.recv.at[k], peer)
        copy.start()
        self.all.append(copy)
        return copy

    def sent(self):
        for copy in self.all:
            copy.wait_send()


def arrived(copies):
    for copy in copies:
        copy.wait_recv()


def along(here, axis):
    return [moved(here, {axis: k}) for k in (1, 3, 2)]


def sequence_neighbours(here):
    rank = here["xl"] * 4 + here["y"]
    after, before = (rank + 1) % 8, (rank + 7) % 8
    return dict(here, xl=after // 4, y=after % 4), dict(here, xl=before // 4, y=before % 4)


def lanes_of(place):
    return pl.ds(pl.multiple_of(place["y"] * 128, 128), 128)


LEFT, RIGHT = pl.ds(0, 512), pl.ds(512, 512)


class RowGather:
    def __init__(self, here, src, out, send, recv):
        self.here, self.src, self.out = here, src, out
        self.net = Copies(send, recv)
        self.side, self.ups = moved(here, {"xl": 1}), along(here, "y")

    def first(self):
        xl, y = self.here["xl"], self.here["y"]
        go = self.net.go
        self.x = go(self.src.at[:, LEFT], self.out.at[xl, y, :, LEFT], self.side)
        self.y = [go(self.src.at[:, RIGHT], self.out.at[xl, y, :, RIGHT], p) for p in self.ups]

    def then(self):
        xl, y = self.here["xl"], self.here["y"]
        self.x.wait_recv()
        view = self.out.at[:, y, :, LEFT]
        self.beside = [self.net.go(view, view, p) for p in self.ups[:2]]
        arrived(self.y)
        view = self.out.at[xl, :, :, RIGHT]
        self.last = [self.net.go(view, view, self.side)]

    def relay(self):
        arrived(self.beside)
        up, down = self.ups[:2]
        view = self.out.at[0, down["y"], :, LEFT]
        self.last.append(self.net.go(view, view, up))
        view = self.out.at[1, up["y"], :, LEFT]
        self.last.append(self.net.go(view, view, down))

    def finish(self):
        arrived(self.last)
        self.net.sent()


class RowReduce:
    def __init__(self, here, parts, bufs, send, recv):
        self.here, self.parts = here, parts
        self.got_y, self.sum_y, self.got_x, self.sum_x, self.end_y, self.end_x = bufs
        self.net = Copies(send, recv)
        self.side, self.ups = moved(here, {"xl": 1}), along(here, "y")

    def right(self):
        self.x = self.net.go(self.parts.at[self.side["xl"], :, :, RIGHT], self.got_x, self.side)

    def left(self):
        self.y = [
            self.net.go(self.parts.at[:, p["y"], :, LEFT], self.got_y.at[k], p)
            for k, p in enumerate(self.ups)
        ]

    def then_right(self):
        self.x.wait_recv()
        mine = self.parts[self.here["xl"], :, :, RIGHT].astype(F32)
        self.sum_x[...] = (mine + self.got_x[...].astype(F32)).astype(BF16)
        self.last_x = [
            self.net.go(self.sum_x.at[p["y"]], self.end_x.at[k], p) for k, p in enumerate(self.ups)
        ]

    def then_left(self):
        arrived(self.y)
        total = self.parts[:, self.here["y"], :, LEFT].astype(F32)
        for k in range(3):
            total = total + self.got_y[k].astype(F32)
        self.sum_y[...] = total.astype(BF16)
        self.last_y = self.net.go(self.sum_y.at[self.side["xl"]], self.end_y, self.side)

    def result(self):
        self.last_y.wait_recv()
        left = self.sum_y[self.here["xl"]].astype(F32) + self.end_y[...].astype(F32)
        arrived(self.last_x)
        right = self.sum_x[self.here["y"]].astype(F32)
        for k in range(3):
            right = right + self.end_x[k].astype(F32)
        return jnp.concatenate([left, right], 1)


def row_reduce_scratch():
    return [
        bf16(3, 2, 128, 512),
        bf16(2, 128, 512),
        bf16(4, 128, 512),
        bf16(4, 128, 512),
        bf16(128, 512),
        bf16(3, 128, 512),
        DMA((8,)),
        DMA((8,)),
    ]


FULL = (2, 2, 4, 2, 64, 512)


def region(ref, place, held):
    xl = slice(None) if "x" in held else place["xl"]
    xh = slice(None) if "x" in held else place["xh"]
    z = slice(None) if "z" in held else place["z"]
    y = pl.ds(0, 512) if "y" in held else lanes_of(place)
    return ref.at[xl, xh, z, place["c"], :, y]


class Spread:
    def __init__(self, here, full, net):
        self.here, self.full, self.net = here, full, net

    def step(self, axis, held, src=None):
        view = region(self.full, self.here, held)
        src = view if src is None else src
        self.group = [self.net.go(src, view, p) for p in along(self.here, axis)]

    def step_beside(self, held):
        view = region(self.full, self.here, held)
        self.group = [self.net.go(view, view, p) for p in along(self.here, "y")[:2]]

    def relay(self):
        arrived(self.group)
        up, down = along(self.here, "y")[:2]
        c = self.here["c"]
        self.group = []
        for half, source, target in ((0, down, up), (1, up, down)):
            view = self.full.at[half, :, :, c, :, lanes_of(source)]
            self.group.append(self.net.go(view, view, target))

    def swap(self):
        view = self.full.at[:, :, :, self.here["c"]]
        self.group = [self.net.go(view, view, moved(self.here, {"c": 1}))]

    def wait(self):
        arrived(self.group)


def matrix(ref, half):
    return ref[half].reshape(1024, 512)


class Reduce:
    def __init__(self, here, parts, bufs, send, recv):
        self.here, self.parts = here, parts
        self.got_core, self.sum_core, self.got_z, self.sum_z, self.got_plane = bufs
        self.net = Copies(send, recv)
        self.other = moved(here, {"c": 1})

    def swap(self):
        view = self.parts.at[:, :, :, self.other["c"]]
        self.group = [self.net.go(view, self.got_core, self.other)]

    def along_z(self):
        arrived(self.group)
        mine = self.parts[:, :, :, self.here["c"]].astype(F32)
        self.sum_core[...] = (mine + self.got_core[...].astype(F32)).astype(BF16)
        self.group = [
            self.net.go(self.sum_core.at[:, :, p["z"]], self.got_z.at[k], p)
            for k, p in enumerate(along(self.here, "z"))
        ]

    def over_plane(self):
        arrived(self.group)
        total = self.sum_core[:, :, self.here["z"]].astype(F32)
        for k in range(3):
            total = total + self.got_z[k].astype(F32)
        self.sum_z[...] = total.astype(BF16)
        peers = [moved(self.here, o) for o in offsets(("x", "y"))]
        self.group = [
            self.net.go(self.sum_z.at[p["xl"], p["xh"], :, lanes_of(p)], self.got_plane.at[k], p)
            for k, p in enumerate(peers)
        ]

    def result(self):
        arrived(self.group)
        here = self.here
        total = self.sum_z[here["xl"], here["xh"], :, lanes_of(here)].astype(F32)
        for k in range(15):
            total = total + self.got_plane[k].astype(F32)
        return total


def reduce_scratch():
    return [
        bf16(2, 2, 4, 64, 512),
        bf16(2, 2, 4, 64, 512),
        bf16(3, 2, 2, 64, 512),
        bf16(2, 2, 64, 512),
        bf16(15, 64, 128),
        DMA((19,)),
        DMA((19,)),
    ]


def nn(a, b):
    return lax.dot_general(a, b, (((1,), (0,)), ((), ())), preferred_element_type=F32)


def nt(a, b):
    return lax.dot_general(a, b, (((1,), (1,)), ((), ())), preferred_element_type=F32)


def tn(a, b):
    return lax.dot_general(a, b, (((0,), (0,)), ((), ())), preferred_element_type=F32)


def one_hot_columns(start, core):
    row = lax.broadcasted_iota(jnp.int32, (1024, 1), 0)
    column = lax.broadcasted_iota(jnp.int32, (1024, 1024), 1)
    expert = 4 * (row // 128) + 2 * core + (row // 64) % 2
    return (column == (row % 64) * 32 + expert - start).astype(F32).astype(BF16)


def rope_partner(values):
    lanes = values.shape[1]
    lane = lax.broadcasted_iota(jnp.int32, values.shape, 1)
    return jnp.where(
        lane % 64 < 32, pltpu.roll(values, lanes - 32, 1), pltpu.roll(values, 32, 1)
    )


def tiled(table):
    return jnp.concatenate([table] * 8, axis=1)


def head_pair(block):
    lane = lax.broadcasted_iota(jnp.int32, block.shape, 1) < 64
    wide = block.astype(F32)
    swapped = pltpu.roll(wide, 64, 1)
    zero = jnp.zeros_like(wide)
    keys = jnp.concatenate([jnp.where(lane, wide, zero), jnp.where(lane, zero, swapped)], 0)
    values = jnp.concatenate([jnp.where(lane, swapped, zero), jnp.where(lane, zero, wide)], 0)
    return keys.astype(BF16), values.astype(BF16)


def window_mask(segq, segk):
    row = lax.broadcasted_iota(jnp.int32, (128, 256), 0)
    column = lax.broadcasted_iota(jnp.int32, (128, 256), 1)
    distance = 128 + row - column
    return (segq == segk) & (distance >= 0) & (distance < WINDOW)


def rope_at(start, rows, freq):
    row = lax.broadcasted_iota(jnp.int32, (rows, 128), 0)
    lane = lax.broadcasted_iota(jnp.int32, (rows, 128), 1)
    angles = (row + start).astype(F32) * freq
    cosine, sine = jnp.cos(angles), jnp.sin(angles)
    return cosine, jnp.where(lane % 64 < 32, -sine, sine), lane < 64


def rope_queries(rank, freq):
    cosine, sine, _ = rope_at(128 * rank, 128, freq)
    return tiled(cosine), tiled(sine)


def rope_keyvals(start, rows, freq):
    cosine, sine, keys = rope_at(start, rows, freq)
    return tiled(jnp.where(keys, cosine, 1.0)), tiled(jnp.where(keys, sine, 0.0))


def mask_at(segments, rank):
    own = segments[:, pl.ds(pl.multiple_of(128 * rank, 128), 128)]
    prev = segments[:, pl.ds(pl.multiple_of(128 * ((rank + 7) % 8), 128), 128)]
    prev = jnp.where(rank == 0, -1, prev)
    row = lax.broadcasted_iota(jnp.int32, (128, 128), 0)
    column = lax.broadcasted_iota(jnp.int32, (128, 128), 1)
    segq = jnp.sum(jnp.where(row == column, own.astype(F32), 0.0), 1, keepdims=True)
    return window_mask(segq, jnp.concatenate([prev, own], 1).astype(F32))


def slot_tables(r, rank):
    row = lax.broadcasted_iota(jnp.int32, (1024, 1024), 0)
    column = lax.broadcasted_iota(jnp.int32, (1024, 1024), 1)
    before = (row < column).astype(F32).astype(BF16)
    routes_t, gates_t = r.routes_t[...], r.gates_t[...]
    hits, shares = [], []
    for el in range(4):
        named = routes_t == 4 * rank + el
        hits.append(jnp.sum(named.astype(F32), 0, keepdims=True))
        shares.append(jnp.sum(jnp.where(named, gates_t, 0.0), 0, keepdims=True))
    earlier = nn(jnp.concatenate(hits + [jnp.zeros((12, 1024), F32)], 0).astype(BF16), before)
    places = [jnp.where(hits[el] > 0, earlier[el : el + 1], -1.0) for el in range(4)]
    columns = jnp.concatenate(places + [jnp.zeros((124, 1024), F32)], 0).T
    slot = lax.broadcasted_iota(jnp.int32, (CAP, 1024), 0).astype(F32)
    wide = lax.broadcasted_iota(jnp.int32, (1024, 2 * CAP), 1).astype(F32)
    for c in range(2):
        for e in range(2):
            el = 2 * c + e
            r.place_t[c, e : e + 1] = places[el]
            hot = slot == places[el]
            r.pick[c, CAP * e : CAP * e + CAP] = hot.astype(F32).astype(BF16)
            share = jnp.sum(jnp.where(hot, shares[el], 0.0), 1, keepdims=True)
            r.slot_gate[c, e] = jnp.broadcast_to(share, (CAP, 128))
        low = (wide == columns[:, 2 * c : 2 * c + 1]) & (wide < CAP)
        high = (wide - CAP == columns[:, 2 * c + 1 : 2 * c + 2]) & (wide >= CAP)
        r.unpick_v[c] = (low | high).astype(F32).astype(BF16)


DEAL_AXES = ("xh", "xl", "y")


def front_kernel(r):
    here = coords()
    c, xh, z, xl, y = (here[a] for a in ("c", "xh", "z", "xl", "y"))
    rank = xl * 4 + y
    other = moved(here, {"c": 1})
    after, before = sequence_neighbours(here)
    dealt = [moved(here, o) for o in offsets(DEAL_AXES)]
    up, down = moved(here, {"z": 1}), moved(here, {"z": 3})
    parts = (r.w_gate, r.w_up, r.w_down)
    fulls = (r.full0_v, r.full1_v, r.full2_v)
    for w, ref in enumerate(parts):
        r.pairs[w, c] = ref[...]
    for p, ref in enumerate((r.w_query, r.w_keyval, r.w_output_t)):
        r.shards[p] = ref[...]
    own = [
        pltpu.make_async_copy(r.shards.at[p], region(fulls[p], here, ""), r.own.at[p])
        for p in range(3)
    ]
    for copy in own:
        copy.start()
    greet([other, after, before] + [p for a in "xyz" for p in along(here, a)] + dealt)
    net = Copies(r.send, r.recv)
    swaps = [net.go(ref, r.pairs.at[w, c], other) for w, ref in enumerate(parts)]
    q_full, kv_full, o_full = (Spread(here, full, net) for full in fulls)
    kv_full.step("y", "", r.shards.at[1])
    q_full.step("z", "", r.shards.at[0])
    o_full.step("z", "", r.shards.at[2])
    cots = RowGather(here, r.cot, r.cot_all, r.cot_send, r.cot_recv)
    first = 4 * rank + 2 * c
    for e in range(2):
        r.bias[e, :, :512] = r.bias_gate[pl.ds(first + e, 1)]
        r.bias[e, :, 512:1024] = r.bias_up[pl.ds(first + e, 1)]
        r.bias[e, :, 1024:] = r.bias_down[pl.ds(first + e, 1)]
    r.cot_all[xl, y] = r.cot[...]
    hot_left = one_hot_columns(0, c)
    for copy in own:
        copy.wait()
    kv_full.wait()
    kv_full.step("x", "y")
    q_full.wait()
    q_full.step("y", "z")
    o_full.wait()
    o_full.step("x", "z")
    halo = net.go(r.tok, r.prev, after)
    hot = jnp.concatenate([hot_left, one_hot_columns(1024, c)], 1)
    deals, keeps = [], []

    def sort(w):
        arrived([swaps[w]])
        rows = r.pairs[w].reshape(128, 2048)
        r.sorted[w] = nt(hot, rows).astype(BF16).reshape(8, 2, 64, 128)
        mine = r.weights.at[w, z, xh, :, rank]
        keeps.append(pltpu.make_async_copy(r.sorted.at[w, rank], mine, r.keep.at[w]))
        keeps[w].start()

    def deal(w):
        mine = r.weights.at[w, z, xh, :, rank]
        deals.append([net.go(r.sorted.at[w, p["xl"] * 4 + p["y"]], mine, p) for p in dealt])

    ring, last_ring = [], []

    def send_on(w):
        arrived(deals[w])
        keeps[w].wait()
        view = r.weights.at[w, z]
        ring.append([net.go(view, view, up), net.go(view, view, down)])

    def pass_on(w):
        arrived(ring[w])
        view = r.weights.at[w, down["z"], 0]
        last_ring.append(net.go(view, view, up))
        view = r.weights.at[w, up["z"], 1]
        last_ring.append(net.go(view, view, down))

    sort(0)
    deal(0)
    kv_full.wait()
    kv_full.step("z", "yx")
    q_full.wait()
    q_full.step("x", "zy")
    o_full.wait()
    o_full.step_beside("zx")
    sort(1)
    sort(2)
    slot_tables(r, rank)
    stores = [pltpu.make_async_copy(r.unpick_v, r.unpick, r.store.at[0])]
    stores[0].start()

    def save(k, full, result):
        stores.append(pltpu.make_async_copy(full, result, r.store.at[k]))
        stores[k].start()

    send_on(0)
    deal(1)
    o_full.relay()
    kv_full.wait()
    kv_full.swap()
    halo.wait_recv()
    tok = r.tok[...].astype(F32)
    both = jnp.concatenate([r.prev[...].astype(F32), tok], 0)
    scale = lax.rsqrt(jnp.mean(both * both, -1, keepdims=True) + EPS)
    normed = (both * scale * r.gain1[...]).astype(BF16)
    normed_own = normed[128:]
    r.normed1[...] = normed_own
    keep_normed = pltpu.make_async_copy(r.normed1, r.normed_all.at[xl, y], r.own.at[3])
    keep_normed.start()
    q_full.wait()
    q_full.swap()
    kv_full.wait()
    deal(2)
    cots.first()
    save(1, r.full1_v, r.full1)
    kv = jnp.concatenate([nn(normed, matrix(r.full1_v, 0)), nn(normed, matrix(r.full1_v, 1))], 1)
    cosine, sine = rope_keyvals(128 * rank - 128, 256, r.freq[...])
    kv = (kv * cosine + rope_partner(kv) * sine).astype(BF16)
    r.keyvals[...] = kv
    o_full.wait()
    o_full.swap()
    pass_on(0)
    gates = net.go(r.slot_gate.at[other["c"]], r.gate_rows.at[c], other)
    r.gate_rows[c] = r.slot_gate[c]
    mask = mask_at(r.segments, rank)
    lane = lax.broadcasted_iota(jnp.int32, (128, 128), 1)
    q_full.wait()
    save(2, r.full0_v, r.full0)
    q = jnp.concatenate(
        [nn(normed_own, matrix(r.full0_v, 0)), nn(normed_own, matrix(r.full0_v, 1))], 1
    )
    cosine, sine = rope_queries(rank, r.freq[...])
    q = (q * cosine + rope_partner(q) * sine).astype(BF16)
    r.queries[...] = q
    send_on(1)
    sums = jnp.zeros((128, 128), F32)
    for g in range(8):
        part = slice(128 * g, 128 * g + 128)
        keys, values = head_pair(kv[:, part])
        scores = nt(q[:, part], keys) * SCALE
        shares = []
        for h in range(2):
            masked = jnp.where(mask, scores[:, 256 * h : 256 * h + 256], NEG)
            sink = r.sinks[2 * g + h]
            peak = jnp.maximum(jnp.max(masked, -1, keepdims=True), sink)
            total = jnp.exp(sink - peak) + jnp.sum(jnp.exp(masked - peak), -1, keepdims=True)
            log_total = peak + jnp.log(total)
            shares.append(jnp.exp(masked - log_total).astype(BF16))
            sums = jnp.where(lane == 2 * g + h, log_total, sums)
        r.attended[:, part] = nn(jnp.concatenate(shares, 1), values).astype(BF16)
        if g == 4:
            send_on(2)
    r.logsum[...] = sums
    cots.then()
    o_full.wait()
    save(3, r.full2_v, r.full2)
    out = (
        tok
        + nt(r.attended[:, :512], matrix(r.full2_v, 0))
        + nt(r.attended[:, 512:], matrix(r.full2_v, 1))
    )
    r.mid[...] = out
    scale = lax.rsqrt(jnp.mean(out * out, -1, keepdims=True) + EPS)
    r.normed2[...] = (out * scale * r.gain2[...]).astype(BF16)

    rows = RowGather(here, r.normed2, r.row_all, r.row_send, r.row_recv)
    rows.first()
    r.row_all[xl, y] = r.normed2[...]
    cots.relay()

    def to_slots(gathered, outgoing, result):
        tokens = gathered[...].reshape(1024, 1024)
        outgoing[...] = nn(r.pick[other["c"]], tokens).astype(BF16).reshape(2, CAP, 1024)
        copy = net.go(outgoing, result.at[c], other)
        result[c] = nn(r.pick[c], tokens).astype(BF16).reshape(2, CAP, 1024)
        return copy

    rows.then()
    pass_on(1)
    cots.finish()
    cot_copy = to_slots(r.cot_all, r.cot_out, r.cot_rows)
    rows.relay()
    pass_on(2)
    rows.finish()
    near = [
        net.go(r.normed1.at[:, LEFT], r.normed_all.at[xl, y, :, LEFT], moved(here, {"xl": 1}))
    ]
    view = r.normed_all.at[xl, y, :, RIGHT]
    near += [net.go(r.normed1.at[:, RIGHT], view, p) for p in along(here, "y")]
    row_copy = to_slots(r.row_all, r.row_out, r.rows)
    arrived([gates, cot_copy, row_copy])
    arrived(near)
    arrived(last_ring)
    for copy in stores:
        copy.wait()
    keep_normed.wait()
    net.sent()


def expert_kernel(r):
    turn = pl.program_id(0)
    here = coords()
    xl, y = here["xl"], here["y"]
    side, ups = moved(here, {"xl": 1}), along(here, "y")
    out = r.normed_all
    column, line = out.at[:, y, :, LEFT], out.at[xl, :, :, RIGHT]
    then = [
        remote(column, column, r.send.at[k], r.recv.at[k], p) for k, p in enumerate(ups)
    ]
    then.append(remote(line, line, r.send.at[3], r.recv.at[3], side))

    @pl.when(turn == 0)
    def _():
        greet([side] + ups)
        for item in then:
            item.start()

    def stacked(w):
        return jnp.concatenate(
            [r.weights[w, m % 4, m // 4, 0].reshape(512, 128) for m in range(8)], 1
        )

    w_gate, w_up, w_down = stacked(0), stacked(1), stacked(2)
    bias = r.bias[0]
    x = r.rows[:, 0].reshape(2 * CAP, 1024)
    tanh_gate = jnp.tanh((nt(x, w_gate) + bias[:, :512]) / CLAMP)
    tanh_up = jnp.tanh((nt(x, w_up) + bias[:, 512:1024]) / CLAMP)
    soft_gate, soft_up = CLAMP * tanh_gate, CLAMP * tanh_up
    sig = jax.nn.sigmoid(SLOPE * soft_gate)
    glu = soft_gate * sig
    hidden = (glu * (soft_up + 1.0)).astype(BF16)
    produced = nn(hidden, w_down) + bias[:, 1024:]
    share = r.gate_rows[:, 0].reshape(2 * CAP, 128)[:, :1]
    cot = r.cot_rows[:, 0].reshape(2 * CAP, 1024).astype(F32)
    r.out_rows[:, 0] = (share * produced).astype(BF16).reshape(2, CAP, 1024)

    products = produced * cot
    partial = products[:, :128]
    for m in range(1, 8):
        partial = partial + products[:, 128 * m : 128 * m + 128]
    r.dots[:, 0] = partial.reshape(2, CAP, 128)
    scaled = share * cot
    r.grad_bias[0, :, 1024:] = jnp.sum(scaled, 0, keepdims=True)
    rows_grad = scaled.astype(BF16)
    hidden_grad = nt(rows_grad, w_down)
    gate_grad = (
        hidden_grad
        * (soft_up + 1.0)
        * (sig + SLOPE * glu * (1.0 - sig))
        * (1.0 - tanh_gate * tanh_gate)
    )
    up_grad = hidden_grad * glu * (1.0 - tanh_up * tanh_up)
    r.grad_bias[0, :, :512] = jnp.sum(gate_grad, 0, keepdims=True)
    r.grad_bias[0, :, 512:1024] = jnp.sum(up_grad, 0, keepdims=True)
    gate_low, up_low = gate_grad.astype(BF16), up_grad.astype(BF16)
    back = (nn(gate_low, w_gate) + nn(up_low, w_up)).astype(BF16)
    r.back_rows[:, 0] = back.reshape(2, CAP, 1024)
    for w, (left, right) in enumerate(((gate_low, x), (up_low, x), (hidden, rows_grad))):
        grad = tn(left, right).astype(BF16)
        for m in range(8):
            r.grads[m % 4, m // 4, w, 0] = grad[:, 128 * m : 128 * m + 128]

    @pl.when(turn == 1)
    def _():
        for item in then:
            item.wait()


def expert_block(front):
    def at(dim, *shape):
        return pl.BlockSpec(
            shape[:dim] + (1,) + shape[dim:],
            lambda e: (0,) * dim + (e,) + (0,) * (len(shape) - dim),
        )

    per_row, per_slot = at(1, 2, CAP, 1024), at(1, 2, CAP, 128)
    stacked, vector = at(3, 4, 2, 3, 512, 128), at(0, 1, 2048)
    return call(
        expert_kernel,
        "experts",
        1,
        dict(
            rows=(front.rows, per_row),
            cot_rows=(front.cot_rows, per_row),
            gate_rows=(front.gate_rows, per_slot),
            weights=(front.weights, at(3, 3, 4, 2, 8, 64, 128)),
            bias=(front.bias, vector),
            normed_near=(front.normed_all, ANY),
        ),
        dict(
            out_rows=((2, 2, CAP, 1024), BF16, per_row),
            back_rows=((2, 2, CAP, 1024), BF16, per_row),
            dots=((2, 2, CAP, 128), F32, per_slot),
            grads=((4, 2, 3, 2, 512, 128), BF16, stacked),
            grad_bias=((2, 1, 2048), F32, vector),
            normed_all=((2, 4, 128, 1024), BF16, ANY),
        ),
        dict(send=DMA((4,)), recv=DMA((4,))),
        grid=(2,),
        input_output_aliases={5: 5},
    )


def norm_back(values, gain, grad):
    scale = lax.rsqrt(jnp.mean(values * values, -1, keepdims=True) + EPS)
    normed = values * scale
    weighted = gain * grad
    back = scale * (weighted - normed * jnp.mean(weighted * normed, -1, keepdims=True))
    return back, jnp.sum(grad * normed, 0, keepdims=True)


class ZSum:
    def __init__(self, r, here, net):
        self.r, self.net, self.z = r, net, here["z"]
        self.up, self.down = moved(here, {"z": 1}), moved(here, {"z": 3})
        far = (self.z + 2) % 4
        self.solo, self.both = [None] * 3, [None] * 3
        self.far = [
            [
                net.go(r.grads.at[far, 0, w], r.z_far.at[0, w], self.up),
                net.go(r.grads.at[far, 1, w], r.z_far.at[1, w], self.down),
            ]
            for w in range(3)
        ]

    def alone(self, w):
        r, up, down = self.r, self.up, self.down
        self.solo[w] = [
            self.net.go(r.grads.at[up["z"], 1, w], r.z_solo.at[1, w], up),
            self.net.go(r.grads.at[down["z"], 0, w], r.z_solo.at[0, w], down),
        ]

    def add(self, w):
        r = self.r
        arrived(self.far[w])
        for half in range(2):
            r.z_send[half, w] = (
                r.z_near[half, w].astype(F32) + r.z_far[half, w].astype(F32)
            ).astype(BF16)
        self.both[w] = [
            self.net.go(r.z_send.at[0, w], r.z_got.at[0, w], self.up),
            self.net.go(r.z_send.at[1, w], r.z_got.at[1, w], self.down),
        ]

    def total(self, w, half):
        r = self.r
        return (
            r.z_own[half, w].astype(F32)
            + r.z_got[half, w].astype(F32)
            + r.z_solo[half, w].astype(F32)
        ).astype(BF16)

    def wait(self, w):
        arrived(self.solo[w] + self.both[w])


def back_kernel(r):
    here = coords()
    c, xh, z, xl, y = (here[a] for a in ("c", "xh", "z", "xl", "y"))
    rank = xl * 4 + y
    other = moved(here, {"c": 1})
    after, before = sequence_neighbours(here)
    everyone = [moved(here, o) for o in offsets(("xl", "y"))]
    dealt = [moved(here, o) for o in offsets(DEAL_AXES)]
    owners = [moved(here, o) for o in offsets(("xh", "z", "c"))]
    planes = [moved(here, o) for o in offsets(("xh", "z"))]
    places = [moved(here, o) for o in offsets(("c", "xl", "y"))]
    loads = []

    def load(src, dst):
        copy = pltpu.make_async_copy(src, dst, r.load.at[len(loads)])
        copy.start()
        loads.append(copy)
        return copy

    get_unpick = load(r.unpick, r.unpick_v)
    get_back = load(r.back_rows.at[c], r.back_own)
    get_dots = load(r.dots.at[c], r.dot_own)
    get_near = [
        load(r.grads.at[(z + 1) % 4, 0], r.z_near.at[0]),
        load(r.grads.at[(z + 3) % 4, 1], r.z_near.at[1]),
    ]
    get_full2 = load(r.full2, r.full2_v)
    get_z = load(r.grads.at[z], r.z_own)
    get_full0 = load(r.full0, r.full0_v)
    get_full1 = load(r.full1, r.full1_v)
    get_normed = load(r.normed_all, r.normed_v)
    greet(
        [other, after, before]
        + [p for a in "xyz" for p in along(here, a)]
        + everyone + dealt + owners + planes + places
    )
    net = Copies(r.send, r.recv)
    back_swap = net.go(r.back_rows.at[other["c"]], r.back_got, other)
    for e in range(2):
        r.bias_sum[2 * e : 2 * e + 1] = r.grad_bias[e, :, :1024]
        r.bias_sum[2 * e + 1 : 2 * e + 2] = r.grad_bias[e, :, 1024:]
    biases = [net.go(r.bias_sum, r.bias_got.at[k], p) for k, p in enumerate(planes)]
    zsum = ZSum(r, here, net)

    def to_tokens(own, got, parts, columns):
        mine = nn(r.unpick_v[c], own[:, :, columns].reshape(2 * CAP, 512))
        theirs = nn(r.unpick_v[other["c"]], got[:, :, columns].reshape(2 * CAP, 512))
        parts[:, :, :, columns] = (mine + theirs).astype(BF16).reshape(2, 4, 128, 512)

    back = RowReduce(here, r.back_parts, r.back_bufs[:6], *r.back_bufs[6:])
    out = RowReduce(here, r.out_parts, r.out_bufs[:6], *r.out_bufs[6:])
    get_unpick.wait()
    get_back.wait()
    back_swap.wait_recv()
    dot_swap = net.go(r.dots.at[other["c"]], r.dot_got, other)
    out_swap = net.go(r.out_rows.at[other["c"]], r.out_got, other)
    to_tokens(r.back_own, r.back_got, r.back_parts, RIGHT)
    back.right()
    to_tokens(r.back_own, r.back_got, r.back_parts, LEFT)
    back.left()
    get_out = load(r.out_rows.at[c], r.back_own)

    get_dots.wait()
    dot_swap.wait_recv()
    slot = lax.broadcasted_iota(jnp.int32, (CAP, 1024), 0).astype(F32)
    for source, core in ((r.dot_own, c), (r.dot_got, other["c"])):
        for e in range(2):
            totals = jnp.sum(source[e], 1, keepdims=True)
            hot = slot == r.place_t[core, e : e + 1]
            line = jnp.sum(jnp.where(hot, totals, 0.0), 0, keepdims=True)
            for j in range(8):
                r.token_dots[j, core, e : e + 1] = line[:, 128 * j : 128 * j + 128]
    r.dots_all[rank] = r.token_dots[rank]
    dot_copies = [
        net.go(r.token_dots.at[p["xl"] * 4 + p["y"]], r.dots_all.at[rank], p) for p in everyone
    ]
    for copy in get_near:
        copy.wait()
    zsum.add(0)
    zsum.alone(0)
    get_out.wait()
    out_swap.wait_recv()
    to_tokens(r.back_own, r.out_got, r.out_parts, RIGHT)
    to_tokens(r.back_own, r.out_got, r.out_parts, LEFT)
    back.then_right()
    back.then_left()
    out.right()
    out.left()
    for w in (1, 2):
        zsum.add(w)
        zsum.alone(w)
    spot = c * 8 + rank
    arrived(biases)
    total = r.bias_sum[...]
    for k in range(7):
        total = total + r.bias_got[k]
    r.bias_all[spot] = total
    biases = [net.go(r.bias_all.at[spot], r.bias_all.at[spot], p) for p in places]
    moved_in = back.result()

    step, gain_part = norm_back(r.mid[...], r.gain2[...], moved_in)
    for k in range(8):
        r.small[8 + k : 9 + k] = gain_part[:, 128 * k : 128 * k + 128]
    mid_grad = r.cot[...].astype(F32) + step
    low = mid_grad.astype(BF16)
    for half in range(2):
        columns = slice(512 * half, 512 * half + 512)
        r.grad_wo[half] = tn(low, r.attended[:, columns]).astype(BF16).reshape(FULL[1:])
    wo = Reduce(here, r.grad_wo, r.wo_bufs[:5], *r.wo_bufs[5:])
    wo.swap()
    get_full2.wait()
    out_grad = jnp.concatenate([nn(low, matrix(r.full2_v, 0)), nn(low, matrix(r.full2_v, 1))], 1)
    out_grad = out_grad.astype(BF16)
    mask = mask_at(r.segments, rank)
    lane_row = lax.broadcasted_iota(jnp.int32, (1, 128), 1)
    lane = lax.broadcasted_iota(jnp.int32, (256, 128), 1) < 64
    sink_grads = jnp.zeros((1, 128), F32)
    halos = []
    for g in range(8):
        part = slice(128 * g, 128 * g + 128)
        keys, values = head_pair(r.keyvals[:, part])
        q = r.queries[:, part]
        grad_block = out_grad[:, part]
        scores = nt(q, keys) * SCALE
        share_grads = nt(grad_block, values)
        shares, score_grads = [], []
        for h in range(2):
            columns = slice(256 * h, 256 * h + 256)
            log_total = r.logsum[:, 2 * g + h : 2 * g + h + 1]
            share = jnp.exp(jnp.where(mask, scores[:, columns], NEG) - log_total)
            term = jnp.sum(share * share_grads[:, columns], -1, keepdims=True)
            shares.append(share.astype(BF16))
            score_grads.append((share * (share_grads[:, columns] - term)).astype(BF16))
            sink_part = -jnp.sum(jnp.exp(r.sinks[2 * g + h] - log_total) * term, 0, keepdims=True)
            sink_grads = jnp.where(lane_row == 2 * g + h, sink_part, sink_grads)
        shares = jnp.concatenate(shares, 1)
        score_grads = jnp.concatenate(score_grads, 1)
        r.dq[:, part] = nn(score_grads, keys) * SCALE
        from_scores = tn(score_grads, q) * SCALE
        from_shares = tn(shares, grad_block)
        joined = jnp.where(
            lane,
            from_scores[:256] + pltpu.roll(from_scores[256:], 64, 1),
            pltpu.roll(from_shares[:256], 64, 1) + from_shares[256:],
        )
        r.halo[:, part] = joined[:128].astype(BF16)
        r.dkv[:, part] = joined[128:]
        if g == 3:
            wo.along_z()
        if g % 4 == 3:
            view = slice(512 * (g // 4), 512 * (g // 4) + 512)
            halos.append(net.go(r.halo.at[:, view], r.halo_got.at[:, view], before))

    get_z.wait()
    deals = []

    def deal(w):
        zsum.wait(w)
        for half in range(2):
            r.deal_out[w, half] = zsum.total(w, half).reshape(2, 8, 64, 128)
        r.deal_got[w, xh, rank] = r.deal_out[w, xh, :, rank]
        deals.append(
            [
                net.go(
                    r.deal_out.at[w, p["xh"], :, p["xl"] * 4 + p["y"]], r.deal_got.at[w, xh, rank], p
                )
                for p in dealt
            ]
        )

    def to_columns(low, k):
        r.low[k] = low
        r.low_all[k, rank] = r.low[k, :, lanes_at(rank)]
        return [net.go(r.low.at[k, :, lanes_at(p["xl"] * 4 + p["y"])], r.low_all.at[k, rank], p) for p in everyone]

    grad_q = r.dq[...]
    cosine, sine = rope_queries(rank, r.freq[...])
    low = (grad_q * cosine - rope_partner(grad_q) * sine).astype(BF16)
    q_copies = to_columns(low, 0)
    get_full0.wait()
    first_back = nt(low[:, :512], matrix(r.full0_v, 0)) + nt(low[:, 512:], matrix(r.full0_v, 1))

    hot = one_hot_columns(0, c)
    r.full2_v[0] = hot[:, :512].reshape(FULL[1:])
    r.full2_v[1] = hot[:, 512:].reshape(FULL[1:])
    hot = one_hot_columns(1024, c)
    r.full0_v[0] = hot[:, :512].reshape(FULL[1:])
    r.full0_v[1] = hot[:, 512:].reshape(FULL[1:])
    arrived(halos)
    grad_kv = r.dkv[...] + r.halo_got[...].astype(F32)
    cosine, sine = rope_keyvals(128 * rank, 128, r.freq[...])
    low = (grad_kv * cosine - rope_partner(grad_kv) * sine).astype(BF16)
    kv_copies = to_columns(low, 1)
    deal(0)
    get_full1.wait()
    first_back = (
        first_back + nt(low[:, :512], matrix(r.full1_v, 0)) + nt(low[:, 512:], matrix(r.full1_v, 1))
    )
    norm_grad, gain_part = norm_back(r.tok[...].astype(F32), r.gain1[...], first_back)
    r.grad_tokens[...] = mid_grad + norm_grad
    for k in range(8):
        r.small[k : k + 1] = gain_part[:, 128 * k : 128 * k + 128]
    r.small[16:24] = jnp.concatenate([sink_grads, jnp.zeros((7, 128), F32)], 0)
    small = [net.go(r.small, r.small_got.at[k], p) for k, p in enumerate(planes)]

    get_normed.wait()
    normed = r.normed_v[...].reshape(1024, 1024)
    mine = (xh * 4 + z) * 2 + c
    sums = []

    def product(k, copies):
        arrived(copies)
        block = tn(normed, r.low_all[k].reshape(1024, 128))
        r.grad_w[k] = block.astype(BF16).reshape(16, 64, 128)
        r.grad_w_got[k, mine] = r.grad_w[k, mine]
        sums.append(
            [
                net.go(
                    r.grad_w.at[k, (p["xh"] * 4 + p["z"]) * 2 + p["c"]], r.grad_w_got.at[k, mine], p
                )
                for p in owners
            ]
        )

    deal(1)
    product(0, q_copies)
    product(1, kv_copies)
    deal(2)
    out.then_right()
    out.then_left()
    unsorted = []

    def unsort(w):
        arrived(deals[w])
        summed = r.deal_got[w, 0].astype(F32) + r.deal_got[w, 1].astype(F32)
        lines = summed.reshape(1024, 128).T.astype(BF16)
        for k in range(4):
            wide = nn(lines, matrix(r.full2_v if k < 2 else r.full0_v, k % 2)).astype(BF16)
            r.unsorted[w, :, :, 512 * k : 512 * k + 512] = wide.reshape(2, 64, 512)
        unsorted.append(net.go(r.unsorted.at[w, other["c"]], r.unsorted_got.at[w], other))

    unsort(0)
    wo.over_plane()
    unsort(1)
    arrived(small)
    total = r.small[...]
    for k in range(7):
        total = total + r.small_got[k]
    r.small_all[spot] = total
    small = [net.go(r.small_all.at[spot], r.small_all.at[spot], p) for p in places]
    r.layer_out[...] = r.mid[...] + out.result()
    arrived(dot_copies)
    own_routes = r.routes_t[:, lanes_at(rank)]
    chosen = jnp.zeros((8, 128), F32)
    for j in range(8):
        for core in range(2):
            for e in range(2):
                line = r.dots_all[j, core, e : e + 1]
                chosen = jnp.where(own_routes == 4 * j + 2 * core + e, line, chosen)
    r.grad_gates[...] = chosen
    unsort(2)
    for k, copies in enumerate(sums):
        arrived(copies)
        total = r.grad_w_got[k, 0].astype(F32)
        for m in range(1, 16):
            total = total + r.grad_w_got[k, m].astype(F32)
        r.grad_qkv[k] = total
    r.grad_o[...] = wo.result()
    arrived(small)
    arrived(biases)
    for w in range(3):
        arrived([unsorted[w]])
        r.grad_experts[w] = r.unsorted[w, c].astype(F32) + r.unsorted_got[w].astype(F32)
    r.totals[...] = r.small_all[...]
    r.biases[...] = r.bias_all[...]
    for sent in (net, back.net, out.net, wo.net):
        sent.sent()


def lanes_at(rank):
    return pl.ds(pl.multiple_of(rank * 128, 128), 128)


def finish_kernel(r):
    r.layer_out[...] = r.layer_in[...]
    r.grad_tokens[...] = r.tokens_in[...]
    r.w_query[...] = r.qkv[0]
    r.w_keyval[...] = r.qkv[1]
    r.w_output_t[...] = r.wo_in[...]
    r.w_gate[...] = r.experts[0]
    r.w_up[...] = r.experts[1]
    r.w_down[...] = r.experts[2]
    r.gates_t[...] = r.gates_in[...]
    total = r.totals[0]
    for k in range(1, 16):
        total = total + r.totals[k]
    for k in range(8):
        r.gain1[:, 128 * k : 128 * k + 128] = total[k : k + 1]
        r.gain2[:, 128 * k : 128 * k + 128] = total[8 + k : 9 + k]
    r.sinks[...] = total[16:17, :16]
    for core in range(2):
        for j in range(8):
            for e in range(2):
                at = slice(4 * j + 2 * core + e, 4 * j + 2 * core + e + 1)
                row = r.biases[core * 8 + j, 2 * e : 2 * e + 2]
                r.bias_gate[at] = row[0:1, :512]
                r.bias_up[at] = row[0:1, 512:]
                r.bias_down[at] = row[1:2]


def local(
    tokens, gain_attention, w_query, key_value_weight, w_output, sinks, gain_expert,
    w_gate, w_up, w_down, bias_gate, bias_up, bias_down, gates, routes, segments, cotangent,
):
    frequency = ROPE_BASE ** (-2.0 * jnp.arange(32, dtype=F32) / HEAD_DIM)
    common = dict(sinks=(sinks, SM)) | given(
        VM,
        gain1=gain_attention[None],
        gain2=gain_expert[None],
        routes_t=routes.T,
        tok=tokens,
        cot=cotangent,
        segments=segments[None],
        freq=jnp.tile(frequency, 4)[None],
    )
    rows = (128, 1024)
    slots = (2, 2, CAP, 1024)
    wide = (2, 1024, 2 * CAP)
    front = call(
        front_kernel,
        "front",
        0,
        common
        | given(
            VM, w_gate=w_gate, w_up=w_up, w_down=w_down, w_query=w_query,
            w_keyval=key_value_weight, w_output_t=w_output.T, gates_t=gates.T,
            bias_gate=bias_gate, bias_up=bias_up, bias_down=bias_down,
        ),
        dict(
            weights=((3, 4, 2, 2, 8, 64, 128), BF16, ANY),
            full0=(FULL, BF16, ANY),
            full1=(FULL, BF16, ANY),
            full2=(FULL, BF16, ANY),
            unpick=(wide, BF16, ANY),
            mid=(rows, F32, VM),
            normed_all=((2, 4, 128, 1024), BF16, ANY),
            queries=(rows, BF16, VM),
            keyvals=((256, 1024), BF16, VM),
            attended=(rows, BF16, VM),
            logsum=((128, 128), F32, VM),
            rows=(slots, BF16, VM),
            cot_rows=(slots, BF16, VM),
            gate_rows=((2, 2, CAP, 128), F32, VM),
            place_t=((2, 2, 1024), F32, VM),
            bias=((2, 1, 2048), F32, VM),
        ),
        dict(
            pairs=bf16(3, 2, 64, 2048),
            shards=bf16(3, 64, 128),
            normed1=bf16(*rows),
            sorted=bf16(3, 8, 2, 64, 128),
            full0_v=bf16(*FULL),
            full1_v=bf16(*FULL),
            full2_v=bf16(*FULL),
            unpick_v=bf16(*wide),
            pick=bf16(2, 2 * CAP, 1024),
            slot_gate=f32(2, 2, CAP, 128),
            prev=bf16(*rows),
            normed2=bf16(*rows),
            row_all=bf16(2, 4, 128, 1024),
            cot_all=bf16(2, 4, 128, 1024),
            row_out=bf16(2, CAP, 1024),
            cot_out=bf16(2, CAP, 1024),
            send=DMA((99,)),
            recv=DMA((99,)),
            cot_send=DMA((9,)),
            cot_recv=DMA((9,)),
            row_send=DMA((9,)),
            row_recv=DMA((9,)),
            own=DMA((4,)),
            keep=DMA((3,)),
            store=DMA((4,)),
        ),
    )
    experts = expert_block(front)
    bufs = dict(
        back_bufs=row_reduce_scratch(), out_bufs=row_reduce_scratch(), wo_bufs=reduce_scratch()
    )
    flat = {}
    for name, items in bufs.items():
        flat |= {name + str(k): item for k, item in enumerate(items)}

    def kernel(r):
        for name, items in bufs.items():
            setattr(r, name, [getattr(r, name + str(k)) for k in range(len(items))])
        back_kernel(r)

    half = (2, 3, 2, 512, 128)
    back = call(
        kernel,
        "back",
        2,
        common
        | given(
            VM, place_t=front.place_t, mid=front.mid, queries=front.queries,
            keyvals=front.keyvals, attended=front.attended, logsum=front.logsum,
            grad_bias=experts.grad_bias,
        )
        | given(
            ANY, out_rows=experts.out_rows, back_rows=experts.back_rows, dots=experts.dots,
            grads=experts.grads, normed_all=experts.normed_all, unpick=front.unpick,
            full0=front.full0, full1=front.full1, full2=front.full2,
        ),
        dict(
            layer_out=(rows, F32, VM),
            grad_tokens=(rows, F32, VM),
            grad_gates=((8, 128), F32, VM),
            grad_qkv=((2, 64, 128), F32, VM),
            grad_o=((64, 128), F32, VM),
            grad_experts=((3, 64, 2048), F32, VM),
            totals=((16, 24, 128), F32, VM),
            biases=((16, 4, 1024), F32, VM),
        ),
        dict(
            unpick_v=bf16(*wide),
            back_own=bf16(2, CAP, 1024),
            back_got=bf16(2, CAP, 1024),
            out_got=bf16(2, CAP, 1024),
            dot_own=f32(2, CAP, 128),
            dot_got=f32(2, CAP, 128),
            back_parts=bf16(2, 4, 128, 1024),
            out_parts=bf16(2, 4, 128, 1024),
            token_dots=f32(8, 2, 2, 128),
            dots_all=f32(8, 2, 2, 128),
            z_own=bf16(*half),
            z_near=bf16(*half),
            z_far=bf16(*half),
            z_solo=bf16(*half),
            z_send=bf16(*half),
            z_got=bf16(*half),
            deal_out=bf16(3, 2, 2, 8, 64, 128),
            deal_got=bf16(3, 2, 8, 2, 64, 128),
            unsorted=bf16(3, 2, 64, 2048),
            unsorted_got=bf16(3, 64, 2048),
            full0_v=bf16(*FULL),
            full1_v=bf16(*FULL),
            full2_v=bf16(*FULL),
            normed_v=bf16(2, 4, 128, 1024),
            grad_wo=bf16(*FULL),
            dq=f32(*rows),
            dkv=f32(*rows),
            halo=bf16(*rows),
            halo_got=bf16(*rows),
            low=bf16(2, 128, 1024),
            low_all=bf16(2, 8, 128, 128),
            grad_w=bf16(2, 16, 64, 128),
            grad_w_got=bf16(2, 16, 64, 128),
            small=f32(24, 128),
            small_got=f32(7, 24, 128),
            small_all=f32(16, 24, 128),
            bias_sum=f32(4, 1024),
            bias_got=f32(7, 4, 1024),
            bias_all=f32(16, 4, 1024),
            send=DMA((166,)),
            recv=DMA((166,)),
            load=DMA((11,)),
        )
        | flat,
    )
    done = call(
        finish_kernel,
        "finish",
        None,
        given(
            VM, layer_in=back.layer_out, tokens_in=back.grad_tokens, qkv=back.grad_qkv,
            wo_in=back.grad_o, experts=back.grad_experts, gates_in=back.grad_gates,
            totals=back.totals, biases=back.biases,
        ),
        dict(
            layer_out=(rows, F32, VM),
            grad_tokens=(rows, F32, VM),
            w_query=((64, 128), F32, VM),
            w_keyval=((64, 128), F32, VM),
            w_output_t=((64, 128), F32, VM),
            w_gate=((64, 2048), F32, VM),
            w_up=((64, 2048), F32, VM),
            w_down=((64, 2048), F32, VM),
            gates_t=((8, 128), F32, VM),
            gain1=((1, 1024), F32, VM),
            gain2=((1, 1024), F32, VM),
            sinks=((1, 16), F32, VM),
            bias_gate=((32, 512), F32, VM),
            bias_up=((32, 512), F32, VM),
            bias_down=((32, 1024), F32, VM),
        ),
        {},
    )
    return (
        done.layer_out,
        done.grad_tokens,
        done.gain1[0],
        done.w_query,
        done.w_keyval,
        done.w_output_t.T,
        done.sinks[0],
        done.gain2[0],
        done.w_gate,
        done.w_up,
        done.w_down,
        done.bias_gate,
        done.bias_up,
        done.bias_down,
        done.gates_t.T,
    )


def solution(mesh):
    fine = Mesh(mesh.devices.reshape(2, 4, 2, 8), ("xh", "z", "core", "tp"))
    fsdp = ("xh", "z", "core")
    rows = P(("xh", "z", "core", "tp"), None)
    return jax.shard_map(
        local,
        mesh=fine,
        in_specs=(
            rows,
            P(),
            P(fsdp, "tp"),
            P(fsdp, "tp"),
            P("tp", fsdp),
            P(),
            P(),
            P(fsdp, "tp"),
            P(fsdp, "tp"),
            P(fsdp, "tp"),
            P(),
            P(),
            P(),
            P(fsdp, None),
            P(fsdp, None),
            P(fsdp),
            rows,
        ),
        out_specs=(
            rows,
            rows,
            P(),
            P(fsdp, "tp"),
            P(fsdp, "tp"),
            P("tp", fsdp),
            P(),
            P(),
            P(fsdp, "tp"),
            P(fsdp, "tp"),
            P(fsdp, "tp"),
            P(),
            P(),
            P(),
            rows,
        ),
        check_vma=False,
    )
```

```python
import itertools
import types

import jax
import jax.numpy as jnp
from jax import lax
from jax.experimental import pallas as pl
from jax.experimental.pallas import tpu as pltpu
from jax.sharding import Mesh
from jax.sharding import PartitionSpec as P

MESH = pl.DeviceIdType.MESH
HEAD_DIM = 64
WINDOW = 128
EPS = 1e-05
ROPE_BASE = 10000.0
CLAMP = 7.0
SLOPE = 1.702
SCALE = HEAD_DIM ** (-0.5)
NEG = -1e30
CAP = 272
F32 = jnp.float32
BF16 = jnp.bfloat16
ANY = pl.BlockSpec(memory_space=pl.ANY)
DMA = pltpu.SemaphoreType.DMA
VM = pl.BlockSpec(memory_space=pltpu.VMEM)
SM = pl.BlockSpec(memory_space=pltpu.SMEM)
VMEM_LIMIT = 58 * 1024 * 1024

SIZES = {"xh": 2, "z": 4, "c": 2, "xl": 2, "y": 4, "x": 4}


def coords():
    xh, z = lax.axis_index("xh"), lax.axis_index("z")
    c, t = lax.axis_index("core"), lax.axis_index("tp")
    xl, y = t // 4, t % 4
    return {"xh": xh, "z": z, "c": c, "xl": xl, "y": y, "x": 2 * xh + xl}


def moved(place, offset):
    out = dict(place)
    for axis, step in offset.items():
        out[axis] = (place[axis] + step) % SIZES[axis]
        if axis == "x":
            out["xh"], out["xl"] = out["x"] // 2, out["x"] % 2
    return out


def device(place):
    return (place["xh"], place["z"], place["c"], place["xl"] * 4 + place["y"])


def offsets(axes):
    ranges = [range(SIZES[a]) for a in axes]
    return [dict(zip(axes, o)) for o in itertools.product(*ranges) if any(o)]


def slot(place, axes):
    out = 0
    for a in axes:
        out = out * SIZES[a] + place[a]
    return out


def greet(peers):
    barrier = pltpu.get_barrier_semaphore()
    for peer in peers:
        pl.semaphore_signal(barrier, inc=1, device_id=device(peer), device_id_type=MESH)
    pl.semaphore_wait(barrier, len(peers))


def remote(src, dst, send, recv, peer):
    return pltpu.make_async_remote_copy(
        src_ref=src,
        dst_ref=dst,
        send_sem=send,
        recv_sem=recv,
        device_id=device(peer),
        device_id_type=MESH,
    )


def comm_params(ident):
    return pltpu.CompilerParams(
        collective_id=ident, has_side_effects=True, vmem_limit_bytes=VMEM_LIMIT
    )


def call(kernel, name, ident, ins, outs, scratch, **extra):
    names = list(ins) + list(outs) + list(scratch)

    def body(*refs):
        kernel(types.SimpleNamespace(**dict(zip(names, refs))))

    if ident is None:
        params = pltpu.CompilerParams(vmem_limit_bytes=VMEM_LIMIT)
    else:
        params = comm_params(ident)
    results = pl.pallas_call(
        body,
        out_shape=[jax.ShapeDtypeStruct(o[0], o[1]) for o in outs.values()],
        in_specs=[i[1] for i in ins.values()],
        out_specs=[o[2] for o in outs.values()],
        scratch_shapes=list(scratch.values()),
        compiler_params=params,
        name=name,
        **extra,
    )(*[i[0] for i in ins.values()])
    return types.SimpleNamespace(**dict(zip(outs, results)))


def given(spec, **arrays):
    return {name: (a, spec) for name, a in arrays.items()}


def f32(*shape):
    return pltpu.VMEM(shape, F32)


def bf16(*shape):
    return pltpu.VMEM(shape, BF16)


class Copies:
    def __init__(self, send, recv):
        self.send, self.recv, self.all = send, recv, []

    def go(self, src, dst, peer):
        k = len(self.all)
        copy = remote(src, dst, self.send.at[k], self.recv.at[k], peer)
        copy.start()
        self.all.append(copy)
        return copy

    def sent(self):
        for copy in self.all:
            copy.wait_send()


def arrived(copies):
    for copy in copies:
        copy.wait_recv()


def along(here, axis):
    return [moved(here, {axis: k}) for k in (1, 3, 2)]


def sequence_neighbours(here):
    rank = here["xl"] * 4 + here["y"]
    after, before = (rank + 1) % 8, (rank + 7) % 8
    return dict(here, xl=after // 4, y=after % 4), dict(here, xl=before // 4, y=before % 4)


def lanes_of(place):
    return pl.ds(pl.multiple_of(place["y"] * 128, 128), 128)


LEFT, RIGHT = pl.ds(0, 512), pl.ds(512, 512)


class RowGather:
    def __init__(self, here, src, out, send, recv):
        self.here, self.src, self.out = here, src, out
        self.net = Copies(send, recv)
        self.side, self.ups = moved(here, {"xl": 1}), along(here, "y")

    def first(self):
        xl, y = self.here["xl"], self.here["y"]
        go = self.net.go
        self.x = go(self.src.at[:, LEFT], self.out.at[xl, y, :, LEFT], self.side)
        self.y = [go(self.src.at[:, RIGHT], self.out.at[xl, y, :, RIGHT], p) for p in self.ups]

    def then(self):
        xl, y = self.here["xl"], self.here["y"]
        self.x.wait_recv()
        view = self.out.at[:, y, :, LEFT]
        self.beside = [self.net.go(view, view, p) for p in self.ups[:2]]
        arrived(self.y)
        view = self.out.at[xl, :, :, RIGHT]
        self.last = [self.net.go(view, view, self.side)]

    def relay(self):
        arrived(self.beside)
        up, down = self.ups[:2]
        view = self.out.at[0, down["y"], :, LEFT]
        self.last.append(self.net.go(view, view, up))
        view = self.out.at[1, up["y"], :, LEFT]
        self.last.append(self.net.go(view, view, down))

    def finish(self):
        arrived(self.last)
        self.net.sent()


class RowReduce:
    def __init__(self, here, parts, bufs, send, recv):
        self.here, self.parts = here, parts
        self.got_y, self.sum_y, self.got_x, self.sum_x, self.end_y, self.end_x = bufs
        self.net = Copies(send, recv)
        self.side, self.ups = moved(here, {"xl": 1}), along(here, "y")

    def right(self):
        self.x = self.net.go(self.parts.at[self.side["xl"], :, :, RIGHT], self.got_x, self.side)

    def left(self):
        self.y = [
            self.net.go(self.parts.at[:, p["y"], :, LEFT], self.got_y.at[k], p)
            for k, p in enumerate(self.ups)
        ]

    def then_right(self):
        self.x.wait_recv()
        mine = self.parts[self.here["xl"], :, :, RIGHT].astype(F32)
        self.sum_x[...] = (mine + self.got_x[...].astype(F32)).astype(BF16)
        self.last_x = [
            self.net.go(self.sum_x.at[p["y"]], self.end_x.at[k], p) for k, p in enumerate(self.ups)
        ]

    def then_left(self):
        arrived(self.y)
        total = self.parts[:, self.here["y"], :, LEFT].astype(F32)
        for k in range(3):
            total = total + self.got_y[k].astype(F32)
        self.sum_y[...] = total.astype(BF16)
        self.last_y = self.net.go(self.sum_y.at[self.side["xl"]], self.end_y, self.side)

    def result(self):
        self.last_y.wait_recv()
        left = self.sum_y[self.here["xl"]].astype(F32) + self.end_y[...].astype(F32)
        arrived(self.last_x)
        right = self.sum_x[self.here["y"]].astype(F32)
        for k in range(3):
            right = right + self.end_x[k].astype(F32)
        return jnp.concatenate([left, right], 1)


def row_reduce_scratch():
    return [
        bf16(3, 2, 128, 512),
        bf16(2, 128, 512),
        bf16(4, 128, 512),
        bf16(4, 128, 512),
        bf16(128, 512),
        bf16(3, 128, 512),
        DMA((8,)),
        DMA((8,)),
    ]


FULL = (2, 2, 4, 2, 64, 512)


def region(ref, place, held):
    xl = slice(None) if "x" in held else place["xl"]
    xh = slice(None) if "x" in held else place["xh"]
    z = slice(None) if "z" in held else place["z"]
    y = pl.ds(0, 512) if "y" in held else lanes_of(place)
    return ref.at[xl, xh, z, place["c"], :, y]


class Spread:
    def __init__(self, here, full, net):
        self.here, self.full, self.net = here, full, net

    def step(self, axis, held, src=None):
        view = region(self.full, self.here, held)
        src = view if src is None else src
        self.group = [self.net.go(src, view, p) for p in along(self.here, axis)]

    def step_beside(self, axis, held):
        view = region(self.full, self.here, held)
        self.group = [self.net.go(view, view, p) for p in along(self.here, axis)[:2]]

    def relay_x(self):
        arrived(self.group)
        up, down = along(self.here, "x")[:2]
        c = self.here["c"]
        self.group = []
        for half, source, target in ((0, down, up), (2, up, down)):
            view = self.full.at[source["xl"], source["xh"], pl.ds(half, 2), c]
            self.group.append(self.net.go(view, view, target))

    def relay(self):
        arrived(self.group)
        up, down = along(self.here, "y")[:2]
        c = self.here["c"]
        self.group = []
        for half, source, target in ((0, down, up), (1, up, down)):
            view = self.full.at[half, :, :, c, :, lanes_of(source)]
            self.group.append(self.net.go(view, view, target))

    def swap(self):
        view = self.full.at[:, :, :, self.here["c"]]
        self.group = [self.net.go(view, view, moved(self.here, {"c": 1}))]

    def wait(self):
        arrived(self.group)


def matrix(ref, half):
    return ref[half].reshape(1024, 512)


class Reduce:
    def __init__(self, here, parts, bufs, send, recv):
        self.here, self.parts = here, parts
        self.got_core, self.sum_core, self.got_z, self.sum_z, self.got_plane = bufs
        self.net = Copies(send, recv)
        self.other = moved(here, {"c": 1})

    def swap(self):
        view = self.parts.at[:, :, :, self.other["c"]]
        self.group = [self.net.go(view, self.got_core, self.other)]

    def along_z(self):
        arrived(self.group)
        mine = self.parts[:, :, :, self.here["c"]].astype(F32)
        self.sum_core[...] = (mine + self.got_core[...].astype(F32)).astype(BF16)
        self.group = [
            self.net.go(self.sum_core.at[:, :, p["z"]], self.got_z.at[k], p)
            for k, p in enumerate(along(self.here, "z"))
        ]

    def over_plane(self):
        arrived(self.group)
        total = self.sum_core[:, :, self.here["z"]].astype(F32)
        for k in range(3):
            total = total + self.got_z[k].astype(F32)
        self.sum_z[...] = total.astype(BF16)
        peers = [moved(self.here, o) for o in offsets(("x", "y"))]
        self.group = [
            self.net.go(self.sum_z.at[p["xl"], p["xh"], :, lanes_of(p)], self.got_plane.at[k], p)
            for k, p in enumerate(peers)
        ]

    def result(self):
        arrived(self.group)
        here = self.here
        total = self.sum_z[here["xl"], here["xh"], :, lanes_of(here)].astype(F32)
        for k in range(15):
            total = total + self.got_plane[k].astype(F32)
        return total


def reduce_scratch():
    return [
        bf16(2, 2, 4, 64, 512),
        bf16(2, 2, 4, 64, 512),
        bf16(3, 2, 2, 64, 512),
        bf16(2, 2, 64, 512),
        bf16(15, 64, 128),
        DMA((19,)),
        DMA((19,)),
    ]


def nn(a, b):
    return lax.dot_general(a, b, (((1,), (0,)), ((), ())), preferred_element_type=F32)


def nt(a, b):
    return lax.dot_general(a, b, (((1,), (1,)), ((), ())), preferred_element_type=F32)


def tn(a, b):
    return lax.dot_general(a, b, (((0,), (0,)), ((), ())), preferred_element_type=F32)


def one_hot_columns(start, core):
    row = lax.broadcasted_iota(jnp.int32, (1024, 1), 0)
    column = lax.broadcasted_iota(jnp.int32, (1024, 1024), 1)
    expert = 4 * (row // 128) + 2 * core + (row // 64) % 2
    return (column == (row % 64) * 32 + expert - start).astype(F32).astype(BF16)


def rope_partner(values):
    lanes = values.shape[1]
    lane = lax.broadcasted_iota(jnp.int32, values.shape, 1)
    return jnp.where(
        lane % 64 < 32, pltpu.roll(values, lanes - 32, 1), pltpu.roll(values, 32, 1)
    )


def tiled(table):
    return jnp.concatenate([table] * 8, axis=1)


def head_pair(block):
    lane = lax.broadcasted_iota(jnp.int32, block.shape, 1) < 64
    wide = block.astype(F32)
    swapped = pltpu.roll(wide, 64, 1)
    zero = jnp.zeros_like(wide)
    keys = jnp.concatenate([jnp.where(lane, wide, zero), jnp.where(lane, zero, swapped)], 0)
    values = jnp.concatenate([jnp.where(lane, swapped, zero), jnp.where(lane, zero, wide)], 0)
    return keys.astype(BF16), values.astype(BF16)


def window_mask(segq, segk):
    row = lax.broadcasted_iota(jnp.int32, (128, 256), 0)
    column = lax.broadcasted_iota(jnp.int32, (128, 256), 1)
    distance = 128 + row - column
    return (segq == segk) & (distance >= 0) & (distance < WINDOW)


def rope_at(start, rows, freq):
    row = lax.broadcasted_iota(jnp.int32, (rows, 128), 0)
    lane = lax.broadcasted_iota(jnp.int32, (rows, 128), 1)
    angles = (row + start).astype(F32) * freq
    cosine, sine = jnp.cos(angles), jnp.sin(angles)
    return cosine, jnp.where(lane % 64 < 32, -sine, sine), lane < 64


def rope_queries(rank, freq):
    cosine, sine, _ = rope_at(128 * rank, 128, freq)
    return tiled(cosine), tiled(sine)


def rope_keyvals(start, rows, freq):
    cosine, sine, keys = rope_at(start, rows, freq)
    return tiled(jnp.where(keys, cosine, 1.0)), tiled(jnp.where(keys, sine, 0.0))


def mask_at(segments, rank):
    own = segments[:, pl.ds(pl.multiple_of(128 * rank, 128), 128)]
    prev = segments[:, pl.ds(pl.multiple_of(128 * ((rank + 7) % 8), 128), 128)]
    prev = jnp.where(rank == 0, -1, prev)
    row = lax.broadcasted_iota(jnp.int32, (128, 128), 0)
    column = lax.broadcasted_iota(jnp.int32, (128, 128), 1)
    segq = jnp.sum(jnp.where(row == column, own.astype(F32), 0.0), 1, keepdims=True)
    return window_mask(segq, jnp.concatenate([prev, own], 1).astype(F32))


def slot_tables(r, rank):
    row = lax.broadcasted_iota(jnp.int32, (1024, 1024), 0)
    column = lax.broadcasted_iota(jnp.int32, (1024, 1024), 1)
    before = (row < column).astype(F32).astype(BF16)
    routes_t, gates_t = r.routes_t[...], r.gates_t[...]
    hits, shares = [], []
    for el in range(4):
        named = routes_t == 4 * rank + el
        hits.append(jnp.sum(named.astype(F32), 0, keepdims=True))
        shares.append(jnp.sum(jnp.where(named, gates_t, 0.0), 0, keepdims=True))
    earlier = nn(jnp.concatenate(hits + [jnp.zeros((12, 1024), F32)], 0).astype(BF16), before)
    places = [jnp.where(hits[el] > 0, earlier[el : el + 1], -1.0) for el in range(4)]
    columns = jnp.concatenate(places + [jnp.zeros((124, 1024), F32)], 0).T
    slot = lax.broadcasted_iota(jnp.int32, (CAP, 1024), 0).astype(F32)
    wide = lax.broadcasted_iota(jnp.int32, (1024, 2 * CAP), 1).astype(F32)
    for c in range(2):
        for e in range(2):
            el = 2 * c + e
            r.place_t[c, e : e + 1] = places[el]
            hot = slot == places[el]
            r.pick[c, CAP * e : CAP * e + CAP] = hot.astype(F32).astype(BF16)
            share = jnp.sum(jnp.where(hot, shares[el], 0.0), 1, keepdims=True)
            r.slot_gate[c, e] = jnp.broadcast_to(share, (CAP, 128))
        low = (wide == columns[:, 2 * c : 2 * c + 1]) & (wide < CAP)
        high = (wide - CAP == columns[:, 2 * c + 1 : 2 * c + 2]) & (wide >= CAP)
        r.unpick_v[c] = (low | high).astype(F32).astype(BF16)


DEAL_AXES = ("xh", "xl", "y")


def front_kernel(r):
    here = coords()
    c, xh, z, xl, y = (here[a] for a in ("c", "xh", "z", "xl", "y"))
    rank = xl * 4 + y
    other = moved(here, {"c": 1})
    after, before = sequence_neighbours(here)
    dealt = [moved(here, o) for o in offsets(DEAL_AXES)]
    up, down = moved(here, {"z": 1}), moved(here, {"z": 3})
    parts = (r.w_gate, r.w_up, r.w_down)
    fulls = (r.full0_v, r.full1_v, r.full2_v)
    for w, ref in enumerate(parts):
        r.pairs[w, c] = ref[...]
    for p, ref in enumerate((r.w_query, r.w_keyval, r.w_output_t)):
        r.shards[p] = ref[...]
    own = [
        pltpu.make_async_copy(r.shards.at[p], region(fulls[p], here, ""), r.own.at[p])
        for p in range(3)
    ]
    for copy in own:
        copy.start()
    greet([other, after, before] + [p for a in "xyz" for p in along(here, a)] + dealt)
    net = Copies(r.send, r.recv)
    swaps = [net.go(ref, r.pairs.at[w, c], other) for w, ref in enumerate(parts)]
    q_full, kv_full, o_full = (Spread(here, full, net) for full in fulls)
    kv_full.step("y", "", r.shards.at[1])
    q_full.step("z", "", r.shards.at[0])
    o_full.step("z", "", r.shards.at[2])
    cots = RowGather(here, r.cot, r.cot_all, r.cot_send, r.cot_recv)
    first = 4 * rank + 2 * c
    for e in range(2):
        r.bias[e, :, :512] = r.bias_gate[pl.ds(first + e, 1)]
        r.bias[e, :, 512:1024] = r.bias_up[pl.ds(first + e, 1)]
        r.bias[e, :, 1024:] = r.bias_down[pl.ds(first + e, 1)]
    r.cot_all[xl, y] = r.cot[...]
    hot_left = one_hot_columns(0, c)
    for copy in own:
        copy.wait()
    kv_full.wait()
    kv_full.step("x", "y")
    q_full.wait()
    q_full.step("y", "z")
    o_full.wait()
    o_full.step("x", "z")
    halo = net.go(r.tok, r.prev, after)
    hot = jnp.concatenate([hot_left, one_hot_columns(1024, c)], 1)
    deals, keeps = [], []

    def sort(w):
        arrived([swaps[w]])
        rows = r.pairs[w].reshape(128, 2048)
        r.sorted[w] = nt(hot, rows).astype(BF16).reshape(8, 2, 64, 128)
        mine = r.weights.at[w, z, xh, :, rank]
        keeps.append(pltpu.make_async_copy(r.sorted.at[w, rank], mine, r.keep.at[w]))
        keeps[w].start()

    def deal(w):
        mine = r.weights.at[w, z, xh, :, rank]
        deals.append([net.go(r.sorted.at[w, p["xl"] * 4 + p["y"]], mine, p) for p in dealt])

    ring, last_ring = [], []

    def send_on(w):
        arrived(deals[w])
        keeps[w].wait()
        view = r.weights.at[w, z]
        ring.append([net.go(view, view, up), net.go(view, view, down)])

    def pass_on(w):
        arrived(ring[w])
        view = r.weights.at[w, down["z"], 0]
        last_ring.append(net.go(view, view, up))
        view = r.weights.at[w, up["z"], 1]
        last_ring.append(net.go(view, view, down))

    sort(0)
    deal(0)
    kv_full.wait()
    kv_full.step("z", "yx")
    q_full.wait()
    q_full.step_beside("x", "zy")
    o_full.wait()
    o_full.step_beside("y", "zx")
    sort(1)
    sort(2)
    slot_tables(r, rank)
    stores = [pltpu.make_async_copy(r.unpick_v, r.unpick, r.store.at[0])]
    stores[0].start()

    def save(k, full, result):
        stores.append(pltpu.make_async_copy(full, result, r.store.at[k]))
        stores[k].start()

    send_on(0)
    q_full.relay_x()
    deal(1)
    o_full.relay()
    kv_full.wait()
    kv_full.swap()
    halo.wait_recv()
    tok = r.tok[...].astype(F32)
    both = jnp.concatenate([r.prev[...].astype(F32), tok], 0)
    scale = lax.rsqrt(jnp.mean(both * both, -1, keepdims=True) + EPS)
    normed = (both * scale * r.gain1[...]).astype(BF16)
    normed_own = normed[128:]
    r.normed1[...] = normed_own
    keep_normed = pltpu.make_async_copy(r.normed1, r.normed_all.at[xl, y], r.own.at[3])
    keep_normed.start()
    q_full.wait()
    q_full.swap()
    kv_full.wait()
    deal(2)
    cots.first()
    save(1, r.full1_v, r.full1)
    kv = jnp.concatenate([nn(normed, matrix(r.full1_v, 0)), nn(normed, matrix(r.full1_v, 1))], 1)
    cosine, sine = rope_keyvals(128 * rank - 128, 256, r.freq[...])
    kv = (kv * cosine + rope_partner(kv) * sine).astype(BF16)
    r.keyvals[...] = kv
    o_full.wait()
    o_full.swap()
    pass_on(0)
    gates = net.go(r.slot_gate.at[other["c"]], r.gate_rows.at[c], other)
    r.gate_rows[c] = r.slot_gate[c]
    mask = mask_at(r.segments, rank)
    lane = lax.broadcasted_iota(jnp.int32, (128, 128), 1)
    q_full.wait()
    save(2, r.full0_v, r.full0)
    q = jnp.concatenate(
        [nn(normed_own, matrix(r.full0_v, 0)), nn(normed_own, matrix(r.full0_v, 1))], 1
    )
    cosine, sine = rope_queries(rank, r.freq[...])
    q = (q * cosine + rope_partner(q) * sine).astype(BF16)
    r.queries[...] = q
    send_on(1)
    sums = jnp.zeros((128, 128), F32)
    for g in range(8):
        part = slice(128 * g, 128 * g + 128)
        keys, values = head_pair(kv[:, part])
        scores = nt(q[:, part], keys) * SCALE
        shares = []
        for h in range(2):
            masked = jnp.where(mask, scores[:, 256 * h : 256 * h + 256], NEG)
            sink = r.sinks[2 * g + h]
            peak = jnp.maximum(jnp.max(masked, -1, keepdims=True), sink)
            total = jnp.exp(sink - peak) + jnp.sum(jnp.exp(masked - peak), -1, keepdims=True)
            log_total = peak + jnp.log(total)
            shares.append(jnp.exp(masked - log_total).astype(BF16))
            sums = jnp.where(lane == 2 * g + h, log_total, sums)
        r.attended[:, part] = nn(jnp.concatenate(shares, 1), values).astype(BF16)
        if g == 4:
            send_on(2)
    r.logsum[...] = sums
    cots.then()
    o_full.wait()
    save(3, r.full2_v, r.full2)
    out = (
        tok
        + nt(r.attended[:, :512], matrix(r.full2_v, 0))
        + nt(r.attended[:, 512:], matrix(r.full2_v, 1))
    )
    r.mid[...] = out
    scale = lax.rsqrt(jnp.mean(out * out, -1, keepdims=True) + EPS)
    r.normed2[...] = (out * scale * r.gain2[...]).astype(BF16)

    rows = RowGather(here, r.normed2, r.row_all, r.row_send, r.row_recv)
    rows.first()
    r.row_all[xl, y] = r.normed2[...]
    cots.relay()

    def to_slots(gathered, outgoing, result):
        tokens = gathered[...].reshape(1024, 1024)
        outgoing[...] = nn(r.pick[other["c"]], tokens).astype(BF16).reshape(2, CAP, 1024)
        copy = net.go(outgoing, result.at[c], other)
        result[c] = nn(r.pick[c], tokens).astype(BF16).reshape(2, CAP, 1024)
        return copy

    rows.then()
    pass_on(1)
    cots.finish()
    cot_copy = to_slots(r.cot_all, r.cot_out, r.cot_rows)
    rows.relay()
    pass_on(2)
    rows.finish()
    near = [
        net.go(r.normed1.at[:, LEFT], r.normed_all.at[xl, y, :, LEFT], moved(here, {"xl": 1}))
    ]
    view = r.normed_all.at[xl, y, :, RIGHT]
    near += [net.go(r.normed1.at[:, RIGHT], view, p) for p in along(here, "y")]
    row_copy = to_slots(r.row_all, r.row_out, r.rows)
    arrived([gates, cot_copy, row_copy])
    arrived(near)
    arrived(last_ring)
    for copy in stores:
        copy.wait()
    keep_normed.wait()
    net.sent()


def expert_kernel(r):
    turn = pl.program_id(0)
    here = coords()
    xl, y = here["xl"], here["y"]
    side, ups = moved(here, {"xl": 1}), along(here, "y")
    out = r.normed_all
    column, line = out.at[:, y, :, LEFT], out.at[xl, :, :, RIGHT]
    then = [
        remote(column, column, r.send.at[k], r.recv.at[k], p) for k, p in enumerate(ups)
    ]
    then.append(remote(line, line, r.send.at[3], r.recv.at[3], side))

    @pl.when(turn == 0)
    def _():
        greet([side] + ups)
        for item in then:
            item.start()

    def stacked(w):
        return jnp.concatenate(
            [r.weights[w, m % 4, m // 4, 0].reshape(512, 128) for m in range(8)], 1
        )

    w_gate, w_up, w_down = stacked(0), stacked(1), stacked(2)
    bias = r.bias[0]
    x = r.rows[:, 0].reshape(2 * CAP, 1024)
    tanh_gate = jnp.tanh((nt(x, w_gate) + bias[:, :512]) / CLAMP)
    tanh_up = jnp.tanh((nt(x, w_up) + bias[:, 512:1024]) / CLAMP)
    soft_gate, soft_up = CLAMP * tanh_gate, CLAMP * tanh_up
    sig = jax.nn.sigmoid(SLOPE * soft_gate)
    glu = soft_gate * sig
    hidden = (glu * (soft_up + 1.0)).astype(BF16)
    produced = nn(hidden, w_down) + bias[:, 1024:]
    share = r.gate_rows[:, 0].reshape(2 * CAP, 128)[:, :1]
    cot = r.cot_rows[:, 0].reshape(2 * CAP, 1024).astype(F32)
    r.out_rows[:, 0] = (share * produced).astype(BF16).reshape(2, CAP, 1024)

    products = produced * cot
    partial = products[:, :128]
    for m in range(1, 8):
        partial = partial + products[:, 128 * m : 128 * m + 128]
    r.dots[:, 0] = partial.reshape(2, CAP, 128)
    scaled = share * cot
    r.grad_bias[0, :, 1024:] = jnp.sum(scaled, 0, keepdims=True)
    rows_grad = scaled.astype(BF16)
    hidden_grad = nt(rows_grad, w_down)
    gate_grad = (
        hidden_grad
        * (soft_up + 1.0)
        * (sig + SLOPE * glu * (1.0 - sig))
        * (1.0 - tanh_gate * tanh_gate)
    )
    up_grad = hidden_grad * glu * (1.0 - tanh_up * tanh_up)
    r.grad_bias[0, :, :512] = jnp.sum(gate_grad, 0, keepdims=True)
    r.grad_bias[0, :, 512:1024] = jnp.sum(up_grad, 0, keepdims=True)
    gate_low, up_low = gate_grad.astype(BF16), up_grad.astype(BF16)
    back = (nn(gate_low, w_gate) + nn(up_low, w_up)).astype(BF16)
    r.back_rows[:, 0] = back.reshape(2, CAP, 1024)
    for w, (left, right) in enumerate(((gate_low, x), (up_low, x), (hidden, rows_grad))):
        grad = tn(left, right).astype(BF16)
        for m in range(8):
            r.grads[m % 4, m // 4, w, 0] = grad[:, 128 * m : 128 * m + 128]

    @pl.when(turn == 1)
    def _():
        for item in then:
            item.wait()


def expert_block(front):
    def at(dim, *shape):
        return pl.BlockSpec(
            shape[:dim] + (1,) + shape[dim:],
            lambda e: (0,) * dim + (e,) + (0,) * (len(shape) - dim),
        )

    per_row, per_slot = at(1, 2, CAP, 1024), at(1, 2, CAP, 128)
    stacked, vector = at(3, 4, 2, 3, 512, 128), at(0, 1, 2048)
    return call(
        expert_kernel,
        "experts",
        1,
        dict(
            rows=(front.rows, per_row),
            cot_rows=(front.cot_rows, per_row),
            gate_rows=(front.gate_rows, per_slot),
            weights=(front.weights, at(3, 3, 4, 2, 8, 64, 128)),
            bias=(front.bias, vector),
            normed_near=(front.normed_all, ANY),
        ),
        dict(
            out_rows=((2, 2, CAP, 1024), BF16, per_row),
            back_rows=((2, 2, CAP, 1024), BF16, per_row),
            dots=((2, 2, CAP, 128), F32, per_slot),
            grads=((4, 2, 3, 2, 512, 128), BF16, stacked),
            grad_bias=((2, 1, 2048), F32, vector),
            normed_all=((2, 4, 128, 1024), BF16, ANY),
        ),
        dict(send=DMA((4,)), recv=DMA((4,))),
        grid=(2,),
        input_output_aliases={5: 5},
    )


def norm_back(values, gain, grad):
    scale = lax.rsqrt(jnp.mean(values * values, -1, keepdims=True) + EPS)
    normed = values * scale
    weighted = gain * grad
    back = scale * (weighted - normed * jnp.mean(weighted * normed, -1, keepdims=True))
    return back, jnp.sum(grad * normed, 0, keepdims=True)


class ZSum:
    def __init__(self, r, here, net):
        self.r, self.net, self.z = r, net, here["z"]
        self.up, self.down = moved(here, {"z": 1}), moved(here, {"z": 3})
        far = (self.z + 2) % 4
        self.solo, self.both = [None] * 3, [None] * 3
        self.far = [
            [
                net.go(r.grads.at[far, 0, w], r.z_far.at[0, w], self.up),
                net.go(r.grads.at[far, 1, w], r.z_far.at[1, w], self.down),
            ]
            for w in range(3)
        ]

    def alone(self, w):
        r, up, down = self.r, self.up, self.down
        self.solo[w] = [
            self.net.go(r.grads.at[up["z"], 1, w], r.z_solo.at[1, w], up),
            self.net.go(r.grads.at[down["z"], 0, w], r.z_solo.at[0, w], down),
        ]

    def add(self, w):
        r = self.r
        arrived(self.far[w])
        for half in range(2):
            r.z_send[half, w] = (
                r.z_near[half, w].astype(F32) + r.z_far[half, w].astype(F32)
            ).astype(BF16)
        self.both[w] = [
            self.net.go(r.z_send.at[0, w], r.z_got.at[0, w], self.up),
            self.net.go(r.z_send.at[1, w], r.z_got.at[1, w], self.down),
        ]

    def total(self, w, half):
        r = self.r
        return (
            r.z_own[half, w].astype(F32)
            + r.z_got[half, w].astype(F32)
            + r.z_solo[half, w].astype(F32)
        ).astype(BF16)

    def wait(self, w):
        arrived(self.solo[w] + self.both[w])


def back_kernel(r):
    here = coords()
    c, xh, z, xl, y = (here[a] for a in ("c", "xh", "z", "xl", "y"))
    rank = xl * 4 + y
    other = moved(here, {"c": 1})
    after, before = sequence_neighbours(here)
    everyone = [moved(here, o) for o in offsets(("xl", "y"))]
    dealt = [moved(here, o) for o in offsets(DEAL_AXES)]
    owners = [moved(here, o) for o in offsets(("xh", "z", "c"))]
    planes = [moved(here, o) for o in offsets(("xh", "z"))]
    places = [moved(here, o) for o in offsets(("c", "xl", "y"))]
    loads = []

    def load(src, dst):
        copy = pltpu.make_async_copy(src, dst, r.load.at[len(loads)])
        copy.start()
        loads.append(copy)
        return copy

    get_unpick = load(r.unpick, r.unpick_v)
    get_back = load(r.back_rows.at[c], r.back_own)
    get_dots = load(r.dots.at[c], r.dot_own)
    get_near = [
        load(r.grads.at[(z + 1) % 4, 0], r.z_near.at[0]),
        load(r.grads.at[(z + 3) % 4, 1], r.z_near.at[1]),
    ]
    get_full2 = load(r.full2, r.full2_v)
    get_z = load(r.grads.at[z], r.z_own)
    get_full0 = load(r.full0, r.full0_v)
    get_full1 = load(r.full1, r.full1_v)
    get_normed = load(r.normed_all, r.normed_v)
    greet(
        [other, after, before]
        + [p for a in "xyz" for p in along(here, a)]
        + everyone + dealt + owners + planes + places
    )
    net = Copies(r.send, r.recv)
    back_swap = net.go(r.back_rows.at[other["c"]], r.back_got, other)
    for e in range(2):
        r.bias_sum[2 * e : 2 * e + 1] = r.grad_bias[e, :, :1024]
        r.bias_sum[2 * e + 1 : 2 * e + 2] = r.grad_bias[e, :, 1024:]
    biases = [net.go(r.bias_sum, r.bias_got.at[k], p) for k, p in enumerate(planes)]
    zsum = ZSum(r, here, net)

    def to_tokens(own, got, parts, columns):
        mine = nn(r.unpick_v[c], own[:, :, columns].reshape(2 * CAP, 512))
        theirs = nn(r.unpick_v[other["c"]], got[:, :, columns].reshape(2 * CAP, 512))
        parts[:, :, :, columns] = (mine + theirs).astype(BF16).reshape(2, 4, 128, 512)

    back = RowReduce(here, r.back_parts, r.back_bufs[:6], *r.back_bufs[6:])
    out = RowReduce(here, r.out_parts, r.out_bufs[:6], *r.out_bufs[6:])
    get_unpick.wait()
    get_back.wait()
    back_swap.wait_recv()
    dot_swap = net.go(r.dots.at[other["c"]], r.dot_got, other)
    out_swap = net.go(r.out_rows.at[other["c"]], r.out_got, other)
    to_tokens(r.back_own, r.back_got, r.back_parts, RIGHT)
    back.right()
    to_tokens(r.back_own, r.back_got, r.back_parts, LEFT)
    back.left()
    get_out = load(r.out_rows.at[c], r.back_own)

    get_dots.wait()
    dot_swap.wait_recv()
    slot = lax.broadcasted_iota(jnp.int32, (CAP, 1024), 0).astype(F32)
    for source, core in ((r.dot_own, c), (r.dot_got, other["c"])):
        for e in range(2):
            totals = jnp.sum(source[e], 1, keepdims=True)
            hot = slot == r.place_t[core, e : e + 1]
            line = jnp.sum(jnp.where(hot, totals, 0.0), 0, keepdims=True)
            for j in range(8):
                r.token_dots[j, core, e : e + 1] = line[:, 128 * j : 128 * j + 128]
    r.dots_all[rank] = r.token_dots[rank]
    dot_copies = [
        net.go(r.token_dots.at[p["xl"] * 4 + p["y"]], r.dots_all.at[rank], p) for p in everyone
    ]
    for copy in get_near:
        copy.wait()
    zsum.add(0)
    zsum.alone(0)
    get_out.wait()
    out_swap.wait_recv()
    to_tokens(r.back_own, r.out_got, r.out_parts, RIGHT)
    to_tokens(r.back_own, r.out_got, r.out_parts, LEFT)
    back.then_right()
    back.then_left()
    out.right()
    out.left()
    for w in (1, 2):
        zsum.add(w)
        zsum.alone(w)
    spot = c * 8 + rank
    arrived(biases)
    total = r.bias_sum[...]
    for k in range(7):
        total = total + r.bias_got[k]
    r.bias_all[spot] = total
    biases = [net.go(r.bias_all.at[spot], r.bias_all.at[spot], p) for p in places]
    moved_in = back.result()

    step, gain_part = norm_back(r.mid[...], r.gain2[...], moved_in)
    for k in range(8):
        r.small[8 + k : 9 + k] = gain_part[:, 128 * k : 128 * k + 128]
    mid_grad = r.cot[...].astype(F32) + step
    low = mid_grad.astype(BF16)
    for half in range(2):
        columns = slice(512 * half, 512 * half + 512)
        r.grad_wo[half] = tn(low, r.attended[:, columns]).astype(BF16).reshape(FULL[1:])
    wo = Reduce(here, r.grad_wo, r.wo_bufs[:5], *r.wo_bufs[5:])
    wo.swap()
    get_full2.wait()
    out_grad = jnp.concatenate([nn(low, matrix(r.full2_v, 0)), nn(low, matrix(r.full2_v, 1))], 1)
    out_grad = out_grad.astype(BF16)
    mask = mask_at(r.segments, rank)
    lane_row = lax.broadcasted_iota(jnp.int32, (1, 128), 1)
    lane = lax.broadcasted_iota(jnp.int32, (256, 128), 1) < 64
    sink_grads = jnp.zeros((1, 128), F32)
    halos = []
    for g in range(8):
        part = slice(128 * g, 128 * g + 128)
        keys, values = head_pair(r.keyvals[:, part])
        q = r.queries[:, part]
        grad_block = out_grad[:, part]
        scores = nt(q, keys) * SCALE
        share_grads = nt(grad_block, values)
        shares, score_grads = [], []
        for h in range(2):
            columns = slice(256 * h, 256 * h + 256)
            log_total = r.logsum[:, 2 * g + h : 2 * g + h + 1]
            share = jnp.exp(jnp.where(mask, scores[:, columns], NEG) - log_total)
            term = jnp.sum(share * share_grads[:, columns], -1, keepdims=True)
            shares.append(share.astype(BF16))
            score_grads.append((share * (share_grads[:, columns] - term)).astype(BF16))
            sink_part = -jnp.sum(jnp.exp(r.sinks[2 * g + h] - log_total) * term, 0, keepdims=True)
            sink_grads = jnp.where(lane_row == 2 * g + h, sink_part, sink_grads)
        shares = jnp.concatenate(shares, 1)
        score_grads = jnp.concatenate(score_grads, 1)
        r.dq[:, part] = nn(score_grads, keys) * SCALE
        from_scores = tn(score_grads, q) * SCALE
        from_shares = tn(shares, grad_block)
        joined = jnp.where(
            lane,
            from_scores[:256] + pltpu.roll(from_scores[256:], 64, 1),
            pltpu.roll(from_shares[:256], 64, 1) + from_shares[256:],
        )
        r.halo[:, part] = joined[:128].astype(BF16)
        r.dkv[:, part] = joined[128:]
        if g == 3:
            wo.along_z()
        if g % 4 == 3:
            view = slice(512 * (g // 4), 512 * (g // 4) + 512)
            halos.append(net.go(r.halo.at[:, view], r.halo_got.at[:, view], before))

    get_z.wait()
    deals = []

    def deal(w):
        zsum.wait(w)
        for half in range(2):
            r.deal_out[w, half] = zsum.total(w, half).reshape(2, 8, 64, 128)
        r.deal_got[w, xh, rank] = r.deal_out[w, xh, :, rank]
        deals.append(
            [
                net.go(
                    r.deal_out.at[w, p["xh"], :, p["xl"] * 4 + p["y"]], r.deal_got.at[w, xh, rank], p
                )
                for p in dealt
            ]
        )

    def to_columns(low, k):
        r.low[k] = low
        r.low_all[k, rank] = r.low[k, :, lanes_at(rank)]
        return [net.go(r.low.at[k, :, lanes_at(p["xl"] * 4 + p["y"])], r.low_all.at[k, rank], p) for p in everyone]

    grad_q = r.dq[...]
    cosine, sine = rope_queries(rank, r.freq[...])
    low = (grad_q * cosine - rope_partner(grad_q) * sine).astype(BF16)
    q_copies = to_columns(low, 0)
    get_full0.wait()
    first_back = nt(low[:, :512], matrix(r.full0_v, 0)) + nt(low[:, 512:], matrix(r.full0_v, 1))

    hot = one_hot_columns(0, c)
    r.full2_v[0] = hot[:, :512].reshape(FULL[1:])
    r.full2_v[1] = hot[:, 512:].reshape(FULL[1:])
    hot = one_hot_columns(1024, c)
    r.full0_v[0] = hot[:, :512].reshape(FULL[1:])
    r.full0_v[1] = hot[:, 512:].reshape(FULL[1:])
    arrived(halos)
    grad_kv = r.dkv[...] + r.halo_got[...].astype(F32)
    cosine, sine = rope_keyvals(128 * rank, 128, r.freq[...])
    low = (grad_kv * cosine - rope_partner(grad_kv) * sine).astype(BF16)
    kv_copies = to_columns(low, 1)
    deal(0)
    get_full1.wait()
    first_back = (
        first_back + nt(low[:, :512], matrix(r.full1_v, 0)) + nt(low[:, 512:], matrix(r.full1_v, 1))
    )
    norm_grad, gain_part = norm_back(r.tok[...].astype(F32), r.gain1[...], first_back)
    r.grad_tokens[...] = mid_grad + norm_grad
    for k in range(8):
        r.small[k : k + 1] = gain_part[:, 128 * k : 128 * k + 128]
    r.small[16:24] = jnp.concatenate([sink_grads, jnp.zeros((7, 128), F32)], 0)
    small = [net.go(r.small, r.small_got.at[k], p) for k, p in enumerate(planes)]

    get_normed.wait()
    normed = r.normed_v[...].reshape(1024, 1024)
    mine = (xh * 4 + z) * 2 + c
    sums = []

    def product(k, copies):
        arrived(copies)
        block = tn(normed, r.low_all[k].reshape(1024, 128))
        r.grad_w[k] = block.astype(BF16).reshape(16, 64, 128)
        r.grad_w_got[k, mine] = r.grad_w[k, mine]
        sums.append(
            [
                net.go(
                    r.grad_w.at[k, (p["xh"] * 4 + p["z"]) * 2 + p["c"]], r.grad_w_got.at[k, mine], p
                )
                for p in owners
            ]
        )

    deal(1)
    product(0, q_copies)
    product(1, kv_copies)
    deal(2)
    out.then_right()
    out.then_left()
    unsorted = []

    def unsort(w):
        arrived(deals[w])
        summed = r.deal_got[w, 0].astype(F32) + r.deal_got[w, 1].astype(F32)
        lines = summed.reshape(1024, 128).T.astype(BF16)
        for k in range(4):
            wide = nn(lines, matrix(r.full2_v if k < 2 else r.full0_v, k % 2)).astype(BF16)
            r.unsorted[w, :, :, 512 * k : 512 * k + 512] = wide.reshape(2, 64, 512)
        unsorted.append(net.go(r.unsorted.at[w, other["c"]], r.unsorted_got.at[w], other))

    unsort(0)
    wo.over_plane()
    unsort(1)
    arrived(small)
    total = r.small[...]
    for k in range(7):
        total = total + r.small_got[k]
    r.small_all[spot] = total
    small = [net.go(r.small_all.at[spot], r.small_all.at[spot], p) for p in places]
    r.layer_out[...] = r.mid[...] + out.result()
    arrived(dot_copies)
    own_routes = r.routes_t[:, lanes_at(rank)]
    chosen = jnp.zeros((8, 128), F32)
    for j in range(8):
        for core in range(2):
            for e in range(2):
                line = r.dots_all[j, core, e : e + 1]
                chosen = jnp.where(own_routes == 4 * j + 2 * core + e, line, chosen)
    r.grad_gates[...] = chosen
    unsort(2)
    for k, copies in enumerate(sums):
        arrived(copies)
        total = r.grad_w_got[k, 0].astype(F32)
        for m in range(1, 16):
            total = total + r.grad_w_got[k, m].astype(F32)
        r.grad_qkv[k] = total
    r.grad_o[...] = wo.result()
    arrived(small)
    arrived(biases)
    for w in range(3):
        arrived([unsorted[w]])
        r.grad_experts[w] = r.unsorted[w, c].astype(F32) + r.unsorted_got[w].astype(F32)
    r.totals[...] = r.small_all[...]
    r.biases[...] = r.bias_all[...]
    for sent in (net, back.net, out.net, wo.net):
        sent.sent()


def lanes_at(rank):
    return pl.ds(pl.multiple_of(rank * 128, 128), 128)


def finish_kernel(r):
    r.layer_out[...] = r.layer_in[...]
    r.grad_tokens[...] = r.tokens_in[...]
    r.w_query[...] = r.qkv[0]
    r.w_keyval[...] = r.qkv[1]
    r.w_output_t[...] = r.wo_in[...]
    r.w_gate[...] = r.experts[0]
    r.w_up[...] = r.experts[1]
    r.w_down[...] = r.experts[2]
    r.gates_t[...] = r.gates_in[...]
    total = r.totals[0]
    for k in range(1, 16):
        total = total + r.totals[k]
    for k in range(8):
        r.gain1[:, 128 * k : 128 * k + 128] = total[k : k + 1]
        r.gain2[:, 128 * k : 128 * k + 128] = total[8 + k : 9 + k]
    r.sinks[...] = total[16:17, :16]
    for core in range(2):
        for j in range(8):
            for e in range(2):
                at = slice(4 * j + 2 * core + e, 4 * j + 2 * core + e + 1)
                row = r.biases[core * 8 + j, 2 * e : 2 * e + 2]
                r.bias_gate[at] = row[0:1, :512]
                r.bias_up[at] = row[0:1, 512:]
                r.bias_down[at] = row[1:2]


def local(
    tokens, gain_attention, w_query, key_value_weight, w_output, sinks, gain_expert,
    w_gate, w_up, w_down, bias_gate, bias_up, bias_down, gates, routes, segments, cotangent,
):
    frequency = ROPE_BASE ** (-2.0 * jnp.arange(32, dtype=F32) / HEAD_DIM)
    common = dict(sinks=(sinks, SM)) | given(
        VM,
        gain1=gain_attention[None],
        gain2=gain_expert[None],
        routes_t=routes.T,
        tok=tokens,
        cot=cotangent,
        segments=segments[None],
        freq=jnp.tile(frequency, 4)[None],
    )
    rows = (128, 1024)
    slots = (2, 2, CAP, 1024)
    wide = (2, 1024, 2 * CAP)
    front = call(
        front_kernel,
        "front",
        0,
        common
        | given(
            VM, w_gate=w_gate, w_up=w_up, w_down=w_down, w_query=w_query,
            w_keyval=key_value_weight, w_output_t=w_output.T, gates_t=gates.T,
            bias_gate=bias_gate, bias_up=bias_up, bias_down=bias_down,
        ),
        dict(
            weights=((3, 4, 2, 2, 8, 64, 128), BF16, ANY),
            full0=(FULL, BF16, ANY),
            full1=(FULL, BF16, ANY),
            full2=(FULL, BF16, ANY),
            unpick=(wide, BF16, ANY),
            mid=(rows, F32, VM),
            normed_all=((2, 4, 128, 1024), BF16, ANY),
            queries=(rows, BF16, VM),
            keyvals=((256, 1024), BF16, VM),
            attended=(rows, BF16, VM),
            logsum=((128, 128), F32, VM),
            rows=(slots, BF16, VM),
            cot_rows=(slots, BF16, VM),
            gate_rows=((2, 2, CAP, 128), F32, VM),
            place_t=((2, 2, 1024), F32, VM),
            bias=((2, 1, 2048), F32, VM),
        ),
        dict(
            pairs=bf16(3, 2, 64, 2048),
            shards=bf16(3, 64, 128),
            normed1=bf16(*rows),
            sorted=bf16(3, 8, 2, 64, 128),
            full0_v=bf16(*FULL),
            full1_v=bf16(*FULL),
            full2_v=bf16(*FULL),
            unpick_v=bf16(*wide),
            pick=bf16(2, 2 * CAP, 1024),
            slot_gate=f32(2, 2, CAP, 128),
            prev=bf16(*rows),
            normed2=bf16(*rows),
            row_all=bf16(2, 4, 128, 1024),
            cot_all=bf16(2, 4, 128, 1024),
            row_out=bf16(2, CAP, 1024),
            cot_out=bf16(2, CAP, 1024),
            send=DMA((100,)),
            recv=DMA((100,)),
            cot_send=DMA((9,)),
            cot_recv=DMA((9,)),
            row_send=DMA((9,)),
            row_recv=DMA((9,)),
            own=DMA((4,)),
            keep=DMA((3,)),
            store=DMA((4,)),
        ),
    )
    experts = expert_block(front)
    bufs = dict(
        back_bufs=row_reduce_scratch(), out_bufs=row_reduce_scratch(), wo_bufs=reduce_scratch()
    )
    flat = {}
    for name, items in bufs.items():
        flat |= {name + str(k): item for k, item in enumerate(items)}

    def kernel(r):
        for name, items in bufs.items():
            setattr(r, name, [getattr(r, name + str(k)) for k in range(len(items))])
        back_kernel(r)

    half = (2, 3, 2, 512, 128)
    back = call(
        kernel,
        "back",
        2,
        common
        | given(
            VM, place_t=front.place_t, mid=front.mid, queries=front.queries,
            keyvals=front.keyvals, attended=front.attended, logsum=front.logsum,
            grad_bias=experts.grad_bias,
        )
        | given(
            ANY, out_rows=experts.out_rows, back_rows=experts.back_rows, dots=experts.dots,
            grads=experts.grads, normed_all=experts.normed_all, unpick=front.unpick,
            full0=front.full0, full1=front.full1, full2=front.full2,
        ),
        dict(
            layer_out=(rows, F32, VM),
            grad_tokens=(rows, F32, VM),
            grad_gates=((8, 128), F32, VM),
            grad_qkv=((2, 64, 128), F32, VM),
            grad_o=((64, 128), F32, VM),
            grad_experts=((3, 64, 2048), F32, VM),
            totals=((16, 24, 128), F32, VM),
            biases=((16, 4, 1024), F32, VM),
        ),
        dict(
            unpick_v=bf16(*wide),
            back_own=bf16(2, CAP, 1024),
            back_got=bf16(2, CAP, 1024),
            out_got=bf16(2, CAP, 1024),
            dot_own=f32(2, CAP, 128),
            dot_got=f32(2, CAP, 128),
            back_parts=bf16(2, 4, 128, 1024),
            out_parts=bf16(2, 4, 128, 1024),
            token_dots=f32(8, 2, 2, 128),
            dots_all=f32(8, 2, 2, 128),
            z_own=bf16(*half),
            z_near=bf16(*half),
            z_far=bf16(*half),
            z_solo=bf16(*half),
            z_send=bf16(*half),
            z_got=bf16(*half),
            deal_out=bf16(3, 2, 2, 8, 64, 128),
            deal_got=bf16(3, 2, 8, 2, 64, 128),
            unsorted=bf16(3, 2, 64, 2048),
            unsorted_got=bf16(3, 64, 2048),
            full0_v=bf16(*FULL),
            full1_v=bf16(*FULL),
            full2_v=bf16(*FULL),
            normed_v=bf16(2, 4, 128, 1024),
            grad_wo=bf16(*FULL),
            dq=f32(*rows),
            dkv=f32(*rows),
            halo=bf16(*rows),
            halo_got=bf16(*rows),
            low=bf16(2, 128, 1024),
            low_all=bf16(2, 8, 128, 128),
            grad_w=bf16(2, 16, 64, 128),
            grad_w_got=bf16(2, 16, 64, 128),
            small=f32(24, 128),
            small_got=f32(7, 24, 128),
            small_all=f32(16, 24, 128),
            bias_sum=f32(4, 1024),
            bias_got=f32(7, 4, 1024),
            bias_all=f32(16, 4, 1024),
            send=DMA((166,)),
            recv=DMA((166,)),
            load=DMA((11,)),
        )
        | flat,
    )
    done = call(
        finish_kernel,
        "finish",
        None,
        given(
            VM, layer_in=back.layer_out, tokens_in=back.grad_tokens, qkv=back.grad_qkv,
            wo_in=back.grad_o, experts=back.grad_experts, gates_in=back.grad_gates,
            totals=back.totals, biases=back.biases,
        ),
        dict(
            layer_out=(rows, F32, VM),
            grad_tokens=(rows, F32, VM),
            w_query=((64, 128), F32, VM),
            w_keyval=((64, 128), F32, VM),
            w_output_t=((64, 128), F32, VM),
            w_gate=((64, 2048), F32, VM),
            w_up=((64, 2048), F32, VM),
            w_down=((64, 2048), F32, VM),
            gates_t=((8, 128), F32, VM),
            gain1=((1, 1024), F32, VM),
            gain2=((1, 1024), F32, VM),
            sinks=((1, 16), F32, VM),
            bias_gate=((32, 512), F32, VM),
            bias_up=((32, 512), F32, VM),
            bias_down=((32, 1024), F32, VM),
        ),
        {},
    )
    return (
        done.layer_out,
        done.grad_tokens,
        done.gain1[0],
        done.w_query,
        done.w_keyval,
        done.w_output_t.T,
        done.sinks[0],
        done.gain2[0],
        done.w_gate,
        done.w_up,
        done.w_down,
        done.bias_gate,
        done.bias_up,
        done.bias_down,
        done.gates_t.T,
    )


def solution(mesh):
    fine = Mesh(mesh.devices.reshape(2, 4, 2, 8), ("xh", "z", "core", "tp"))
    fsdp = ("xh", "z", "core")
    rows = P(("xh", "z", "core", "tp"), None)
    return jax.shard_map(
        local,
        mesh=fine,
        in_specs=(
            rows,
            P(),
            P(fsdp, "tp"),
            P(fsdp, "tp"),
            P("tp", fsdp),
            P(),
            P(),
            P(fsdp, "tp"),
            P(fsdp, "tp"),
            P(fsdp, "tp"),
            P(),
            P(),
            P(),
            P(fsdp, None),
            P(fsdp, None),
            P(fsdp),
            rows,
        ),
        out_specs=(
            rows,
            rows,
            P(),
            P(fsdp, "tp"),
            P(fsdp, "tp"),
            P("tp", fsdp),
            P(),
            P(),
            P(fsdp, "tp"),
            P(fsdp, "tp"),
            P(fsdp, "tp"),
            P(),
            P(),
            P(),
            rows,
        ),
        check_vma=False,
    )
```
